128 devices in a mesh: dom: 64 (over z, y, x), tip: 2 (over core).
Axes of the slice: x: 4, y: 4, z: 4, core: 2. Of those that a mesh axis runs over, the one named last changes fastest.
Arguments:
- band_maps: bfloat16 [64, 1024, 1024], P('dom', None, 'tip')
- right_tips: float32 [64, 32, 1024], P('dom', None, 'tip'), may hold values from -1.5 to 1.5
- spikes: bfloat16 [64, 1024, 2048], P('dom', 'tip'), may hold values from -0.1875 to 0.1875
- local_parts: float32 [64, 32, 2048], P('dom', None, 'tip'), may hold values from -6 to 6
Outputs:
- interface: float32 [64, 32, 1024], P('dom', None, 'tip')
- interior: float32 [64, 32, 2048], P('dom', None, 'tip')
The draws below stay inside these ranges and needn't reach their ends.
All inputs are finite; a program needn't handle non-finite values.
Results may differ from the reference program's by a relative error of at most 0.002.
Values may be sent and summed in bfloat16 or wider, within the bound.
A program may use at most 64 MiB of HBM per device.

```python
import math
import jax
import jax.numpy as jnp
from jax import lax

B = 1024
RHS = 32
ROWS = 2048
PARTITION_COUNT = 64


def draw_band_maps(key, part):
    key = jax.random.fold_in(key, 11)
    first, second_operand, third = jax.random.split(key, 3)
    low_rate, high_rate = (0.001, 0.05)
    discard_factor = jnp.exp(jax.random.uniform(first, (1, 1, B), jnp.float32, math.log(low_rate), math.log(high_rate)))
    spike_columns = jnp.where(jax.random.randint(second_operand, (PARTITION_COUNT, 1, 1), 0, 16) == 0, 0.6, 1.0)
    retained_value = (1.0 - discard_factor) * spike_columns
    index = jnp.arange(B)
    identity = (index[:, None] == index[None, :]).astype(jnp.float32)
    mixing = 0.8 * identity[None] + 0.6 * jax.random.normal(third, (PARTITION_COUNT, B, B), jnp.float32) / math.sqrt(B)
    return (mixing * retained_value).astype(jnp.bfloat16)


def block_scale(rng, extent, cuts, smallest, top_value):
    gain = 1.0
    for axis_at, parts in cuts:
        heights = jax.random.uniform(jax.random.fold_in(jax.random.fold_in(rng, 6), axis_at), (parts,), jnp.float32, smallest / len(cuts), top_value / len(cuts))
        gain = gain * jnp.repeat(jnp.exp(heights), extent[axis_at] // parts).reshape((-1,) + (1,) * (len(extent) - 1 - axis_at))
    return gain


def centred(rng, extent, spread, most, pieces=(), kind=jnp.bfloat16):
    drawn = spread * jax.random.normal(rng, extent, jnp.float32)
    if pieces:
        drawn = drawn * block_scale(rng, extent, pieces, -0.22, 0.18)
    return jnp.clip(drawn, -most, most).astype(kind)


def setup_inputs(seed: int = 0) -> dict:
    arg_keys = jax.random.split(jax.random.key(seed), 5)
    return {
        "band_maps": draw_band_maps(jax.random.fold_in(arg_keys[4], 71), 0),
        "right_tips": centred(arg_keys[1], (PARTITION_COUNT, RHS, B), 0.25, 1.5, ((0, 64), (2, 2)), jnp.float32),
        "spikes": centred(arg_keys[2], (PARTITION_COUNT, B, ROWS), B ** -0.5, 0.1875, ((0, 64), (1, 2))),
        "local_parts": centred(arg_keys[3], (PARTITION_COUNT, RHS, ROWS), 1.0, 6.0, ((0, 64), (2, 2)), jnp.float32),
    }


def reference(band_maps, right_tips, spikes, local_parts):
    def advance(state, pair):
        block, tip_values = pair
        fresh = jnp.dot(state, block.astype(jnp.float32), precision=lax.Precision.HIGHEST) + tip_values
        return fresh, fresh

    start = jnp.zeros((RHS, B), jnp.float32)
    _, interface = lax.scan(advance, start, (band_maps, right_tips))
    prior = jnp.concatenate([jnp.zeros((1, RHS, B), jnp.float32), interface[:-1]], 0)
    rounded = prior.astype(jnp.bfloat16).astype(jnp.float32)
    product = jnp.einsum("prb,pbk->prk", rounded, spikes.astype(jnp.float32), precision=lax.Precision.HIGHEST)
    return interface, local_parts - product
```

```python
import functools

import jax
import jax.numpy as jnp
from jax import lax
from jax.experimental import pallas as pl
from jax.experimental.pallas import tpu as pltpu
from jax.sharding import PartitionSpec as P

MESH = pl.DeviceIdType.MESH
RING = 4
CHAIN_ROWS = 2


def split_rows(value):
    high = value.astype(jnp.bfloat16)
    low = value - high.astype(jnp.float32)
    return jnp.concatenate([high.astype(jnp.float32), low], 0).astype(jnp.bfloat16)


def times_map(value, left, right):
    rows = value.shape[0]
    parts = split_rows(value)
    out = [jnp.dot(parts, half, preferred_element_type=jnp.float32) for half in (left, right)]
    return [piece[:rows] + piece[rows:] for piece in out]


def sweep(
    rows_total, maps_hbm, tips_ref, spikes_hbm, interface_ref, product_ref,
    maps, tips_out, tips_few, tips_many, few_in, many_in, many_out, states, prior, prior_many, full, spikes,
    local_sem, sib_send, sib_recv, link_send, link_recv, fwd_send, opp_recv,
    tip_send, tip_recv, wave_send, wave_recv, home_send, home_recv, side_send, side_recv,
):
    me, tip = lax.axis_index("dom"), lax.axis_index("tip")
    x, row = lax.rem(me, RING), lax.div(me, RING)
    other = 1 - tip
    base = me - x
    depth = maps_hbm.shape[1]
    half = maps_hbm.shape[2]
    cut = depth // 2
    width = spikes_hbm.shape[2] // 2
    chained = row < CHAIN_ROWS
    ringed = row >= CHAIN_ROWS
    last_chain = CHAIN_ROWS * RING - 1
    right, left = base + lax.rem(x + 1, RING), base + lax.rem(x + 3, RING)
    opposite = base + lax.rem(x + 2, RING)
    many = full.shape[0] // 2
    few = many // RING

    def remote(src, dst, send, recv, dom, to):
        return pltpu.make_async_remote_copy(
            src_ref=src, dst_ref=dst, send_sem=send, recv_sem=recv, device_id=(dom, to), device_id_type=MESH
        )

    barrier = pltpu.get_barrier_semaphore()

    def greet(dom, to):
        pl.semaphore_signal(barrier, inc=1, device_id=(dom, to), device_id_type=MESH)

    greet(me, other)

    @pl.when(chained)
    def _():
        @pl.when(me > 0)
        def _():
            greet(me - 1, tip)

    @pl.when(ringed)
    def _():
        for step in range(1, RING):
            for to in range(2):
                greet(base + lax.rem(x + step, RING), to)
        greet(jnp.where(row == CHAIN_ROWS, last_chain, me - RING), tip)

    own_map = pltpu.make_async_copy(maps_hbm.at[0], maps.at[x, tip], local_sem.at[0])
    own_map.start()
    own_columns = pl.ds(pl.multiple_of(tip * width, width), width)
    other_columns = pl.ds(pl.multiple_of(other * width, width), width)
    own_spikes = pltpu.make_async_copy(spikes_hbm.at[0, :, own_columns], spikes.at[tip], local_sem.at[1])
    own_spikes.start()
    for piece in range(2 * RING):
        tips_out[piece] = tips_ref[0, piece * few : (piece + 1) * few, :]

    @pl.when(chained)
    def _():
        pl.semaphore_wait(barrier, jnp.where(me == last_chain, 1 + RING, 2))

    @pl.when(ringed)
    def _():
        pl.semaphore_wait(barrier, jnp.where(row == rows_total - 1, 7, 8))

    pieces = [slice(0, cut), slice(cut, depth)]

    def sibling_map(step, part):
        slot = lax.rem(x + step, RING)
        block = maps.at[slot, tip, pieces[part]]
        return remote(block, block, sib_send.at[step, part], sib_recv.at[step, part], me, other)

    def sibling_map_arrives(step, part):
        slot = lax.rem(x + step, RING)
        block = maps.at[slot, other, pieces[part]]
        remote(block, block, sib_send.at[step, part], sib_recv.at[step, part], me, other).wait_recv()

    def own_sibling_map(part):
        src = maps_hbm.at[0, pieces[part]]
        return remote(src, maps.at[x, tip, pieces[part]], sib_send.at[0, part], sib_recv.at[0, part], me, other)

    spikes_out = remote(
        spikes_hbm.at[0, :, other_columns], spikes.at[tip], side_send.at[0], side_recv.at[0], me, other
    )

    @pl.when(chained)
    def _():
        for part in range(2):
            own_sibling_map(part).start()
        tip_rows = pl.ds(pl.multiple_of(other * many, many), many)
        tips_copy = remote(
            tips_ref.at[0, tip_rows, :], tips_many.at[tip], tip_send.at[0], tip_recv.at[0, 1], me, other
        )
        tips_copy.start()
        spikes_out.start()
        own_map.wait()
        for part in range(2):
            sibling_map_arrives(0, part)
        tips_copy.wait_recv()
        many_from = remote(many_in, many_in, wave_send.at[0], wave_recv.at[0], me, other)

        @pl.when(me > 0)
        def _():
            many_from.wait_recv()

        @pl.when(me == 0)
        def _():
            many_in[...] = jnp.zeros_like(many_in)

        own_rows = pl.ds(pl.multiple_of(tip * many, many), many)
        fresh = times_map(many_in[...], maps[x, 0], maps[x, 1])
        tips_many[tip] = tips_ref[0, own_rows, :]
        fresh = [fresh[h] + tips_many[h] for h in range(2)]

        @pl.when(me < last_chain)
        def _():
            for h in range(2):
                many_out[:, h * half : (h + 1) * half] = fresh[h]
            remote(many_out, many_in, wave_send.at[0], wave_recv.at[0], me + 1, tip).start()

        @pl.when(me == last_chain)
        def _():
            for piece in range(RING):
                for h in range(2):
                    states[piece, :, h * half : (h + 1) * half] = fresh[h][piece * few : (piece + 1) * few]
            for piece in range(RING):
                remote(
                    states.at[piece], few_in, home_send.at[piece, 0], wave_recv.at[1], last_chain + 1 + piece, tip
                ).start()

        to_sibling = remote(many_in, prior_many, side_send.at[1], side_recv.at[1], me, other)
        to_sibling.start()
        full[own_rows, :] = many_in[...]
        to_sibling.wait_recv()
        full[tip_rows, :] = prior_many[...]

        to_sibling.wait_send()
        tips_copy.wait_send()
        for part in range(2):
            own_sibling_map(part).wait_send()

        @pl.when(me < last_chain)
        def _():
            remote(many_out, many_in, wave_send.at[0], wave_recv.at[0], me, other).wait_send()

        @pl.when(me == last_chain)
        def _():
            for piece in range(RING):
                remote(
                    states.at[piece], few_in, home_send.at[piece, 0], wave_recv.at[1], last_chain + 1 + piece, tip
                ).wait_send()

    @pl.when(ringed)
    def _():
        def own_part(part, side):
            return remote(
                maps_hbm.at[0, pieces[part]], maps.at[x, tip, pieces[part]],
                link_send.at[side, part], link_recv.at[side, part], right if side == 0 else left, tip,
            )

        def neighbour_arrives(part, side):
            slot = lax.rem(x + (3 if side == 0 else 1), RING)
            block = maps.at[slot, tip, pieces[part]]
            remote(block, block, link_send.at[side, part], link_recv.at[side, part], right, tip).wait_recv()

        def forward(side):
            slot = lax.rem(x + (3 if side == 0 else 1), RING)
            block = maps.at[slot, tip, pieces[side]]
            return remote(block, block, fwd_send.at[side], opp_recv.at[side], right if side == 0 else left, tip)

        def opposite_arrives(side):
            block = maps.at[lax.rem(x + 2, RING), tip, pieces[side]]
            remote(block, block, fwd_send.at[side], opp_recv.at[side], right, tip).wait_recv()

        own_part(0, 0).start()
        own_part(1, 1).start()
        own_part(1, 0).start()
        own_part(0, 1).start()

        def tip_copy(step, to, number):
            dst_x = lax.rem(x + step, RING)
            return remote(
                tips_out.at[to * RING + dst_x], tips_few.at[x, tip],
                tip_send.at[number], tip_recv.at[step, jnp.where(to == tip, 0, 1)], base + dst_x, to,
            )

        partners = [(0, other), (1, tip), (1, other), (2, tip), (2, other), (3, tip), (3, other)]
        for number, (step, to) in enumerate(partners):
            tip_copy(step, to, number).start()
        tips_few[x, tip] = tips_out[tip * RING + x]
        for part in range(2):
            own_sibling_map(part).start()
        spikes_out.start()
        for part, side in ((0, 0), (1, 1)):
            neighbour_arrives(part, side)
            forward(side).start()
            sibling_map(3 if side == 0 else 1, part).start()
        for part, side in ((1, 0), (0, 1)):
            neighbour_arrives(part, side)
            sibling_map(3 if side == 0 else 1, part).start()
        for side in range(2):
            opposite_arrives(side)
            sibling_map(2, side).start()
        own_map.wait()
        for step in (0, 1, 3, 2):
            for part in range(2):
                sibling_map_arrives(step, part)
        for step, to in partners:
            remote(
                tips_few.at[0, 0], tips_few.at[0, 0], tip_send.at[0],
                tip_recv.at[step, jnp.where(to == tip, 0, 1)], me, other,
            ).wait_recv()

        mine = tip * RING + x

        def home_copy(step, to):
            src = few_in if step == 0 else states.at[step - 1]
            return remote(src, prior.at[mine], home_send.at[step, to], home_recv.at[mine], base + step, to)

        def send_home(step):
            for to in range(2):
                @pl.when(jnp.logical_or(x != step, tip != to))
                def _():
                    home_copy(step, to).start()

            @pl.when(x == step)
            def _():
                prior[mine] = few_in[...] if step == 0 else states[step - 1]

        onward = remote(states.at[RING - 1], few_in, wave_send.at[0], wave_recv.at[1], me + RING, tip)
        remote(few_in, few_in, wave_send.at[0], wave_recv.at[1], me, other).wait_recv()
        state = few_in[...]
        for step in range(RING):
            fresh = times_map(state, maps[step, 0], maps[step, 1])
            for h in range(2):
                states[step, :, h * half : (h + 1) * half] = fresh[h] + tips_few[step, h]
            state = states[step]

        @pl.when(row < rows_total - 1)
        def _():
            onward.start()

        for step in range(RING):
            send_home(step)
        for piece in range(2 * RING):
            @pl.when(piece != mine)
            def _():
                remote(
                    prior.at[piece], prior.at[piece], home_send.at[0, 0], home_recv.at[piece], me, other
                ).wait_recv()
        for piece in range(2 * RING):
            full[piece * few : (piece + 1) * few, :] = prior[piece]

        for part in range(2):
            for side in range(2):
                own_part(part, side).wait_send()
            own_sibling_map(part).wait_send()
            forward(part).wait_send()
            for step in range(1, RING):
                sibling_map(step, part).wait_send()
        for number, (step, to) in enumerate(partners):
            tip_copy(step, to, number).wait_send()

        @pl.when(row < rows_total - 1)
        def _():
            onward.wait_send()

        for step in range(RING):
            for to in range(2):
                @pl.when(jnp.logical_or(x != step, tip != to))
                def _():
                    home_copy(step, to).wait_send()

    own_spikes.wait()
    spikes_out.wait()
    count = full.shape[0]
    parts = split_rows(full[...])
    fresh = jnp.dot(parts, maps[x, tip], preferred_element_type=jnp.float32)
    interface_ref[0] = fresh[:count] + fresh[count:]
    middle = spikes.shape[1]
    product = jnp.dot(parts[:count, :middle], spikes[0], preferred_element_type=jnp.float32)
    product_ref[0] = product + jnp.dot(parts[:count, middle:], spikes[1], preferred_element_type=jnp.float32)


def on_device(band_maps, right_tips, spikes, local_parts):
    rows_total = lax.axis_size("dom") // RING
    _, depth, half = band_maps.shape
    count = right_tips.shape[1]
    many = count // 2
    few = many // RING
    _, spike_rows, spike_columns = spikes.shape
    width = spike_columns // 2
    f32, b16, dma = jnp.float32, jnp.bfloat16, pltpu.SemaphoreType.DMA
    interface, product = pl.pallas_call(
        functools.partial(sweep, rows_total),
        out_shape=(
            jax.ShapeDtypeStruct((1, count, half), f32),
            jax.ShapeDtypeStruct((1, count, width), f32),
        ),
        in_specs=[
            pl.BlockSpec(memory_space=pl.ANY),
            pl.BlockSpec(memory_space=pltpu.VMEM),
            pl.BlockSpec(memory_space=pl.ANY),
        ],
        out_specs=(pl.BlockSpec(memory_space=pltpu.VMEM),) * 2,
        scratch_shapes=[
            pltpu.VMEM((RING, 2, depth, half), b16),
            pltpu.VMEM((2 * RING, few, half), f32),
            pltpu.VMEM((RING, 2, few, half), f32),
            pltpu.VMEM((2, many, half), f32),
            pltpu.VMEM((few, depth), f32),
            pltpu.VMEM((many, depth), f32),
            pltpu.VMEM((many, depth), f32),
            pltpu.VMEM((RING, few, depth), f32),
            pltpu.VMEM((2 * RING, few, depth), f32),
            pltpu.VMEM((many, depth), f32),
            pltpu.VMEM((count, depth), f32),
            pltpu.VMEM((2, spike_rows, width), b16),
            dma((2,)),
            dma((RING, 2)),
            dma((RING, 2)),
            dma((2, 2)),
            dma((2, 2)),
            dma((2,)),
            dma((2,)),
            dma((2 * RING - 1,)),
            dma((RING, 2)),
            dma((2,)),
            dma((2,)),
            dma((RING, 2)),
            dma((2 * RING,)),
            dma((2,)),
            dma((2,)),
        ],
        compiler_params=pltpu.CompilerParams(
            collective_id=0, has_side_effects=True, vmem_limit_bytes=40 << 20
        ),
    )(band_maps, right_tips, spikes)
    return right_tips + interface, local_parts - product


def solution(mesh):
    return jax.shard_map(
        on_device,
        mesh=mesh,
        in_specs=(
            P("dom", None, "tip"),
            P("dom", None, "tip"),
            P("dom", "tip", None),
            P("dom", None, "tip"),
        ),
        out_specs=(P("dom", None, "tip"), P("dom", None, "tip")),
        check_vma=False,
    )
```

```python
import functools

import jax
import jax.numpy as jnp
from jax import lax
from jax.experimental import pallas as pl
from jax.experimental.pallas import tpu as pltpu
from jax.sharding import PartitionSpec as P

MESH = pl.DeviceIdType.MESH
RING = 4
CHAIN_ROWS = 2
PRODUCT_ROW = 4


def split_rows(value):
    high = value.astype(jnp.bfloat16)
    low = value - high.astype(jnp.float32)
    return jnp.concatenate([high.astype(jnp.float32), low], 0).astype(jnp.bfloat16)


def times_map(value, left, right):
    rows = value.shape[0]
    parts = split_rows(value)
    out = [jnp.dot(parts, half, preferred_element_type=jnp.float32) for half in (left, right)]
    return [piece[:rows] + piece[rows:] for piece in out]


def four_maps(maps, tip, high, low):
    depth, half = maps.shape[2], maps.shape[3]
    block = min(256, depth)

    for turn, step in enumerate((2, 1, 0)):
        def rows_of(index, _, turn=turn, step=step):
            rows = pl.ds(pl.multiple_of(index * block, block), block)
            total = None
            for h in range(2):
                lhs = maps[step, h, rows, :]
                if turn == 0:
                    factors = [maps[3, tip, h * half : (h + 1) * half, :]]
                else:
                    factors = [ref[(turn - 1) % 2, h * half : (h + 1) * half, :] for ref in (high, low)]
                for factor in factors:
                    term = jnp.dot(lhs, factor, preferred_element_type=jnp.float32)
                    total = term if total is None else total + term
            top = total.astype(jnp.bfloat16)
            high[turn % 2, rows, :] = top
            low[turn % 2, rows, :] = (total - top.astype(jnp.float32)).astype(jnp.bfloat16)
            return 0

        lax.fori_loop(0, depth // block, rows_of, 0)


def sweep(
    rows_total, maps_hbm, tips_hbm, spikes_hbm, interface_ref, product_ref,
    maps, tips_ref, tips_out, tips_both, tips_few, tips_many, few_in, pair_in, columns_in, columns_out, eight, local,
    high, low, many_in, many_out, states, prior, prior_many, full, spikes,
    local_sem, sib_send, sib_recv, link_send, link_recv, fwd_send, opp_recv,
    tip_send, tip_recv, wave_send, wave_recv, home_send, home_recv, side_send, side_recv,
):
    me, tip = lax.axis_index("dom"), lax.axis_index("tip")
    x, row = lax.rem(me, RING), lax.div(me, RING)
    other = 1 - tip
    base = me - x
    depth = maps_hbm.shape[1]
    half = maps_hbm.shape[2]
    cut = depth // 2
    width = spikes_hbm.shape[2] // 2
    chained = row < CHAIN_ROWS
    ringed = row >= CHAIN_ROWS
    last_chain = CHAIN_ROWS * RING - 1
    right, left = base + lax.rem(x + 1, RING), base + lax.rem(x + 3, RING)
    opposite = base + lax.rem(x + 2, RING)
    many = full.shape[0] // 2
    few = many // RING

    def remote(src, dst, send, recv, dom, to):
        return pltpu.make_async_remote_copy(
            src_ref=src, dst_ref=dst, send_sem=send, recv_sem=recv, device_id=(dom, to), device_id_type=MESH
        )

    barrier = pltpu.get_barrier_semaphore()

    def greet(dom, to):
        pl.semaphore_signal(barrier, inc=1, device_id=(dom, to), device_id_type=MESH)

    greet(me, other)

    @pl.when(chained)
    def _():
        @pl.when(me > 0)
        def _():
            greet(me - 1, tip)

    @pl.when(ringed)
    def _():
        for step in range(1, RING):
            for to in range(2):
                greet(base + lax.rem(x + step, RING), to)
        before = jnp.where(row == CHAIN_ROWS, last_chain, me - RING)
        greet(before, tip)

        @pl.when(row >= PRODUCT_ROW)
        def _():
            greet(before, other)

    own_map = pltpu.make_async_copy(maps_hbm.at[0], maps.at[x, tip], local_sem.at[0])
    own_map.start()
    own_columns = pl.ds(pl.multiple_of(tip * width, width), width)
    other_columns = pl.ds(pl.multiple_of(other * width, width), width)
    own_spikes = pltpu.make_async_copy(spikes_hbm.at[0, :, own_columns], spikes.at[tip], local_sem.at[1])
    own_spikes.start()
    own_tips = pltpu.make_async_copy(tips_hbm.at[0], tips_ref, local_sem.at[2])
    own_tips.start()
    own_tips.wait()
    for piece in range(RING):
        for to in range(2):
            start = to * many + piece * few
            tips_out[piece, to * few : (to + 1) * few, :] = tips_ref[start : start + few, :]

    @pl.when(chained)
    def _():
        pl.semaphore_wait(barrier, jnp.where(me == last_chain, 1 + RING, 2))

    @pl.when(ringed)
    def _():
        after = jnp.where(row == rows_total - 1, 0, jnp.where(row >= PRODUCT_ROW - 1, 2, 1))
        pl.semaphore_wait(barrier, 2 * RING - 1 + after)

    pieces = [slice(0, cut), slice(cut, depth)]

    def sibling_map(step, part):
        slot = lax.rem(x + step, RING)
        block = maps.at[slot, tip, pieces[part]]
        return remote(block, block, sib_send.at[step, part], sib_recv.at[step, part], me, other)

    def sibling_map_arrives(step, part):
        slot = lax.rem(x + step, RING)
        block = maps.at[slot, other, pieces[part]]
        remote(block, block, sib_send.at[step, part], sib_recv.at[step, part], me, other).wait_recv()

    def own_sibling_map(part):
        src = maps_hbm.at[0, pieces[part]]
        return remote(src, maps.at[x, tip, pieces[part]], sib_send.at[0, part], sib_recv.at[0, part], me, other)

    spikes_out = remote(
        spikes_hbm.at[0, :, other_columns], spikes.at[tip], side_send.at[0], side_recv.at[0], me, other
    )

    @pl.when(chained)
    def _():
        for part in range(2):
            own_sibling_map(part).start()
        tip_rows = pl.ds(pl.multiple_of(other * many, many), many)
        tips_copy = remote(
            tips_ref.at[tip_rows, :], tips_many.at[tip], tip_send.at[0], tip_recv.at[0, 1], me, other
        )
        tips_copy.start()
        spikes_out.start()
        own_map.wait()
        for part in range(2):
            sibling_map_arrives(0, part)
        tips_copy.wait_recv()

        def many_send(h, dom):
            return remote(many_out.at[h], many_in.at[h], wave_send.at[h], wave_recv.at[h], dom, tip)

        own_rows = pl.ds(pl.multiple_of(tip * many, many), many)
        tips_many[tip] = tips_ref[own_rows, :]

        @pl.when(me == 0)
        def _():
            many_in[...] = jnp.zeros_like(many_in)

        total = [None, None]
        for k in range(2):
            @pl.when(me > 0)
            def _():
                remote(many_in.at[k], many_in.at[k], wave_send.at[k], wave_recv.at[k], me, other).wait_recv()

            parts = split_rows(many_in[k])
            for h in range(2):
                term = jnp.dot(parts, maps[x, h, k * half : (k + 1) * half, :], preferred_element_type=jnp.float32)
                total[h] = term if k == 0 else total[h] + term
                if k == 1:
                    fresh = total[h][:many] + total[h][many:] + tips_many[h]
                    many_out[h] = fresh

                    @pl.when(me < last_chain)
                    def _():
                        many_send(h, me + 1).start()

        @pl.when(me == last_chain)
        def _():
            for piece in range(RING):
                for h in range(2):
                    states[piece, :, h * half : (h + 1) * half] = many_out[h, piece * few : (piece + 1) * few, :]
            for piece in range(RING):
                remote(
                    states.at[piece], few_in, home_send.at[piece, 0], wave_recv.at[2], last_chain + 1 + piece, tip
                ).start()

        to_sibling = remote(many_in, prior_many, side_send.at[1], side_recv.at[1], me, other)
        to_sibling.start()
        for h in range(2):
            full[own_rows, h * half : (h + 1) * half] = many_in[h]
        to_sibling.wait_recv()
        for h in range(2):
            full[tip_rows, h * half : (h + 1) * half] = prior_many[h]

        to_sibling.wait_send()
        tips_copy.wait_send()
        for part in range(2):
            own_sibling_map(part).wait_send()

        @pl.when(me < last_chain)
        def _():
            for h in range(2):
                many_send(h, me + 1).wait_send()

        @pl.when(me == last_chain)
        def _():
            for piece in range(RING):
                remote(
                    states.at[piece], few_in, home_send.at[piece, 0], wave_recv.at[2], last_chain + 1 + piece, tip
                ).wait_send()

    @pl.when(ringed)
    def _():
        def own_part(part, side):
            return remote(
                maps_hbm.at[0, pieces[part]], maps.at[x, tip, pieces[part]],
                link_send.at[side, part], link_recv.at[side, part], right if side == 0 else left, tip,
            )

        def neighbour_arrives(part, side):
            slot = lax.rem(x + (3 if side == 0 else 1), RING)
            block = maps.at[slot, tip, pieces[part]]
            remote(block, block, link_send.at[side, part], link_recv.at[side, part], right, tip).wait_recv()

        def forward(side):
            slot = lax.rem(x + (3 if side == 0 else 1), RING)
            block = maps.at[slot, tip, pieces[side]]
            return remote(block, block, fwd_send.at[side], opp_recv.at[side], right if side == 0 else left, tip)

        def opposite_arrives(side):
            block = maps.at[lax.rem(x + 2, RING), tip, pieces[side]]
            remote(block, block, fwd_send.at[side], opp_recv.at[side], right, tip).wait_recv()

        own_part(0, 0).start()
        own_part(1, 1).start()
        own_part(1, 0).start()
        own_part(0, 1).start()

        def tip_copy(step, to, number):
            dst_x = lax.rem(x + step, RING)
            return remote(
                tips_out.at[dst_x], tips_both.at[x, tip],
                tip_send.at[number], tip_recv.at[step, jnp.where(to == tip, 0, 1)], base + dst_x, to,
            )

        partners = [(0, other), (1, tip), (1, other), (2, tip), (2, other), (3, tip), (3, other)]
        for number, (step, to) in enumerate(partners):
            tip_copy(step, to, number).start()
        tips_both[x, tip] = tips_out[x]
        for part in range(2):
            own_sibling_map(part).start()
        spikes_out.start()
        for part, side in ((0, 0), (1, 1)):
            neighbour_arrives(part, side)
            forward(side).start()
            sibling_map(3 if side == 0 else 1, part).start()
        for part, side in ((1, 0), (0, 1)):
            neighbour_arrives(part, side)
            sibling_map(3 if side == 0 else 1, part).start()
        for side in range(2):
            opposite_arrives(side)
            sibling_map(2, side).start()
        own_map.wait()
        for step in (0, 1, 3, 2):
            for part in range(2):
                sibling_map_arrives(step, part)
        for step, to in partners:
            remote(
                tips_both.at[0, 0], tips_both.at[0, 0], tip_send.at[0],
                tip_recv.at[step, jnp.where(to == tip, 0, 1)], me, other,
            ).wait_recv()

        mine = tip * RING + x

        def home_copy(step, to):
            src = few_in if step == 0 else states.at[step - 1]
            return remote(src, prior.at[mine], home_send.at[step, to], home_recv.at[mine], base + step, to)

        def send_home(step):
            for to in range(2):
                @pl.when(jnp.logical_or(x != step, tip != to))
                def _():
                    home_copy(step, to).start()

            @pl.when(x == step)
            def _():
                prior[mine] = few_in[...] if step == 0 else states[step - 1]

        def next_state(step, state):
            fresh = times_map(state, maps[step, 0], maps[step, 1])
            for h in range(2):
                states[step, :, h * half : (h + 1) * half] = fresh[h] + tips_few[step, h]
            return states[step]

        def own_of(pair):
            return jnp.where(tip == 0, pair[:few], pair[few:])

        for step in range(RING):
            for h in range(2):
                tips_few[step, h] = own_of(tips_both[step, h])

        final_row = row == rows_total - 1
        direct = row < PRODUCT_ROW

        def onward_rows(to):
            return remote(states.at[RING - 1], few_in, wave_send.at[to], wave_recv.at[2], me + RING, tip)

        def onward_pair(to):
            return remote(
                states.at[RING - 1], pair_in.at[tip], wave_send.at[to], wave_recv.at[3 + tip], me + RING, to
            )

        def onward_columns(to):
            return remote(columns_out, columns_in.at[tip], wave_send.at[to], wave_recv.at[5 + tip], me + RING, to)

        @pl.when(direct)
        def _():
            remote(few_in, few_in, wave_send.at[0], wave_recv.at[2], me, other).wait_recv()
            state = few_in[...]
            for step in range(RING):
                state = next_state(step, state)

            @pl.when(row < PRODUCT_ROW - 1)
            def _():
                onward_rows(0).start()

            @pl.when(jnp.logical_and(row == PRODUCT_ROW - 1, jnp.logical_not(final_row)))
            def _():
                for to in range(2):
                    onward_pair(to).start()

            for step in range(RING):
                send_home(step)

        @pl.when(jnp.logical_not(direct))
        def _():
            @pl.when(jnp.logical_not(final_row))
            def _():
                four_maps(maps, tip, high, low)
                state = jnp.concatenate([tips_both[0, 0], tips_both[0, 1]], 1)
                for step in (1, 2):
                    fresh = times_map(state, maps[step, 0], maps[step, 1])
                    state = jnp.concatenate([fresh[h] + tips_both[step, h] for h in range(2)], 1)
                parts = split_rows(state)
                fresh = jnp.dot(parts, maps[3, tip], preferred_element_type=jnp.float32)
                local[...] = fresh[: 2 * few] + fresh[2 * few :] + tips_both[3, tip]

            @pl.when(row == PRODUCT_ROW)
            def _():
                for core in range(2):
                    remote(
                        pair_in.at[core], pair_in.at[core], wave_send.at[0], wave_recv.at[3 + core], me, other
                    ).wait_recv()
                for core in range(2):
                    eight[core * few : (core + 1) * few, :] = pair_in[core]

            @pl.when(row > PRODUCT_ROW)
            def _():
                for core in range(2):
                    remote(
                        columns_in.at[core], columns_in.at[core], wave_send.at[0], wave_recv.at[5 + core], me, other
                    ).wait_recv()
                for core in range(2):
                    eight[:, core * half : (core + 1) * half] = columns_in[core]

            @pl.when(jnp.logical_not(final_row))
            def _():
                parts = split_rows(eight[...])
                fresh = jnp.dot(parts, high[0], preferred_element_type=jnp.float32)
                fresh = fresh + jnp.dot(parts, low[0], preferred_element_type=jnp.float32)
                columns_out[...] = fresh[: 2 * few] + fresh[2 * few :] + local[...]
                for to in range(2):
                    onward_columns(to).start()

            few_in[...] = own_of(eight[...])
            send_home(0)
            state = few_in[...]
            for step in range(RING - 1):
                state = next_state(step, state)
                send_home(step + 1)

        for piece in range(2 * RING):
            @pl.when(piece != mine)
            def _():
                remote(
                    prior.at[piece], prior.at[piece], home_send.at[0, 0], home_recv.at[piece], me, other
                ).wait_recv()
        for piece in range(2 * RING):
            full[piece * few : (piece + 1) * few, :] = prior[piece]

        for part in range(2):
            for side in range(2):
                own_part(part, side).wait_send()
            own_sibling_map(part).wait_send()
            forward(part).wait_send()
            for step in range(1, RING):
                sibling_map(step, part).wait_send()
        for number, (step, to) in enumerate(partners):
            tip_copy(step, to, number).wait_send()

        @pl.when(row < PRODUCT_ROW - 1)
        def _():
            onward_rows(0).wait_send()

        @pl.when(jnp.logical_and(row == PRODUCT_ROW - 1, jnp.logical_not(final_row)))
        def _():
            for to in range(2):
                onward_pair(to).wait_send()

        @pl.when(jnp.logical_and(row >= PRODUCT_ROW, jnp.logical_not(final_row)))
        def _():
            for to in range(2):
                onward_columns(to).wait_send()

        for step in range(RING):
            for to in range(2):
                @pl.when(jnp.logical_or(x != step, tip != to))
                def _():
                    home_copy(step, to).wait_send()

    own_spikes.wait()
    spikes_out.wait()
    count = full.shape[0]
    parts = split_rows(full[...])
    fresh = jnp.dot(parts, maps[x, tip], preferred_element_type=jnp.float32)
    interface_ref[0] = fresh[:count] + fresh[count:]
    middle = spikes.shape[1]
    product = jnp.dot(parts[:count, :middle], spikes[0], preferred_element_type=jnp.float32)
    product_ref[0] = product + jnp.dot(parts[:count, middle:], spikes[1], preferred_element_type=jnp.float32)


def on_device(band_maps, right_tips, spikes, local_parts):
    rows_total = lax.axis_size("dom") // RING
    _, depth, half = band_maps.shape
    count = right_tips.shape[1]
    many = count // 2
    few = many // RING
    _, spike_rows, spike_columns = spikes.shape
    width = spike_columns // 2
    f32, b16, dma = jnp.float32, jnp.bfloat16, pltpu.SemaphoreType.DMA
    interface, product = pl.pallas_call(
        functools.partial(sweep, rows_total),
        out_shape=(
            jax.ShapeDtypeStruct((1, count, half), f32),
            jax.ShapeDtypeStruct((1, count, width), f32),
        ),
        in_specs=[
            pl.BlockSpec(memory_space=pltpu.HBM),
            pl.BlockSpec(memory_space=pltpu.HBM),
            pl.BlockSpec(memory_space=pltpu.HBM),
        ],
        out_specs=(pl.BlockSpec(memory_space=pltpu.VMEM),) * 2,
        scratch_shapes=[
            pltpu.VMEM((RING, 2, depth, half), b16),
            pltpu.VMEM((count, half), f32),
            pltpu.VMEM((RING, 2 * few, half), f32),
            pltpu.VMEM((RING, 2, 2 * few, half), f32),
            pltpu.VMEM((RING, 2, few, half), f32),
            pltpu.VMEM((2, many, half), f32),
            pltpu.VMEM((few, depth), f32),
            pltpu.VMEM((2, few, depth), f32),
            pltpu.VMEM((2, 2 * few, half), f32),
            pltpu.VMEM((2 * few, half), f32),
            pltpu.VMEM((2 * few, depth), f32),
            pltpu.VMEM((2 * few, half), f32),
            pltpu.VMEM((2, depth, half), b16),
            pltpu.VMEM((2, depth, half), b16),
            pltpu.VMEM((2, many, half), f32),
            pltpu.VMEM((2, many, half), f32),
            pltpu.VMEM((RING, few, depth), f32),
            pltpu.VMEM((2 * RING, few, depth), f32),
            pltpu.VMEM((2, many, half), f32),
            pltpu.VMEM((count, depth), f32),
            pltpu.VMEM((2, spike_rows, width), b16),
            dma((3,)),
            dma((RING, 2)),
            dma((RING, 2)),
            dma((2, 2)),
            dma((2, 2)),
            dma((2,)),
            dma((2,)),
            dma((2 * RING - 1,)),
            dma((RING, 2)),
            dma((2,)),
            dma((7,)),
            dma((RING, 2)),
            dma((2 * RING,)),
            dma((2,)),
            dma((2,)),
        ],
        compiler_params=pltpu.CompilerParams(
            collective_id=0, has_side_effects=True, vmem_limit_bytes=48 << 20
        ),
    )(band_maps, right_tips, spikes)
    return right_tips + interface, local_parts - product


def solution(mesh):
    return jax.shard_map(
        on_device,
        mesh=mesh,
        in_specs=(
            P("dom", None, "tip"),
            P("dom", None, "tip"),
            P("dom", "tip", None),
            P("dom", None, "tip"),
        ),
        out_specs=(P("dom", None, "tip"), P("dom", None, "tip")),
        check_vma=False,
    )
```

```python
import functools

import jax
import jax.numpy as jnp
from jax import lax
from jax.experimental import pallas as pl
from jax.experimental.pallas import tpu as pltpu
from jax.sharding import PartitionSpec as P

MESH = pl.DeviceIdType.MESH
RING = 4
CHAIN_ROWS = 3
PRODUCT_ROW = 5


def split_rows(value):
    high = value.astype(jnp.bfloat16)
    low = value - high.astype(jnp.float32)
    return jnp.concatenate([high.astype(jnp.float32), low], 0).astype(jnp.bfloat16)


def times_map(value, left, right):
    rows = value.shape[0]
    parts = split_rows(value)
    out = [jnp.dot(parts, half, preferred_element_type=jnp.float32) for half in (left, right)]
    return [piece[:rows] + piece[rows:] for piece in out]


def four_maps(maps, tip, high, low):
    depth, half = maps.shape[2], maps.shape[3]
    block = min(256, depth)

    for turn, step in enumerate((2, 1, 0)):
        def rows_of(index, _, turn=turn, step=step):
            rows = pl.ds(pl.multiple_of(index * block, block), block)
            total = None
            for h in range(2):
                lhs = maps[step, h, rows, :]
                if turn == 0:
                    factors = [maps[3, tip, h * half : (h + 1) * half, :]]
                else:
                    factors = [ref[(turn - 1) % 2, h * half : (h + 1) * half, :] for ref in (high, low)]
                for factor in factors:
                    term = jnp.dot(lhs, factor, preferred_element_type=jnp.float32)
                    total = term if total is None else total + term
            top = total.astype(jnp.bfloat16)
            high[turn % 2, rows, :] = top
            low[turn % 2, rows, :] = (total - top.astype(jnp.float32)).astype(jnp.bfloat16)
            return 0

        lax.fori_loop(0, depth // block, rows_of, 0)


def sweep(
    rows_total, maps_hbm, tips_hbm, spikes_hbm, interface_ref, product_ref,
    maps, tips_ref, tips_out, tips_both, tips_few, tips_many, few_in, pair_in, columns_in, columns_out, eight, local,
    high, low, many_in, many_out, states, prior, prior_many, full, spikes,
    local_sem, sib_send, sib_recv, link_send, link_recv, fwd_send, opp_recv,
    tip_send, tip_recv, wave_send, wave_recv, home_send, home_recv, side_send, side_recv,
):
    me, tip = lax.axis_index("dom"), lax.axis_index("tip")
    x, row = lax.rem(me, RING), lax.div(me, RING)
    other = 1 - tip
    base = me - x
    depth = maps_hbm.shape[1]
    half = maps_hbm.shape[2]
    cut = depth // 2
    width = spikes_hbm.shape[2] // 2
    chained = row < CHAIN_ROWS
    ringed = row >= CHAIN_ROWS
    last_chain = CHAIN_ROWS * RING - 1
    right, left = base + lax.rem(x + 1, RING), base + lax.rem(x + 3, RING)
    opposite = base + lax.rem(x + 2, RING)
    many = full.shape[0] // 2
    few = many // RING

    def remote(src, dst, send, recv, dom, to):
        return pltpu.make_async_remote_copy(
            src_ref=src, dst_ref=dst, send_sem=send, recv_sem=recv, device_id=(dom, to), device_id_type=MESH
        )

    barrier = pltpu.get_barrier_semaphore()

    def greet(dom, to):
        pl.semaphore_signal(barrier, inc=1, device_id=(dom, to), device_id_type=MESH)

    greet(me, other)

    @pl.when(chained)
    def _():
        @pl.when(me > 0)
        def _():
            greet(me - 1, tip)

        @pl.when(me == 1)
        def _():
            greet(0, other)

    @pl.when(ringed)
    def _():
        for step in range(1, RING):
            for to in range(2):
                greet(base + lax.rem(x + step, RING), to)
        before = jnp.where(row == CHAIN_ROWS, last_chain, me - RING)
        greet(before, tip)

        @pl.when(row >= PRODUCT_ROW)
        def _():
            greet(before, other)

    own_map = pltpu.make_async_copy(maps_hbm.at[0], maps.at[x, tip], local_sem.at[0])
    own_map.start()
    own_columns = pl.ds(pl.multiple_of(tip * width, width), width)
    other_columns = pl.ds(pl.multiple_of(other * width, width), width)
    own_spikes = pltpu.make_async_copy(spikes_hbm.at[0, :, own_columns], spikes.at[tip], local_sem.at[1])
    own_spikes.start()
    own_tips = pltpu.make_async_copy(tips_hbm.at[0], tips_ref, local_sem.at[2])
    own_tips.start()
    own_tips.wait()
    for piece in range(RING):
        for to in range(2):
            start = to * many + piece * few
            tips_out[piece, to * few : (to + 1) * few, :] = tips_ref[start : start + few, :]

    @pl.when(chained)
    def _():
        pl.semaphore_wait(barrier, jnp.where(me == last_chain, 1 + RING, jnp.where(me == 0, 3, 2)))

    @pl.when(ringed)
    def _():
        after = jnp.where(row == rows_total - 1, 0, jnp.where(row >= PRODUCT_ROW - 1, 2, 1))
        pl.semaphore_wait(barrier, 2 * RING - 1 + after)

    pieces = [slice(0, cut), slice(cut, depth)]

    def sibling_map(step, part):
        slot = lax.rem(x + step, RING)
        block = maps.at[slot, tip, pieces[part]]
        return remote(block, block, sib_send.at[step, part], sib_recv.at[step, part], me, other)

    def sibling_map_arrives(step, part):
        slot = lax.rem(x + step, RING)
        block = maps.at[slot, other, pieces[part]]
        remote(block, block, sib_send.at[step, part], sib_recv.at[step, part], me, other).wait_recv()

    def own_sibling_map(part):
        src = maps_hbm.at[0, pieces[part]]
        return remote(src, maps.at[x, tip, pieces[part]], sib_send.at[0, part], sib_recv.at[0, part], me, other)

    spikes_out = remote(
        spikes_hbm.at[0, :, other_columns], spikes.at[tip], side_send.at[0], side_recv.at[0], me, other
    )

    def first_rows(to):
        rows = slice(to * many, (to + 1) * many)
        return remote(tips_ref.at[rows, :], many_in.at[tip], wave_send.at[to], wave_recv.at[tip], 1, to)

    @pl.when(chained)
    def _():
        @pl.when(me == 0)
        def _():
            for to in range(2):
                first_rows(to).start()

        for part in range(2):
            own_sibling_map(part).start()
        tip_rows = pl.ds(pl.multiple_of(other * many, many), many)
        tips_copy = remote(
            tips_ref.at[tip_rows, :], tips_many.at[tip], tip_send.at[0], tip_recv.at[0, 1], me, other
        )
        tips_copy.start()
        spikes_out.start()
        own_map.wait()
        for part in range(2):
            sibling_map_arrives(0, part)
        tips_copy.wait_recv()

        def many_send(h, dom):
            return remote(many_out.at[h], many_in.at[h], wave_send.at[h], wave_recv.at[h], dom, tip)

        own_rows = pl.ds(pl.multiple_of(tip * many, many), many)
        tips_many[tip] = tips_ref[own_rows, :]

        @pl.when(me == 0)
        def _():
            many_in[...] = jnp.zeros_like(many_in)

        total = [None, None]
        for k in range(2):
            @pl.when(me > 0)
            def _():
                remote(many_in.at[k], many_in.at[k], wave_send.at[k], wave_recv.at[k], me, other).wait_recv()

            parts = split_rows(many_in[k])
            for h in range(2):
                term = jnp.dot(parts, maps[x, h, k * half : (k + 1) * half, :], preferred_element_type=jnp.float32)
                total[h] = term if k == 0 else total[h] + term
                if k == 1:
                    fresh = total[h][:many] + total[h][many:] + tips_many[h]
                    many_out[h] = fresh

                    @pl.when(jnp.logical_and(me > 0, me < last_chain))
                    def _():
                        many_send(h, me + 1).start()

        @pl.when(me == last_chain)
        def _():
            for piece in range(RING):
                for h in range(2):
                    states[piece, :, h * half : (h + 1) * half] = many_out[h, piece * few : (piece + 1) * few, :]
            for piece in range(RING):
                remote(
                    states.at[piece], few_in, home_send.at[piece, 0], wave_recv.at[2], last_chain + 1 + piece, tip
                ).start()

        to_sibling = remote(many_in, prior_many, side_send.at[1], side_recv.at[1], me, other)
        to_sibling.start()
        for h in range(2):
            full[own_rows, h * half : (h + 1) * half] = many_in[h]
        to_sibling.wait_recv()
        for h in range(2):
            full[tip_rows, h * half : (h + 1) * half] = prior_many[h]

        to_sibling.wait_send()
        tips_copy.wait_send()
        for part in range(2):
            own_sibling_map(part).wait_send()

        @pl.when(me == 0)
        def _():
            for to in range(2):
                first_rows(to).wait_send()

        @pl.when(jnp.logical_and(me > 0, me < last_chain))
        def _():
            for h in range(2):
                many_send(h, me + 1).wait_send()

        @pl.when(me == last_chain)
        def _():
            for piece in range(RING):
                remote(
                    states.at[piece], few_in, home_send.at[piece, 0], wave_recv.at[2], last_chain + 1 + piece, tip
                ).wait_send()

    @pl.when(ringed)
    def _():
        def own_part(part, side):
            return remote(
                maps_hbm.at[0, pieces[part]], maps.at[x, tip, pieces[part]],
                link_send.at[side, part], link_recv.at[side, part], right if side == 0 else left, tip,
            )

        def neighbour_arrives(part, side):
            slot = lax.rem(x + (3 if side == 0 else 1), RING)
            block = maps.at[slot, tip, pieces[part]]
            remote(block, block, link_send.at[side, part], link_recv.at[side, part], right, tip).wait_recv()

        def forward(side):
            slot = lax.rem(x + (3 if side == 0 else 1), RING)
            block = maps.at[slot, tip, pieces[side]]
            return remote(block, block, fwd_send.at[side], opp_recv.at[side], right if side == 0 else left, tip)

        def opposite_arrives(side):
            block = maps.at[lax.rem(x + 2, RING), tip, pieces[side]]
            remote(block, block, fwd_send.at[side], opp_recv.at[side], right, tip).wait_recv()

        own_part(0, 0).start()
        own_part(1, 1).start()
        own_part(1, 0).start()
        own_part(0, 1).start()

        def tip_copy(step, to, number):
            dst_x = lax.rem(x + step, RING)
            return remote(
                tips_out.at[dst_x], tips_both.at[x, tip],
                tip_send.at[number], tip_recv.at[step, jnp.where(to == tip, 0, 1)], base + dst_x, to,
            )

        partners = [(0, other), (1, tip), (1, other), (2, tip), (2, other), (3, tip), (3, other)]
        for number, (step, to) in enumerate(partners):
            tip_copy(step, to, number).start()
        tips_both[x, tip] = tips_out[x]
        for part in range(2):
            own_sibling_map(part).start()
        spikes_out.start()
        for part, side in ((0, 0), (1, 1)):
            neighbour_arrives(part, side)
            forward(side).start()
            sibling_map(3 if side == 0 else 1, part).start()
        for part, side in ((1, 0), (0, 1)):
            neighbour_arrives(part, side)
            sibling_map(3 if side == 0 else 1, part).start()
        for side in range(2):
            opposite_arrives(side)
            sibling_map(2, side).start()
        own_map.wait()
        for step in (0, 1, 3, 2):
            for part in range(2):
                sibling_map_arrives(step, part)
        for step, to in partners:
            remote(
                tips_both.at[0, 0], tips_both.at[0, 0], tip_send.at[0],
                tip_recv.at[step, jnp.where(to == tip, 0, 1)], me, other,
            ).wait_recv()

        mine = tip * RING + x

        def home_copy(step, to):
            src = few_in if step == 0 else states.at[step - 1]
            return remote(src, prior.at[mine], home_send.at[step, to], home_recv.at[mine], base + step, to)

        def send_home(step):
            for to in range(2):
                @pl.when(jnp.logical_or(x != step, tip != to))
                def _():
                    home_copy(step, to).start()

            @pl.when(x == step)
            def _():
                prior[mine] = few_in[...] if step == 0 else states[step - 1]

        def next_state(step, state):
            fresh = times_map(state, maps[step, 0], maps[step, 1])
            for h in range(2):
                states[step, :, h * half : (h + 1) * half] = fresh[h] + tips_few[step, h]
            return states[step]

        def own_of(pair):
            return jnp.where(tip == 0, pair[:few], pair[few:])

        for step in range(RING):
            for h in range(2):
                tips_few[step, h] = own_of(tips_both[step, h])

        final_row = row == rows_total - 1
        direct = row < PRODUCT_ROW

        def onward_rows(to):
            return remote(states.at[RING - 1], few_in, wave_send.at[to], wave_recv.at[2], me + RING, tip)

        def onward_pair(to):
            return remote(
                states.at[RING - 1], pair_in.at[tip], wave_send.at[to], wave_recv.at[3 + tip], me + RING, to
            )

        def onward_columns(to):
            return remote(columns_out, columns_in.at[tip], wave_send.at[to], wave_recv.at[5 + tip], me + RING, to)

        @pl.when(direct)
        def _():
            remote(few_in, few_in, wave_send.at[0], wave_recv.at[2], me, other).wait_recv()
            state = few_in[...]
            for step in range(RING):
                state = next_state(step, state)

            @pl.when(row < PRODUCT_ROW - 1)
            def _():
                onward_rows(0).start()

            @pl.when(jnp.logical_and(row == PRODUCT_ROW - 1, jnp.logical_not(final_row)))
            def _():
                for to in range(2):
                    onward_pair(to).start()

            for step in range(RING):
                send_home(step)

        @pl.when(jnp.logical_not(direct))
        def _():
            @pl.when(jnp.logical_not(final_row))
            def _():
                four_maps(maps, tip, high, low)
                state = jnp.concatenate([tips_both[0, 0], tips_both[0, 1]], 1)
                for step in (1, 2):
                    fresh = times_map(state, maps[step, 0], maps[step, 1])
                    state = jnp.concatenate([fresh[h] + tips_both[step, h] for h in range(2)], 1)
                parts = split_rows(state)
                fresh = jnp.dot(parts, maps[3, tip], preferred_element_type=jnp.float32)
                local[...] = fresh[: 2 * few] + fresh[2 * few :] + tips_both[3, tip]

            @pl.when(row == PRODUCT_ROW)
            def _():
                for core in range(2):
                    remote(
                        pair_in.at[core], pair_in.at[core], wave_send.at[0], wave_recv.at[3 + core], me, other
                    ).wait_recv()
                for core in range(2):
                    eight[core * few : (core + 1) * few, :] = pair_in[core]

            @pl.when(row > PRODUCT_ROW)
            def _():
                for core in range(2):
                    remote(
                        columns_in.at[core], columns_in.at[core], wave_send.at[0], wave_recv.at[5 + core], me, other
                    ).wait_recv()
                for core in range(2):
                    eight[:, core * half : (core + 1) * half] = columns_in[core]

            @pl.when(jnp.logical_not(final_row))
            def _():
                parts = split_rows(eight[...])
                fresh = jnp.dot(parts, high[0], preferred_element_type=jnp.float32)
                fresh = fresh + jnp.dot(parts, low[0], preferred_element_type=jnp.float32)
                columns_out[...] = fresh[: 2 * few] + fresh[2 * few :] + local[...]
                for to in range(2):
                    onward_columns(to).start()

            few_in[...] = own_of(eight[...])
            send_home(0)
            state = few_in[...]
            for step in range(RING - 1):
                state = next_state(step, state)
                send_home(step + 1)

        for piece in range(2 * RING):
            @pl.when(piece != mine)
            def _():
                remote(
                    prior.at[piece], prior.at[piece], home_send.at[0, 0], home_recv.at[piece], me, other
                ).wait_recv()
        for piece in range(2 * RING):
            full[piece * few : (piece + 1) * few, :] = prior[piece]

        for part in range(2):
            for side in range(2):
                own_part(part, side).wait_send()
            own_sibling_map(part).wait_send()
            forward(part).wait_send()
            for step in range(1, RING):
                sibling_map(step, part).wait_send()
        for number, (step, to) in enumerate(partners):
            tip_copy(step, to, number).wait_send()

        @pl.when(row < PRODUCT_ROW - 1)
        def _():
            onward_rows(0).wait_send()

        @pl.when(jnp.logical_and(row == PRODUCT_ROW - 1, jnp.logical_not(final_row)))
        def _():
            for to in range(2):
                onward_pair(to).wait_send()

        @pl.when(jnp.logical_and(row >= PRODUCT_ROW, jnp.logical_not(final_row)))
        def _():
            for to in range(2):
                onward_columns(to).wait_send()

        for step in range(RING):
            for to in range(2):
                @pl.when(jnp.logical_or(x != step, tip != to))
                def _():
                    home_copy(step, to).wait_send()

    own_spikes.wait()
    spikes_out.wait()
    count = full.shape[0]
    parts = split_rows(full[...])
    fresh = jnp.dot(parts, maps[x, tip], preferred_element_type=jnp.float32)
    interface_ref[0] = fresh[:count] + fresh[count:]
    middle = spikes.shape[1]
    product = jnp.dot(parts[:count, :middle], spikes[0], preferred_element_type=jnp.float32)
    product_ref[0] = product + jnp.dot(parts[:count, middle:], spikes[1], preferred_element_type=jnp.float32)


def on_device(band_maps, right_tips, spikes, local_parts):
    rows_total = lax.axis_size("dom") // RING
    _, depth, half = band_maps.shape
    count = right_tips.shape[1]
    many = count // 2
    few = many // RING
    _, spike_rows, spike_columns = spikes.shape
    width = spike_columns // 2
    f32, b16, dma = jnp.float32, jnp.bfloat16, pltpu.SemaphoreType.DMA
    interface, product = pl.pallas_call(
        functools.partial(sweep, rows_total),
        out_shape=(
            jax.ShapeDtypeStruct((1, count, half), f32),
            jax.ShapeDtypeStruct((1, count, width), f32),
        ),
        in_specs=[
            pl.BlockSpec(memory_space=pltpu.HBM),
            pl.BlockSpec(memory_space=pltpu.HBM),
            pl.BlockSpec(memory_space=pltpu.HBM),
        ],
        out_specs=(pl.BlockSpec(memory_space=pltpu.VMEM),) * 2,
        scratch_shapes=[
            pltpu.VMEM((RING, 2, depth, half), b16),
            pltpu.VMEM((count, half), f32),
            pltpu.VMEM((RING, 2 * few, half), f32),
            pltpu.VMEM((RING, 2, 2 * few, half), f32),
            pltpu.VMEM((RING, 2, few, half), f32),
            pltpu.VMEM((2, many, half), f32),
            pltpu.VMEM((few, depth), f32),
            pltpu.VMEM((2, few, depth), f32),
            pltpu.VMEM((2, 2 * few, half), f32),
            pltpu.VMEM((2 * few, half), f32),
            pltpu.VMEM((2 * few, depth), f32),
            pltpu.VMEM((2 * few, half), f32),
            pltpu.VMEM((2, depth, half), b16),
            pltpu.VMEM((2, depth, half), b16),
            pltpu.VMEM((2, many, half), f32),
            pltpu.VMEM((2, many, half), f32),
            pltpu.VMEM((RING, few, depth), f32),
            pltpu.VMEM((2 * RING, few, depth), f32),
            pltpu.VMEM((2, many, half), f32),
            pltpu.VMEM((count, depth), f32),
            pltpu.VMEM((2, spike_rows, width), b16),
            dma((3,)),
            dma((RING, 2)),
            dma((RING, 2)),
            dma((2, 2)),
            dma((2, 2)),
            dma((2,)),
            dma((2,)),
            dma((2 * RING - 1,)),
            dma((RING, 2)),
            dma((2,)),
            dma((7,)),
            dma((RING, 2)),
            dma((2 * RING,)),
            dma((2,)),
            dma((2,)),
        ],
        compiler_params=pltpu.CompilerParams(
            collective_id=0, has_side_effects=True, vmem_limit_bytes=60 << 20
        ),
    )(band_maps, right_tips, spikes)
    return right_tips + interface, local_parts - product


def solution(mesh):
    return jax.shard_map(
        on_device,
        mesh=mesh,
        in_specs=(
            P("dom", None, "tip"),
            P("dom", None, "tip"),
            P("dom", "tip", None),
            P("dom", None, "tip"),
        ),
        out_specs=(P("dom", None, "tip"), P("dom", None, "tip")),
        check_vma=False,
    )
```

```python
import functools

import jax
import jax.numpy as jnp
from jax import lax
from jax.experimental import pallas as pl
from jax.experimental.pallas import tpu as pltpu
from jax.sharding import PartitionSpec as P

MESH = pl.DeviceIdType.MESH
RING = 4
CHAIN_ROWS = 3
PRODUCT_ROW = 5


def split_rows(value):
    high = value.astype(jnp.bfloat16)
    low = value - high.astype(jnp.float32)
    return jnp.concatenate([high.astype(jnp.float32), low], 0).astype(jnp.bfloat16)


def times_map(value, left, right):
    rows = value.shape[0]
    parts = split_rows(value)
    out = [jnp.dot(parts, half, preferred_element_type=jnp.float32) for half in (left, right)]
    return [piece[:rows] + piece[rows:] for piece in out]


def four_maps(maps, tip, high, low):
    depth, half = maps.shape[2], maps.shape[3]
    block = min(256, depth)

    for turn, step in enumerate((2, 1, 0)):
        def rows_of(index, _, turn=turn, step=step):
            rows = pl.ds(pl.multiple_of(index * block, block), block)
            total = None
            for h in range(2):
                lhs = maps[step, h, rows, :]
                if turn == 0:
                    factors = [maps[3, tip, h * half : (h + 1) * half, :]]
                else:
                    factors = [ref[(turn - 1) % 2, h * half : (h + 1) * half, :] for ref in (high, low)]
                for factor in factors:
                    term = jnp.dot(lhs, factor, preferred_element_type=jnp.float32)
                    total = term if total is None else total + term
            top = total.astype(jnp.bfloat16)
            high[turn % 2, rows, :] = top
            low[turn % 2, rows, :] = (total - top.astype(jnp.float32)).astype(jnp.bfloat16)
            return 0

        lax.fori_loop(0, depth // block, rows_of, 0)


def sweep(
    rows_total, maps_hbm, tips_hbm, spikes_hbm, interface_ref, product_ref,
    maps, tips_ref, tips_out, tips_both, tips_few, tips_many, few_in, pair_in, columns_in, columns_out, local,
    high, low, many_in, many_out, states, prior, prior_many, full, spikes,
    local_sem, sib_send, sib_recv, quarter_send, quarter_recv, link_send, link_recv, fwd_send, opp_recv,
    tip_send, tip_recv, wave_send, wave_recv, home_send, home_recv, side_send, side_recv,
):
    me, tip = lax.axis_index("dom"), lax.axis_index("tip")
    x, row = lax.rem(me, RING), lax.div(me, RING)
    other = 1 - tip
    base = me - x
    depth = maps_hbm.shape[1]
    half = maps_hbm.shape[2]
    cut = depth // 2
    width = spikes_hbm.shape[2] // 2
    chained = row < CHAIN_ROWS
    ringed = row >= CHAIN_ROWS
    last_chain = CHAIN_ROWS * RING - 1
    right, left = base + lax.rem(x + 1, RING), base + lax.rem(x + 3, RING)
    opposite = base + lax.rem(x + 2, RING)
    many = full.shape[0] // 2
    few = many // RING

    def remote(src, dst, send, recv, dom, to):
        return pltpu.make_async_remote_copy(
            src_ref=src, dst_ref=dst, send_sem=send, recv_sem=recv, device_id=(dom, to), device_id_type=MESH
        )

    barrier = pltpu.get_barrier_semaphore()

    def greet(dom, to):
        pl.semaphore_signal(barrier, inc=1, device_id=(dom, to), device_id_type=MESH)

    greet(me, other)

    @pl.when(chained)
    def _():
        @pl.when(me > 0)
        def _():
            greet(me - 1, tip)

        @pl.when(me == 1)
        def _():
            greet(0, other)

    @pl.when(ringed)
    def _():
        for step in range(1, RING):
            for to in range(2):
                greet(base + lax.rem(x + step, RING), to)
        before = jnp.where(row == CHAIN_ROWS, last_chain, me - RING)
        greet(before, tip)

        @pl.when(row >= PRODUCT_ROW)
        def _():
            greet(before, other)

    own_map = pltpu.make_async_copy(maps_hbm.at[0], maps.at[x, tip], local_sem.at[0])
    own_map.start()
    own_columns = pl.ds(pl.multiple_of(tip * width, width), width)
    other_columns = pl.ds(pl.multiple_of(other * width, width), width)
    own_spikes = pltpu.make_async_copy(spikes_hbm.at[0, :, own_columns], spikes.at[tip], local_sem.at[1])
    own_spikes.start()
    own_tips = pltpu.make_async_copy(tips_hbm.at[0], tips_ref, local_sem.at[2])
    own_tips.start()
    own_tips.wait()
    for piece in range(RING):
        for to in range(2):
            start = to * many + piece * few
            tips_out[piece, to * few : (to + 1) * few, :] = tips_ref[start : start + few, :]

    @pl.when(chained)
    def _():
        pl.semaphore_wait(barrier, jnp.where(me == last_chain, 1 + RING, jnp.where(me == 0, 3, 2)))

    @pl.when(ringed)
    def _():
        after = jnp.where(row == rows_total - 1, 0, jnp.where(row >= PRODUCT_ROW - 1, 2, 1))
        pl.semaphore_wait(barrier, 2 * RING - 1 + after)

    pieces = [slice(0, cut), slice(cut, depth)]

    def sibling_map(step, part):
        slot = lax.rem(x + step, RING)
        block = maps.at[slot, tip, pieces[part]]
        return remote(block, block, sib_send.at[step, part], sib_recv.at[step, part], me, other)

    def sibling_map_arrives(step, part):
        slot = lax.rem(x + step, RING)
        block = maps.at[slot, other, pieces[part]]
        remote(block, block, sib_send.at[step, part], sib_recv.at[step, part], me, other).wait_recv()

    def own_sibling_map(part):
        src = maps_hbm.at[0, pieces[part]]
        return remote(src, maps.at[x, tip, pieces[part]], sib_send.at[0, part], sib_recv.at[0, part], me, other)

    spikes_out = remote(
        spikes_hbm.at[0, :, other_columns], spikes.at[tip], side_send.at[0], side_recv.at[0], me, other
    )

    def first_rows(to):
        rows = slice(to * many, (to + 1) * many)
        return remote(tips_ref.at[rows, :], many_in.at[tip], wave_send.at[to], wave_recv.at[tip], 1, to)

    @pl.when(chained)
    def _():
        @pl.when(me == 0)
        def _():
            for to in range(2):
                first_rows(to).start()

        for part in range(2):
            own_sibling_map(part).start()
        tip_rows = pl.ds(pl.multiple_of(other * many, many), many)
        tips_copy = remote(
            tips_ref.at[tip_rows, :], tips_many.at[tip], tip_send.at[0], tip_recv.at[0, 1], me, other
        )
        tips_copy.start()
        spikes_out.start()
        own_map.wait()
        for part in range(2):
            sibling_map_arrives(0, part)
        tips_copy.wait_recv()

        def many_send(h, dom):
            return remote(many_out.at[h], many_in.at[h], wave_send.at[h], wave_recv.at[h], dom, tip)

        own_rows = pl.ds(pl.multiple_of(tip * many, many), many)
        tips_many[tip] = tips_ref[own_rows, :]

        @pl.when(me == 0)
        def _():
            many_in[...] = jnp.zeros_like(many_in)

        total = [None, None]
        for k in range(2):
            @pl.when(me > 0)
            def _():
                remote(many_in.at[k], many_in.at[k], wave_send.at[k], wave_recv.at[k], me, other).wait_recv()

            parts = split_rows(many_in[k])
            for h in range(2):
                term = jnp.dot(parts, maps[x, h, k * half : (k + 1) * half, :], preferred_element_type=jnp.float32)
                total[h] = term if k == 0 else total[h] + term
                if k == 1:
                    fresh = total[h][:many] + total[h][many:] + tips_many[h]
                    many_out[h] = fresh

                    @pl.when(jnp.logical_and(me > 0, me < last_chain))
                    def _():
                        many_send(h, me + 1).start()

        @pl.when(me == last_chain)
        def _():
            for piece in range(RING):
                for h in range(2):
                    states[piece, :, h * half : (h + 1) * half] = many_out[h, piece * few : (piece + 1) * few, :]
            for piece in range(RING):
                remote(
                    states.at[piece], few_in, home_send.at[piece, 0], wave_recv.at[2], last_chain + 1 + piece, tip
                ).start()

        to_sibling = remote(many_in, prior_many, side_send.at[1], side_recv.at[1], me, other)
        to_sibling.start()
        for h in range(2):
            full[own_rows, h * half : (h + 1) * half] = many_in[h]
        to_sibling.wait_recv()
        for h in range(2):
            full[tip_rows, h * half : (h + 1) * half] = prior_many[h]

        to_sibling.wait_send()
        tips_copy.wait_send()
        for part in range(2):
            own_sibling_map(part).wait_send()

        @pl.when(me == 0)
        def _():
            for to in range(2):
                first_rows(to).wait_send()

        @pl.when(jnp.logical_and(me > 0, me < last_chain))
        def _():
            for h in range(2):
                many_send(h, me + 1).wait_send()

        @pl.when(me == last_chain)
        def _():
            for piece in range(RING):
                remote(
                    states.at[piece], few_in, home_send.at[piece, 0], wave_recv.at[2], last_chain + 1 + piece, tip
                ).wait_send()

    @pl.when(ringed)
    def _():
        def own_part(part, side):
            return remote(
                maps_hbm.at[0, pieces[part]], maps.at[x, tip, pieces[part]],
                link_send.at[side, part], link_recv.at[side, part], right if side == 0 else left, tip,
            )

        def neighbour_arrives(part, side):
            slot = lax.rem(x + (3 if side == 0 else 1), RING)
            block = maps.at[slot, tip, pieces[part]]
            remote(block, block, link_send.at[side, part], link_recv.at[side, part], right, tip).wait_recv()

        def quarter(side, k):
            return slice(side * cut + k * (cut // 2), side * cut + (k + 1) * (cut // 2))

        def forward(side, k):
            slot = lax.rem(x + (3 if side == 0 else 1), RING)
            block = maps.at[slot, tip, quarter(side, k)]
            return remote(
                block, block, fwd_send.at[side, k], opp_recv.at[side, k], right if side == 0 else left, tip
            )

        def opposite_arrives(side, k):
            block = maps.at[lax.rem(x + 2, RING), tip, quarter(side, k)]
            remote(block, block, fwd_send.at[side, k], opp_recv.at[side, k], right, tip).wait_recv()

        def sibling_quarter(side, k):
            block = maps.at[lax.rem(x + 2, RING), tip, quarter(side, k)]
            return remote(block, block, quarter_send.at[side, k], quarter_recv.at[side, k], me, other)

        def sibling_quarter_arrives(side, k):
            block = maps.at[lax.rem(x + 2, RING), other, quarter(side, k)]
            remote(block, block, quarter_send.at[side, k], quarter_recv.at[side, k], me, other).wait_recv()

        own_part(0, 0).start()
        own_part(1, 1).start()
        own_part(1, 0).start()
        own_part(0, 1).start()

        def tip_copy(step, to, number):
            dst_x = lax.rem(x + step, RING)
            return remote(
                tips_out.at[dst_x], tips_both.at[x, tip],
                tip_send.at[number], tip_recv.at[step, jnp.where(to == tip, 0, 1)], base + dst_x, to,
            )

        partners = [(0, other), (1, tip), (1, other), (2, tip), (2, other), (3, tip), (3, other)]
        for number, (step, to) in enumerate(partners):
            tip_copy(step, to, number).start()
        tips_both[x, tip] = tips_out[x]
        for part in range(2):
            own_sibling_map(part).start()
        spikes_out.start()
        for part, side in ((0, 0), (1, 1)):
            neighbour_arrives(part, side)
            for k in range(2):
                forward(side, k).start()
            sibling_map(3 if side == 0 else 1, part).start()
        for part, side in ((1, 0), (0, 1)):
            neighbour_arrives(part, side)
            sibling_map(3 if side == 0 else 1, part).start()
        for k in range(2):
            for side in range(2):
                opposite_arrives(side, k)
                sibling_quarter(side, k).start()
        own_map.wait()
        for step in (0, 1, 3):
            for part in range(2):
                sibling_map_arrives(step, part)
        for k in range(2):
            for side in range(2):
                sibling_quarter_arrives(side, k)
        for step, to in partners:
            remote(
                tips_both.at[0, 0], tips_both.at[0, 0], tip_send.at[0],
                tip_recv.at[step, jnp.where(to == tip, 0, 1)], me, other,
            ).wait_recv()

        mine = tip * RING + x

        def home_copy(step, to):
            src = few_in if step == 0 else states.at[step - 1]
            return remote(src, prior.at[mine], home_send.at[step, to], home_recv.at[mine], base + step, to)

        def send_home(step):
            for to in range(2):
                @pl.when(jnp.logical_or(x != step, tip != to))
                def _():
                    home_copy(step, to).start()

            @pl.when(x == step)
            def _():
                prior[mine] = few_in[...] if step == 0 else states[step - 1]

        def next_state(step, state):
            fresh = times_map(state, maps[step, 0], maps[step, 1])
            for h in range(2):
                states[step, :, h * half : (h + 1) * half] = fresh[h] + tips_few[step, h]
            return states[step]

        def own_of(pair):
            return jnp.where(tip == 0, pair[:few], pair[few:])

        for step in range(RING):
            for h in range(2):
                tips_few[step, h] = own_of(tips_both[step, h])

        final_row = row == rows_total - 1
        direct = row < PRODUCT_ROW

        def onward_rows(to):
            return remote(states.at[RING - 1], few_in, wave_send.at[to], wave_recv.at[2], me + RING, tip)

        def onward_pair(to):
            return remote(
                states.at[RING - 1], pair_in.at[tip], wave_send.at[to], wave_recv.at[3 + tip], me + RING, to
            )

        def onward_columns(to):
            return remote(columns_out, columns_in.at[tip], wave_send.at[to], wave_recv.at[5 + tip], me + RING, to)

        @pl.when(direct)
        def _():
            remote(few_in, few_in, wave_send.at[0], wave_recv.at[2], me, other).wait_recv()
            state = few_in[...]
            for step in range(RING):
                state = next_state(step, state)

            @pl.when(row < PRODUCT_ROW - 1)
            def _():
                onward_rows(0).start()

            @pl.when(jnp.logical_and(row == PRODUCT_ROW - 1, jnp.logical_not(final_row)))
            def _():
                for to in range(2):
                    onward_pair(to).start()

            for step in range(RING):
                send_home(step)

        @pl.when(jnp.logical_not(direct))
        def _():
            @pl.when(jnp.logical_not(final_row))
            def _():
                four_maps(maps, tip, high, low)
                state = jnp.concatenate([tips_both[0, 0], tips_both[0, 1]], 1)
                for step in (1, 2):
                    fresh = times_map(state, maps[step, 0], maps[step, 1])
                    state = jnp.concatenate([fresh[h] + tips_both[step, h] for h in range(2)], 1)
                parts = split_rows(state)
                fresh = jnp.dot(parts, maps[3, tip], preferred_element_type=jnp.float32)
                local[...] = fresh[: 2 * few] + fresh[2 * few :] + tips_both[3, tip]

            @pl.when(row == PRODUCT_ROW)
            def _():
                for core in range(2):
                    remote(
                        pair_in.at[core], pair_in.at[core], wave_send.at[0], wave_recv.at[3 + core], me, other
                    ).wait_recv()
                for core in range(2):
                    for h in range(2):
                        columns_in[h, core * few : (core + 1) * few, :] = pair_in[core, :, h * half : (h + 1) * half]

            def columns_arrive(core):
                remote(
                    columns_in.at[core], columns_in.at[core], wave_send.at[0], wave_recv.at[5 + core], me, other
                ).wait_recv()

            @pl.when(final_row)
            def _():
                for core in range(2):
                    columns_arrive(core)

            @pl.when(jnp.logical_not(final_row))
            def _():
                total = local[...]
                for core in range(2):
                    @pl.when(row > PRODUCT_ROW)
                    def _():
                        columns_arrive(core)

                    parts = split_rows(columns_in[core])
                    for factor in (high, low):
                        rows = factor[0, core * half : (core + 1) * half, :]
                        fresh = jnp.dot(parts, rows, preferred_element_type=jnp.float32)
                        total = total + fresh[: 2 * few] + fresh[2 * few :]
                columns_out[...] = total
                for to in range(2):
                    onward_columns(to).start()

            for h in range(2):
                few_in[:, h * half : (h + 1) * half] = own_of(columns_in[h])
            send_home(0)
            state = few_in[...]
            for step in range(RING - 1):
                state = next_state(step, state)
                send_home(step + 1)

        for piece in range(2 * RING):
            @pl.when(piece != mine)
            def _():
                remote(
                    prior.at[piece], prior.at[piece], home_send.at[0, 0], home_recv.at[piece], me, other
                ).wait_recv()
        for piece in range(2 * RING):
            full[piece * few : (piece + 1) * few, :] = prior[piece]

        for part in range(2):
            for side in range(2):
                own_part(part, side).wait_send()
            own_sibling_map(part).wait_send()
            for k in range(2):
                forward(part, k).wait_send()
                sibling_quarter(part, k).wait_send()
            for step in (1, 3):
                sibling_map(step, part).wait_send()
        for number, (step, to) in enumerate(partners):
            tip_copy(step, to, number).wait_send()

        @pl.when(row < PRODUCT_ROW - 1)
        def _():
            onward_rows(0).wait_send()

        @pl.when(jnp.logical_and(row == PRODUCT_ROW - 1, jnp.logical_not(final_row)))
        def _():
            for to in range(2):
                onward_pair(to).wait_send()

        @pl.when(jnp.logical_and(row >= PRODUCT_ROW, jnp.logical_not(final_row)))
        def _():
            for to in range(2):
                onward_columns(to).wait_send()

        for step in range(RING):
            for to in range(2):
                @pl.when(jnp.logical_or(x != step, tip != to))
                def _():
                    home_copy(step, to).wait_send()

    own_spikes.wait()
    spikes_out.wait()
    count = full.shape[0]
    parts = split_rows(full[...])
    fresh = jnp.dot(parts, maps[x, tip], preferred_element_type=jnp.float32)
    interface_ref[0] = fresh[:count] + fresh[count:]
    middle = spikes.shape[1]
    product = jnp.dot(parts[:count, :middle], spikes[0], preferred_element_type=jnp.float32)
    product_ref[0] = product + jnp.dot(parts[:count, middle:], spikes[1], preferred_element_type=jnp.float32)


def on_device(band_maps, right_tips, spikes, local_parts):
    rows_total = lax.axis_size("dom") // RING
    _, depth, half = band_maps.shape
    count = right_tips.shape[1]
    many = count // 2
    few = many // RING
    _, spike_rows, spike_columns = spikes.shape
    width = spike_columns // 2
    f32, b16, dma = jnp.float32, jnp.bfloat16, pltpu.SemaphoreType.DMA
    interface, product = pl.pallas_call(
        functools.partial(sweep, rows_total),
        out_shape=(
            jax.ShapeDtypeStruct((1, count, half), f32),
            jax.ShapeDtypeStruct((1, count, width), f32),
        ),
        in_specs=[
            pl.BlockSpec(memory_space=pltpu.HBM),
            pl.BlockSpec(memory_space=pltpu.HBM),
            pl.BlockSpec(memory_space=pltpu.HBM),
        ],
        out_specs=(pl.BlockSpec(memory_space=pltpu.VMEM),) * 2,
        scratch_shapes=[
            pltpu.VMEM((RING, 2, depth, half), b16),
            pltpu.VMEM((count, half), f32),
            pltpu.VMEM((RING, 2 * few, half), f32),
            pltpu.VMEM((RING, 2, 2 * few, half), f32),
            pltpu.VMEM((RING, 2, few, half), f32),
            pltpu.VMEM((2, many, half), f32),
            pltpu.VMEM((few, depth), f32),
            pltpu.VMEM((2, few, depth), f32),
            pltpu.VMEM((2, 2 * few, half), f32),
            pltpu.VMEM((2 * few, half), f32),
            pltpu.VMEM((2 * few, half), f32),
            pltpu.VMEM((2, depth, half), b16),
            pltpu.VMEM((2, depth, half), b16),
            pltpu.VMEM((2, many, half), f32),
            pltpu.VMEM((2, many, half), f32),
            pltpu.VMEM((RING, few, depth), f32),
            pltpu.VMEM((2 * RING, few, depth), f32),
            pltpu.VMEM((2, many, half), f32),
            pltpu.VMEM((count, depth), f32),
            pltpu.VMEM((2, spike_rows, width), b16),
            dma((3,)),
            dma((RING, 2)),
            dma((RING, 2)),
            dma((2, 2)),
            dma((2, 2)),
            dma((2, 2)),
            dma((2, 2)),
            dma((2, 2)),
            dma((2, 2)),
            dma((2 * RING - 1,)),
            dma((RING, 2)),
            dma((2,)),
            dma((7,)),
            dma((RING, 2)),
            dma((2 * RING,)),
            dma((2,)),
            dma((2,)),
        ],
        compiler_params=pltpu.CompilerParams(
            collective_id=0, has_side_effects=True, vmem_limit_bytes=53 << 20
        ),
    )(band_maps, right_tips, spikes)
    return right_tips + interface, local_parts - product


def solution(mesh):
    return jax.shard_map(
        on_device,
        mesh=mesh,
        in_specs=(
            P("dom", None, "tip"),
            P("dom", None, "tip"),
            P("dom", "tip", None),
            P("dom", None, "tip"),
        ),
        out_specs=(P("dom", None, "tip"), P("dom", None, "tip")),
        check_vma=False,
    )
```

```python
import functools

import jax
import jax.numpy as jnp
from jax import lax
from jax.experimental import pallas as pl
from jax.experimental.pallas import tpu as pltpu
from jax.sharding import PartitionSpec as P

MESH = pl.DeviceIdType.MESH
RING = 4
CHAIN_ROWS = 3
PRODUCT_ROW = 4


def split_rows(value):
    high = value.astype(jnp.bfloat16)
    low = value - high.astype(jnp.float32)
    return jnp.concatenate([high.astype(jnp.float32), low], 0).astype(jnp.bfloat16)


def times_map(value, left, right):
    rows = value.shape[0]
    parts = split_rows(value)
    out = [jnp.dot(parts, half, preferred_element_type=jnp.float32) for half in (left, right)]
    return [piece[:rows] + piece[rows:] for piece in out]


def four_maps(maps, tip, high, low):
    half = maps.shape[3]
    block = min(256, half)
    for turn, step in enumerate((2, 1, 0)):
        factor = jnp.concatenate([maps[step, 0], maps[step, 1]], 1)
        for start in range(0, half, block):
            columns = slice(start, start + block)
            if turn == 0:
                total = jnp.dot(factor, maps[3, tip, :, columns], preferred_element_type=jnp.float32)
            else:
                total = jnp.dot(factor, high[(turn - 1) % 2, :, columns], preferred_element_type=jnp.float32)
                total += jnp.dot(factor, low[(turn - 1) % 2, :, columns], preferred_element_type=jnp.float32)
            top = total.astype(jnp.bfloat16)
            high[turn % 2, :, columns] = top
            low[turn % 2, :, columns] = (total - top.astype(jnp.float32)).astype(jnp.bfloat16)


def sweep(
    rows_total, maps_hbm, tips_hbm, spikes_hbm, interface_ref, product_ref,
    maps, tips_ref, tips_out, tips_both, tips_few, tips_many, few_in, pair_in, columns_in, columns_out, local,
    high, low, many_in, many_out, states, prior, prior_many, full, spikes,
    local_sem, sib_send, sib_recv, quarter_send, quarter_recv, link_send, link_recv, fwd_send, opp_recv,
    tip_send, tip_recv, wave_send, wave_recv, home_send, home_recv, side_send, side_recv,
):
    me, tip = lax.axis_index("dom"), lax.axis_index("tip")
    x, row = lax.rem(me, RING), lax.div(me, RING)
    other = 1 - tip
    base = me - x
    depth = maps_hbm.shape[1]
    half = maps_hbm.shape[2]
    cut = depth // 2
    width = spikes_hbm.shape[2] // 2
    chained = row < CHAIN_ROWS
    ringed = row >= CHAIN_ROWS
    last_chain = CHAIN_ROWS * RING - 1
    right, left = base + lax.rem(x + 1, RING), base + lax.rem(x + 3, RING)
    opposite = base + lax.rem(x + 2, RING)
    many = full.shape[0] // 2
    few = many // RING

    def remote(src, dst, send, recv, dom, to):
        return pltpu.make_async_remote_copy(
            src_ref=src, dst_ref=dst, send_sem=send, recv_sem=recv, device_id=(dom, to), device_id_type=MESH
        )

    barrier = pltpu.get_barrier_semaphore()

    def greet(dom, to):
        pl.semaphore_signal(barrier, inc=1, device_id=(dom, to), device_id_type=MESH)

    greet(me, other)

    @pl.when(chained)
    def _():
        @pl.when(me > 0)
        def _():
            greet(me - 1, tip)

        @pl.when(me == 1)
        def _():
            greet(0, other)

    @pl.when(ringed)
    def _():
        for step in range(1, RING):
            for to in range(2):
                greet(base + lax.rem(x + step, RING), to)
        before = jnp.where(row == CHAIN_ROWS, last_chain, me - RING)
        greet(before, tip)

        @pl.when(row >= PRODUCT_ROW)
        def _():
            greet(before, other)

    own_map = pltpu.make_async_copy(maps_hbm.at[0], maps.at[x, tip], local_sem.at[0])
    own_map.start()
    own_columns = pl.ds(pl.multiple_of(tip * width, width), width)
    other_columns = pl.ds(pl.multiple_of(other * width, width), width)
    own_spikes = pltpu.make_async_copy(spikes_hbm.at[0, :, own_columns], spikes.at[tip], local_sem.at[1])
    own_spikes.start()
    own_tips = pltpu.make_async_copy(tips_hbm.at[0], tips_ref, local_sem.at[2])
    own_tips.start()
    @pl.when(chained)
    def _():
        pl.semaphore_wait(barrier, jnp.where(me == last_chain, 1 + RING, jnp.where(me == 0, 3, 2)))

    @pl.when(ringed)
    def _():
        after = jnp.where(row == rows_total - 1, 0, jnp.where(row >= PRODUCT_ROW - 1, 2, 1))
        pl.semaphore_wait(barrier, 2 * RING - 1 + after)

    pieces = [slice(0, cut), slice(cut, depth)]

    def sibling_map(step, part):
        slot = lax.rem(x + step, RING)
        block = maps.at[slot, tip, pieces[part]]
        return remote(block, block, sib_send.at[step, part], sib_recv.at[step, part], me, other)

    def sibling_map_arrives(step, part):
        slot = lax.rem(x + step, RING)
        block = maps.at[slot, other, pieces[part]]
        remote(block, block, sib_send.at[step, part], sib_recv.at[step, part], me, other).wait_recv()

    def own_sibling_map(part):
        src = maps_hbm.at[0, pieces[part]]
        return remote(src, maps.at[x, tip, pieces[part]], sib_send.at[0, part], sib_recv.at[0, part], me, other)

    spikes_out = remote(
        spikes_hbm.at[0, :, other_columns], spikes.at[tip], side_send.at[0], side_recv.at[0], me, other
    )

    def first_rows(to):
        rows = slice(to * many, (to + 1) * many)
        return remote(tips_hbm.at[0, rows, :], many_in.at[tip], wave_send.at[to], wave_recv.at[tip], 1, to)

    @pl.when(chained)
    def _():
        @pl.when(me == 0)
        def _():
            for to in range(2):
                first_rows(to).start()

        own_tips.wait()
        for part in range(2):
            own_sibling_map(part).start()
        tip_rows = pl.ds(pl.multiple_of(other * many, many), many)
        tips_copy = remote(
            tips_ref.at[tip_rows, :], tips_many.at[tip], tip_send.at[0], tip_recv.at[0, 1], me, other
        )
        tips_copy.start()
        spikes_out.start()
        own_map.wait()
        for part in range(2):
            sibling_map_arrives(0, part)
        tips_copy.wait_recv()

        def many_send(h, dom):
            return remote(many_out.at[h], many_in.at[h], wave_send.at[h], wave_recv.at[h], dom, tip)

        own_rows = pl.ds(pl.multiple_of(tip * many, many), many)
        tips_many[tip] = tips_ref[own_rows, :]

        @pl.when(me == 0)
        def _():
            many_in[...] = jnp.zeros_like(many_in)

        total = [None, None]
        for k in range(2):
            @pl.when(me > 0)
            def _():
                remote(many_in.at[k], many_in.at[k], wave_send.at[k], wave_recv.at[k], me, other).wait_recv()

            parts = split_rows(many_in[k])
            for h in range(2):
                term = jnp.dot(parts, maps[x, h, k * half : (k + 1) * half, :], preferred_element_type=jnp.float32)
                total[h] = term if k == 0 else total[h] + term
                if k == 1:
                    fresh = total[h][:many] + total[h][many:] + tips_many[h]
                    many_out[h] = fresh

                    @pl.when(jnp.logical_and(me > 0, me < last_chain))
                    def _():
                        many_send(h, me + 1).start()

        @pl.when(me == last_chain)
        def _():
            for piece in range(RING):
                for h in range(2):
                    states[piece, :, h * half : (h + 1) * half] = many_out[h, piece * few : (piece + 1) * few, :]
            for piece in range(RING):
                remote(
                    states.at[piece], few_in, home_send.at[piece, 0], wave_recv.at[2], last_chain + 1 + piece, tip
                ).start()

        to_sibling = remote(many_in, prior_many, side_send.at[1], side_recv.at[1], me, other)
        to_sibling.start()
        for h in range(2):
            full[own_rows, h * half : (h + 1) * half] = many_in[h]
        to_sibling.wait_recv()
        for h in range(2):
            full[tip_rows, h * half : (h + 1) * half] = prior_many[h]

        to_sibling.wait_send()
        tips_copy.wait_send()
        for part in range(2):
            own_sibling_map(part).wait_send()

        @pl.when(me == 0)
        def _():
            for to in range(2):
                first_rows(to).wait_send()

        @pl.when(jnp.logical_and(me > 0, me < last_chain))
        def _():
            for h in range(2):
                many_send(h, me + 1).wait_send()

        @pl.when(me == last_chain)
        def _():
            for piece in range(RING):
                remote(
                    states.at[piece], few_in, home_send.at[piece, 0], wave_recv.at[2], last_chain + 1 + piece, tip
                ).wait_send()

    @pl.when(ringed)
    def _():
        def own_part(part, side):
            return remote(
                maps_hbm.at[0, pieces[part]], maps.at[x, tip, pieces[part]],
                link_send.at[side, part], link_recv.at[side, part], right if side == 0 else left, tip,
            )

        def neighbour_arrives(part, side):
            slot = lax.rem(x + (3 if side == 0 else 1), RING)
            block = maps.at[slot, tip, pieces[part]]
            remote(block, block, link_send.at[side, part], link_recv.at[side, part], right, tip).wait_recv()

        def quarter(side, k):
            return slice(side * cut + k * (cut // 2), side * cut + (k + 1) * (cut // 2))

        def forward(side, k):
            slot = lax.rem(x + (3 if side == 0 else 1), RING)
            block = maps.at[slot, tip, quarter(side, k)]
            return remote(
                block, block, fwd_send.at[side, k], opp_recv.at[side, k], right if side == 0 else left, tip
            )

        def opposite_arrives(side, k):
            block = maps.at[lax.rem(x + 2, RING), tip, quarter(side, k)]
            remote(block, block, fwd_send.at[side, k], opp_recv.at[side, k], right, tip).wait_recv()

        def sibling_quarter(side, k):
            block = maps.at[lax.rem(x + 2, RING), tip, quarter(side, k)]
            return remote(block, block, quarter_send.at[side, k], quarter_recv.at[side, k], me, other)

        def sibling_quarter_arrives(side, k):
            block = maps.at[lax.rem(x + 2, RING), other, quarter(side, k)]
            remote(block, block, quarter_send.at[side, k], quarter_recv.at[side, k], me, other).wait_recv()

        own_part(0, 0).start()
        own_part(1, 1).start()
        own_part(1, 0).start()
        own_part(0, 1).start()

        own_tips.wait()
        for piece in range(RING):
            for to in range(2):
                start = to * many + piece * few
                tips_out[piece, to * few : (to + 1) * few, :] = tips_ref[start : start + few, :]

        def tip_copy(step, to, number):
            dst_x = lax.rem(x + step, RING)
            return remote(
                tips_out.at[dst_x], tips_both.at[x, tip],
                tip_send.at[number], tip_recv.at[step, jnp.where(to == tip, 0, 1)], base + dst_x, to,
            )

        partners = [(0, other), (1, tip), (1, other), (2, tip), (2, other), (3, tip), (3, other)]
        for number, (step, to) in enumerate(partners):
            tip_copy(step, to, number).start()
        tips_both[x, tip] = tips_out[x]
        for part in range(2):
            own_sibling_map(part).start()
        spikes_out.start()
        for part, side in ((0, 0), (1, 1)):
            neighbour_arrives(part, side)
            for k in range(2):
                forward(side, k).start()
            sibling_map(3 if side == 0 else 1, part).start()
        for part, side in ((1, 0), (0, 1)):
            neighbour_arrives(part, side)
            sibling_map(3 if side == 0 else 1, part).start()
        for k in range(2):
            for side in range(2):
                opposite_arrives(side, k)
                sibling_quarter(side, k).start()
        own_map.wait()
        for step in (0, 1, 3):
            for part in range(2):
                sibling_map_arrives(step, part)
        for k in range(2):
            for side in range(2):
                sibling_quarter_arrives(side, k)
        for step, to in partners:
            remote(
                tips_both.at[0, 0], tips_both.at[0, 0], tip_send.at[0],
                tip_recv.at[step, jnp.where(to == tip, 0, 1)], me, other,
            ).wait_recv()

        mine = tip * RING + x

        def home_copy(step, to):
            src = few_in if step == 0 else states.at[step - 1]
            return remote(src, prior.at[mine], home_send.at[step, to], home_recv.at[mine], base + step, to)

        def send_home(step):
            for to in range(2):
                @pl.when(jnp.logical_or(x != step, tip != to))
                def _():
                    home_copy(step, to).start()

            @pl.when(x == step)
            def _():
                prior[mine] = few_in[...] if step == 0 else states[step - 1]

        def next_state(step, state):
            fresh = times_map(state, maps[step, 0], maps[step, 1])
            for h in range(2):
                states[step, :, h * half : (h + 1) * half] = fresh[h] + tips_few[step, h]
            return states[step]

        def own_of(pair):
            return jnp.where(tip == 0, pair[:few], pair[few:])

        for step in range(RING):
            for h in range(2):
                tips_few[step, h] = own_of(tips_both[step, h])

        final_row = row == rows_total - 1
        direct = row < PRODUCT_ROW

        def onward_rows(to):
            return remote(states.at[RING - 1], few_in, wave_send.at[to], wave_recv.at[2], me + RING, tip)

        def onward_pair(to):
            return remote(
                states.at[RING - 1], pair_in.at[tip], wave_send.at[to], wave_recv.at[3 + tip], me + RING, to
            )

        def onward_columns(to):
            return remote(columns_out, columns_in.at[tip], wave_send.at[to], wave_recv.at[5 + tip], me + RING, to)

        @pl.when(direct)
        def _():
            remote(few_in, few_in, wave_send.at[0], wave_recv.at[2], me, other).wait_recv()
            state = few_in[...]
            for step in range(RING):
                state = next_state(step, state)

            @pl.when(row < PRODUCT_ROW - 1)
            def _():
                onward_rows(0).start()

            @pl.when(jnp.logical_and(row == PRODUCT_ROW - 1, jnp.logical_not(final_row)))
            def _():
                for to in range(2):
                    onward_pair(to).start()

            for step in range(RING):
                send_home(step)

        @pl.when(jnp.logical_not(direct))
        def _():
            @pl.when(jnp.logical_not(final_row))
            def _():
                four_maps(maps, tip, high, low)
                state = jnp.concatenate([tips_both[0, 0], tips_both[0, 1]], 1)
                for step in (1, 2):
                    fresh = times_map(state, maps[step, 0], maps[step, 1])
                    state = jnp.concatenate([fresh[h] + tips_both[step, h] for h in range(2)], 1)
                parts = split_rows(state)
                fresh = jnp.dot(parts, maps[3, tip], preferred_element_type=jnp.float32)
                local[...] = fresh[: 2 * few] + fresh[2 * few :] + tips_both[3, tip]

            @pl.when(row == PRODUCT_ROW)
            def _():
                for core in range(2):
                    remote(
                        pair_in.at[core], pair_in.at[core], wave_send.at[0], wave_recv.at[3 + core], me, other
                    ).wait_recv()
                for core in range(2):
                    for h in range(2):
                        columns_in[h, core * few : (core + 1) * few, :] = pair_in[core, :, h * half : (h + 1) * half]

            def columns_arrive(core):
                remote(
                    columns_in.at[core], columns_in.at[core], wave_send.at[0], wave_recv.at[5 + core], me, other
                ).wait_recv()

            @pl.when(final_row)
            def _():
                for core in range(2):
                    columns_arrive(core)

            @pl.when(jnp.logical_not(final_row))
            def _():
                @pl.when(row > PRODUCT_ROW)
                def _():
                    for core in range(2):
                        columns_arrive(core)

                parts = split_rows(jnp.concatenate([columns_in[0], columns_in[1]], 1))
                fresh = jnp.dot(parts, high[0], preferred_element_type=jnp.float32)
                fresh = fresh + jnp.dot(parts, low[0], preferred_element_type=jnp.float32)
                columns_out[...] = fresh[: 2 * few] + fresh[2 * few :] + local[...]
                for to in range(2):
                    onward_columns(to).start()

            for h in range(2):
                few_in[:, h * half : (h + 1) * half] = own_of(columns_in[h])
            send_home(0)
            state = few_in[...]
            for step in range(RING - 1):
                state = next_state(step, state)
                send_home(step + 1)

        for piece in range(2 * RING):
            @pl.when(piece != mine)
            def _():
                remote(
                    prior.at[piece], prior.at[piece], home_send.at[0, 0], home_recv.at[piece], me, other
                ).wait_recv()
        for piece in range(2 * RING):
            full[piece * few : (piece + 1) * few, :] = prior[piece]

        for part in range(2):
            for side in range(2):
                own_part(part, side).wait_send()
            own_sibling_map(part).wait_send()
            for k in range(2):
                forward(part, k).wait_send()
                sibling_quarter(part, k).wait_send()
            for step in (1, 3):
                sibling_map(step, part).wait_send()
        for number, (step, to) in enumerate(partners):
            tip_copy(step, to, number).wait_send()

        @pl.when(row < PRODUCT_ROW - 1)
        def _():
            onward_rows(0).wait_send()

        @pl.when(jnp.logical_and(row == PRODUCT_ROW - 1, jnp.logical_not(final_row)))
        def _():
            for to in range(2):
                onward_pair(to).wait_send()

        @pl.when(jnp.logical_and(row >= PRODUCT_ROW, jnp.logical_not(final_row)))
        def _():
            for to in range(2):
                onward_columns(to).wait_send()

        for step in range(RING):
            for to in range(2):
                @pl.when(jnp.logical_or(x != step, tip != to))
                def _():
                    home_copy(step, to).wait_send()

    own_spikes.wait()
    spikes_out.wait()
    count = full.shape[0]
    parts = split_rows(full[...])
    fresh = jnp.dot(parts, maps[x, tip], preferred_element_type=jnp.float32)
    interface_ref[0] = fresh[:count] + fresh[count:]
    middle = spikes.shape[1]
    product = jnp.dot(parts[:count, :middle], spikes[0], preferred_element_type=jnp.float32)
    product_ref[0] = product + jnp.dot(parts[:count, middle:], spikes[1], preferred_element_type=jnp.float32)


def on_device(band_maps, right_tips, spikes, local_parts):
    rows_total = lax.axis_size("dom") // RING
    _, depth, half = band_maps.shape
    count = right_tips.shape[1]
    many = count // 2
    few = many // RING
    _, spike_rows, spike_columns = spikes.shape
    width = spike_columns // 2
    f32, b16, dma = jnp.float32, jnp.bfloat16, pltpu.SemaphoreType.DMA
    interface, product = pl.pallas_call(
        functools.partial(sweep, rows_total),
        out_shape=(
            jax.ShapeDtypeStruct((1, count, half), f32),
            jax.ShapeDtypeStruct((1, count, width), f32),
        ),
        in_specs=[
            pl.BlockSpec(memory_space=pltpu.HBM),
            pl.BlockSpec(memory_space=pltpu.HBM),
            pl.BlockSpec(memory_space=pltpu.HBM),
        ],
        out_specs=(pl.BlockSpec(memory_space=pltpu.VMEM),) * 2,
        scratch_shapes=[
            pltpu.VMEM((RING, 2, depth, half), b16),
            pltpu.VMEM((count, half), f32),
            pltpu.VMEM((RING, 2 * few, half), f32),
            pltpu.VMEM((RING, 2, 2 * few, half), f32),
            pltpu.VMEM((RING, 2, few, half), f32),
            pltpu.VMEM((2, many, half), f32),
            pltpu.VMEM((few, depth), f32),
            pltpu.VMEM((2, few, depth), f32),
            pltpu.VMEM((2, 2 * few, half), f32),
            pltpu.VMEM((2 * few, half), f32),
            pltpu.VMEM((2 * few, half), f32),
            pltpu.VMEM((2, depth, half), b16),
            pltpu.VMEM((2, depth, half), b16),
            pltpu.VMEM((2, many, half), f32),
            pltpu.VMEM((2, many, half), f32),
            pltpu.VMEM((RING, few, depth), f32),
            pltpu.VMEM((2 * RING, few, depth), f32),
            pltpu.VMEM((2, many, half), f32),
            pltpu.VMEM((count, depth), f32),
            pltpu.VMEM((2, spike_rows, width), b16),
            dma((3,)),
            dma((RING, 2)),
            dma((RING, 2)),
            dma((2, 2)),
            dma((2, 2)),
            dma((2, 2)),
            dma((2, 2)),
            dma((2, 2)),
            dma((2, 2)),
            dma((2 * RING - 1,)),
            dma((RING, 2)),
            dma((2,)),
            dma((7,)),
            dma((RING, 2)),
            dma((2 * RING,)),
            dma((2,)),
            dma((2,)),
        ],
        compiler_params=pltpu.CompilerParams(
            collective_id=0, has_side_effects=True, vmem_limit_bytes=53 << 20
        ),
    )(band_maps, right_tips, spikes)
    return right_tips + interface, local_parts - product


def solution(mesh):
    return jax.shard_map(
        on_device,
        mesh=mesh,
        in_specs=(
            P("dom", None, "tip"),
            P("dom", None, "tip"),
            P("dom", "tip", None),
            P("dom", None, "tip"),
        ),
        out_specs=(P("dom", None, "tip"), P("dom", None, "tip")),
        check_vma=False,
    )
```

```python
import functools

import jax
import jax.numpy as jnp
from jax import lax
from jax.experimental import pallas as pl
from jax.experimental.pallas import tpu as pltpu
from jax.sharding import PartitionSpec as P

MESH = pl.DeviceIdType.MESH
RING = 4
CHAIN_ROWS = 2
HELPED_ROWS = 2
PRODUCT_ROW = 6


def split_rows(value):
    high = value.astype(jnp.bfloat16)
    low = value - high.astype(jnp.float32)
    return jnp.concatenate([high.astype(jnp.float32), low], 0).astype(jnp.bfloat16)


def times_map(value, left, right):
    rows = value.shape[0]
    parts = split_rows(value)
    out = [jnp.dot(parts, half, preferred_element_type=jnp.float32) for half in (left, right)]
    return [piece[:rows] + piece[rows:] for piece in out]


def four_maps(maps, tip, high, low):
    half = maps.shape[3]
    block = min(256, half)
    for turn, step in enumerate((2, 1, 0)):
        factor = jnp.concatenate([maps[step, 0], maps[step, 1]], 1)
        for start in range(0, half, block):
            columns = slice(start, start + block)
            if turn == 0:
                total = jnp.dot(factor, maps[3, tip, :, columns], preferred_element_type=jnp.float32)
            else:
                total = jnp.dot(factor, high[(turn - 1) % 2, :, columns], preferred_element_type=jnp.float32)
                total += jnp.dot(factor, low[(turn - 1) % 2, :, columns], preferred_element_type=jnp.float32)
            top = total.astype(jnp.bfloat16)
            high[turn % 2, :, columns] = top
            low[turn % 2, :, columns] = (total - top.astype(jnp.float32)).astype(jnp.bfloat16)


def sweep(
    rows_total, maps_hbm, tips_hbm, spikes_hbm, interface_ref, product_ref,
    maps, tips_ref, tips_out, tips_both, tips_few, tips_many, few_in, pair_in, columns_in, columns_out, local,
    high, low, many_in, many_out, states, prior, prior_many, full, spikes,
    local_sem, sib_send, sib_recv, quarter_send, quarter_recv, relay, relay_send, relay_recv, relay_sib_send, relay_sib_recv,
    link_send, link_recv, fwd_send, opp_recv,
    tip_send, tip_recv, wave_send, wave_recv, home_send, home_recv, side_send, side_recv,
):
    me, tip = lax.axis_index("dom"), lax.axis_index("tip")
    x, row = lax.rem(me, RING), lax.div(me, RING)
    other = 1 - tip
    base = me - x
    depth = maps_hbm.shape[1]
    half = maps_hbm.shape[2]
    cut = depth // 2
    width = spikes_hbm.shape[2] // 2
    chained = row < CHAIN_ROWS
    ringed = row >= CHAIN_ROWS
    helped = jnp.logical_and(ringed, row < CHAIN_ROWS + HELPED_ROWS)
    alone = row >= CHAIN_ROWS + HELPED_ROWS
    helper = jnp.logical_and(chained, row >= CHAIN_ROWS - HELPED_ROWS)
    mirrored = (2 * CHAIN_ROWS - 1 - row) * RING
    relayed = maps_hbm.shape[1] // 4
    last_chain = CHAIN_ROWS * RING - 1
    right, left = base + lax.rem(x + 1, RING), base + lax.rem(x + 3, RING)
    opposite = base + lax.rem(x + 2, RING)
    many = full.shape[0] // 2
    few = many // RING

    def remote(src, dst, send, recv, dom, to):
        return pltpu.make_async_remote_copy(
            src_ref=src, dst_ref=dst, send_sem=send, recv_sem=recv, device_id=(dom, to), device_id_type=MESH
        )

    barrier = pltpu.get_barrier_semaphore()

    def greet(dom, to):
        pl.semaphore_signal(barrier, inc=1, device_id=(dom, to), device_id_type=MESH)

    greet(me, other)

    @pl.when(chained)
    def _():
        @pl.when(me > 0)
        def _():
            greet(me - 1, tip)

        @pl.when(me == 1)
        def _():
            greet(0, other)

        @pl.when(helper)
        def _():
            greet(mirrored + x, tip)

    @pl.when(ringed)
    def _():
        for step in range(1, RING):
            for to in range(2):
                greet(base + lax.rem(x + step, RING), to)
        before = jnp.where(row == CHAIN_ROWS, last_chain, me - RING)
        greet(before, tip)

        @pl.when(row >= PRODUCT_ROW)
        def _():
            greet(before, other)

    own_map = pltpu.make_async_copy(maps_hbm.at[0], maps.at[x, tip], local_sem.at[0])
    own_map.start()
    own_columns = pl.ds(pl.multiple_of(tip * width, width), width)
    other_columns = pl.ds(pl.multiple_of(other * width, width), width)
    own_spikes = pltpu.make_async_copy(spikes_hbm.at[0, :, own_columns], spikes.at[tip], local_sem.at[1])
    own_spikes.start()
    own_tips = pltpu.make_async_copy(tips_hbm.at[0], tips_ref, local_sem.at[2])
    own_tips.start()
    @pl.when(chained)
    def _():
        pl.semaphore_wait(barrier, jnp.where(me == last_chain, 1 + RING, jnp.where(me == 0, 3, 2)))

    @pl.when(ringed)
    def _():
        after = jnp.where(row == rows_total - 1, 0, jnp.where(row >= PRODUCT_ROW - 1, 2, 1))
        pl.semaphore_wait(barrier, 2 * RING - 1 + after + jnp.where(helped, 1, 0))

    pieces = [slice(0, cut), slice(cut, depth)]

    def sibling_map_arrives(step, part):
        slot = lax.rem(x + step, RING)
        block = maps.at[slot, other, pieces[part]]
        remote(block, block, sib_send.at[step, part], sib_recv.at[step, part], me, other).wait_recv()

    def own_sibling_map(part):
        src = maps_hbm.at[0, pieces[part]]
        return remote(src, maps.at[x, tip, pieces[part]], sib_send.at[0, part], sib_recv.at[0, part], me, other)

    spikes_out = remote(
        spikes_hbm.at[0, :, other_columns], spikes.at[tip], side_send.at[0], side_recv.at[0], me, other
    )

    def first_rows(to):
        rows = slice(to * many, (to + 1) * many)
        return remote(tips_hbm.at[0, rows, :], many_in.at[tip], wave_send.at[to], wave_recv.at[tip], 1, to)

    def relay_rows(k):
        start = depth - relayed + k * (relayed // 2)
        return slice(start, start + relayed // 2)

    def to_relay(k):
        src = maps_hbm.at[0, relay_rows(k)]
        return remote(src, relay.at[k], relay_send.at[0, k], relay_recv.at[0, k], mirrored + x, tip)

    def from_relay(step, k):
        dst = maps.at[x, tip, relay_rows(k)]
        dom = mirrored + lax.rem(x + step, RING)
        return remote(relay.at[k], dst, relay_send.at[step, k], relay_recv.at[step, k], dom, tip)

    def pass_on():
        for k in range(2):
            remote(relay.at[k], relay.at[k], relay_send.at[0, k], relay_recv.at[0, k], me, other).wait_recv()
            for step in range(1, RING):
                from_relay(step, k).start()

    @pl.when(chained)
    def _():
        @pl.when(me == 0)
        def _():
            for to in range(2):
                first_rows(to).start()

        own_tips.wait()
        for part in range(2):
            own_sibling_map(part).start()
        tip_rows = pl.ds(pl.multiple_of(other * many, many), many)
        tips_copy = remote(
            tips_ref.at[tip_rows, :], tips_many.at[tip], tip_send.at[0], tip_recv.at[0, 1], me, other
        )
        tips_copy.start()
        spikes_out.start()
        own_map.wait()
        for part in range(2):
            sibling_map_arrives(0, part)
        tips_copy.wait_recv()

        def many_send(h, dom):
            return remote(many_out.at[h], many_in.at[h], wave_send.at[h], wave_recv.at[h], dom, tip)

        own_rows = pl.ds(pl.multiple_of(tip * many, many), many)
        tips_many[tip] = tips_ref[own_rows, :]

        @pl.when(me == 0)
        def _():
            many_in[...] = jnp.zeros_like(many_in)

        @pl.when(jnp.logical_and(helper, row == CHAIN_ROWS - 1))
        def _():
            pass_on()

        total = [None, None]
        for k in range(2):
            @pl.when(me > 0)
            def _():
                remote(many_in.at[k], many_in.at[k], wave_send.at[k], wave_recv.at[k], me, other).wait_recv()

            parts = split_rows(many_in[k])
            for h in range(2):
                term = jnp.dot(parts, maps[x, h, k * half : (k + 1) * half, :], preferred_element_type=jnp.float32)
                total[h] = term if k == 0 else total[h] + term
                if k == 1:
                    fresh = total[h][:many] + total[h][many:] + tips_many[h]
                    many_out[h] = fresh

                    @pl.when(jnp.logical_and(me > 0, me < last_chain))
                    def _():
                        many_send(h, me + 1).start()

        @pl.when(me == last_chain)
        def _():
            for piece in range(RING):
                for h in range(2):
                    states[piece, :, h * half : (h + 1) * half] = many_out[h, piece * few : (piece + 1) * few, :]
            for piece in range(RING):
                remote(
                    states.at[piece], few_in, home_send.at[piece, 0], wave_recv.at[2], last_chain + 1 + piece, tip
                ).start()

        @pl.when(jnp.logical_and(helper, row < CHAIN_ROWS - 1))
        def _():
            pass_on()

        to_sibling = remote(many_in, prior_many, side_send.at[1], side_recv.at[1], me, other)
        to_sibling.start()
        for h in range(2):
            full[own_rows, h * half : (h + 1) * half] = many_in[h]
        to_sibling.wait_recv()
        for h in range(2):
            full[tip_rows, h * half : (h + 1) * half] = prior_many[h]

        @pl.when(helper)
        def _():
            for k in range(2):
                for step in range(1, RING):
                    from_relay(step, k).wait_send()

        to_sibling.wait_send()
        tips_copy.wait_send()
        for part in range(2):
            own_sibling_map(part).wait_send()

        @pl.when(me == 0)
        def _():
            for to in range(2):
                first_rows(to).wait_send()

        @pl.when(jnp.logical_and(me > 0, me < last_chain))
        def _():
            for h in range(2):
                many_send(h, me + 1).wait_send()

        @pl.when(me == last_chain)
        def _():
            for piece in range(RING):
                remote(
                    states.at[piece], few_in, home_send.at[piece, 0], wave_recv.at[2], last_chain + 1 + piece, tip
                ).wait_send()

    @pl.when(ringed)
    def _():
        class Gather:
            def __init__(self, count):
                self.cut = count // 2

            def rows(self, part, k=None):
                if k is None:
                    return slice(part * self.cut, (part + 1) * self.cut)
                size = self.cut // 2
                return slice(part * self.cut + k * size, part * self.cut + (k + 1) * size)

            def own(self, part, side):
                rows = self.rows(part)
                return remote(
                    maps_hbm.at[0, rows], maps.at[x, tip, rows],
                    link_send.at[side, part], link_recv.at[side, part], right if side == 0 else left, tip,
                )

            def neighbour_arrives(self, part, side):
                block = maps.at[lax.rem(x + (3 if side == 0 else 1), RING), tip, self.rows(part)]
                remote(block, block, link_send.at[side, part], link_recv.at[side, part], right, tip).wait_recv()

            def forward(self, side, k):
                block = maps.at[lax.rem(x + (3 if side == 0 else 1), RING), tip, self.rows(side, k)]
                dom = right if side == 0 else left
                return remote(block, block, fwd_send.at[side, k], opp_recv.at[side, k], dom, tip)

            def opposite_arrives(self, side, k):
                block = maps.at[lax.rem(x + 2, RING), tip, self.rows(side, k)]
                remote(block, block, fwd_send.at[side, k], opp_recv.at[side, k], right, tip).wait_recv()

            def to_sibling(self, step, part):
                block = maps.at[lax.rem(x + step, RING), tip, self.rows(part)]
                return remote(block, block, sib_send.at[step, part], sib_recv.at[step, part], me, other)

            def sibling_arrives(self, step, part):
                block = maps.at[lax.rem(x + step, RING), other, self.rows(part)]
                remote(block, block, sib_send.at[step, part], sib_recv.at[step, part], me, other).wait_recv()

            def quarter_to_sibling(self, side, k):
                block = maps.at[lax.rem(x + 2, RING), tip, self.rows(side, k)]
                return remote(block, block, quarter_send.at[side, k], quarter_recv.at[side, k], me, other)

            def sibling_quarter_arrives(self, side, k):
                block = maps.at[lax.rem(x + 2, RING), other, self.rows(side, k)]
                remote(block, block, quarter_send.at[side, k], quarter_recv.at[side, k], me, other).wait_recv()

            def start(self):
                for part, side in ((0, 0), (1, 1), (1, 0), (0, 1)):
                    self.own(part, side).start()

            def middle(self):
                for part, side in ((0, 0), (1, 1)):
                    self.neighbour_arrives(part, side)
                    for k in range(2):
                        self.forward(side, k).start()
                    self.to_sibling(3 if side == 0 else 1, part).start()
                for part, side in ((1, 0), (0, 1)):
                    self.neighbour_arrives(part, side)
                    self.to_sibling(3 if side == 0 else 1, part).start()

            def last(self):
                for k in range(2):
                    for side in range(2):
                        self.opposite_arrives(side, k)
                        self.quarter_to_sibling(side, k).start()
                for step in (1, 3):
                    for part in range(2):
                        self.sibling_arrives(step, part)
                for k in range(2):
                    for side in range(2):
                        self.sibling_quarter_arrives(side, k)

            def drain(self):
                for part in range(2):
                    for side in range(2):
                        self.own(part, side).wait_send()
                    for k in range(2):
                        self.forward(part, k).wait_send()
                        self.quarter_to_sibling(part, k).wait_send()
                    for step in (1, 3):
                        self.to_sibling(step, part).wait_send()

        whole, rest = Gather(depth), Gather(depth - relayed)

        def relayed_to_sibling(step, k):
            block = maps.at[lax.rem(x + RING - step, RING), tip, relay_rows(k)]
            return remote(block, block, relay_sib_send.at[step, k], relay_sib_recv.at[step, k], me, other)

        @pl.when(helped)
        def _():
            for k in range(2):
                to_relay(k).start()
            rest.start()

        @pl.when(alone)
        def _():
            whole.start()

        own_tips.wait()
        for piece in range(RING):
            for to in range(2):
                start = to * many + piece * few
                tips_out[piece, to * few : (to + 1) * few, :] = tips_ref[start : start + few, :]

        def tip_copy(step, to, number):
            dst_x = lax.rem(x + step, RING)
            return remote(
                tips_out.at[dst_x], tips_both.at[x, tip],
                tip_send.at[number], tip_recv.at[step, jnp.where(to == tip, 0, 1)], base + dst_x, to,
            )

        partners = [(0, other), (1, tip), (1, other), (2, tip), (2, other), (3, tip), (3, other)]
        for number, (step, to) in enumerate(partners):
            tip_copy(step, to, number).start()
        tips_both[x, tip] = tips_out[x]
        for part in range(2):
            own_sibling_map(part).start()
        spikes_out.start()

        @pl.when(alone)
        def _():
            whole.middle()
            whole.last()

        @pl.when(helped)
        def _():
            rest.middle()
            for k in range(2):
                for step in range(1, RING):
                    block = maps.at[lax.rem(x + RING - step, RING), tip, relay_rows(k)]
                    remote(block, block, relay_send.at[step, k], relay_recv.at[step, k], me, other).wait_recv()
                    relayed_to_sibling(step, k).start()
            rest.last()
            for k in range(2):
                for step in range(1, RING):
                    block = maps.at[lax.rem(x + RING - step, RING), other, relay_rows(k)]
                    remote(block, block, relay_sib_send.at[step, k], relay_sib_recv.at[step, k], me, other).wait_recv()

        own_map.wait()
        for part in range(2):
            sibling_map_arrives(0, part)
        for step, to in partners:
            remote(
                tips_both.at[0, 0], tips_both.at[0, 0], tip_send.at[0],
                tip_recv.at[step, jnp.where(to == tip, 0, 1)], me, other,
            ).wait_recv()

        mine = tip * RING + x

        def home_copy(step, to):
            src = few_in if step == 0 else states.at[step - 1]
            return remote(src, prior.at[mine], home_send.at[step, to], home_recv.at[mine], base + step, to)

        def send_home(step):
            for to in range(2):
                @pl.when(jnp.logical_or(x != step, tip != to))
                def _():
                    home_copy(step, to).start()

            @pl.when(x == step)
            def _():
                prior[mine] = few_in[...] if step == 0 else states[step - 1]

        def next_state(step, state):
            fresh = times_map(state, maps[step, 0], maps[step, 1])
            for h in range(2):
                states[step, :, h * half : (h + 1) * half] = fresh[h] + tips_few[step, h]
            return states[step]

        def own_of(pair):
            return jnp.where(tip == 0, pair[:few], pair[few:])

        for step in range(RING):
            for h in range(2):
                tips_few[step, h] = own_of(tips_both[step, h])

        final_row = row == rows_total - 1
        direct = row < PRODUCT_ROW

        def onward_rows(to):
            return remote(states.at[RING - 1], few_in, wave_send.at[to], wave_recv.at[2], me + RING, tip)

        def onward_pair(to):
            return remote(
                states.at[RING - 1], pair_in.at[tip], wave_send.at[to], wave_recv.at[3 + tip], me + RING, to
            )

        def onward_columns(to):
            return remote(columns_out, columns_in.at[tip], wave_send.at[to], wave_recv.at[5 + tip], me + RING, to)

        @pl.when(direct)
        def _():
            remote(few_in, few_in, wave_send.at[0], wave_recv.at[2], me, other).wait_recv()
            state = few_in[...]
            for step in range(RING):
                state = next_state(step, state)

            @pl.when(row < PRODUCT_ROW - 1)
            def _():
                onward_rows(0).start()

            @pl.when(jnp.logical_and(row == PRODUCT_ROW - 1, jnp.logical_not(final_row)))
            def _():
                for to in range(2):
                    onward_pair(to).start()

            for step in range(RING):
                send_home(step)

        @pl.when(jnp.logical_not(direct))
        def _():
            @pl.when(jnp.logical_not(final_row))
            def _():
                four_maps(maps, tip, high, low)
                state = jnp.concatenate([tips_both[0, 0], tips_both[0, 1]], 1)
                for step in (1, 2):
                    fresh = times_map(state, maps[step, 0], maps[step, 1])
                    state = jnp.concatenate([fresh[h] + tips_both[step, h] for h in range(2)], 1)
                parts = split_rows(state)
                fresh = jnp.dot(parts, maps[3, tip], preferred_element_type=jnp.float32)
                local[...] = fresh[: 2 * few] + fresh[2 * few :] + tips_both[3, tip]

            @pl.when(row == PRODUCT_ROW)
            def _():
                for core in range(2):
                    remote(
                        pair_in.at[core], pair_in.at[core], wave_send.at[0], wave_recv.at[3 + core], me, other
                    ).wait_recv()
                for core in range(2):
                    for h in range(2):
                        columns_in[h, core * few : (core + 1) * few, :] = pair_in[core, :, h * half : (h + 1) * half]

            def columns_arrive(core):
                remote(
                    columns_in.at[core], columns_in.at[core], wave_send.at[0], wave_recv.at[5 + core], me, other
                ).wait_recv()

            @pl.when(final_row)
            def _():
                for core in range(2):
                    columns_arrive(core)

            @pl.when(jnp.logical_not(final_row))
            def _():
                @pl.when(row > PRODUCT_ROW)
                def _():
                    for core in range(2):
                        columns_arrive(core)

                parts = split_rows(jnp.concatenate([columns_in[0], columns_in[1]], 1))
                fresh = jnp.dot(parts, high[0], preferred_element_type=jnp.float32)
                fresh = fresh + jnp.dot(parts, low[0], preferred_element_type=jnp.float32)
                columns_out[...] = fresh[: 2 * few] + fresh[2 * few :] + local[...]
                for to in range(2):
                    onward_columns(to).start()

            for h in range(2):
                few_in[:, h * half : (h + 1) * half] = own_of(columns_in[h])
            send_home(0)
            state = few_in[...]
            for step in range(RING - 1):
                state = next_state(step, state)
                send_home(step + 1)

        for piece in range(2 * RING):
            @pl.when(piece != mine)
            def _():
                remote(
                    prior.at[piece], prior.at[piece], home_send.at[0, 0], home_recv.at[piece], me, other
                ).wait_recv()
        for piece in range(2 * RING):
            full[piece * few : (piece + 1) * few, :] = prior[piece]

        @pl.when(alone)
        def _():
            whole.drain()

        @pl.when(helped)
        def _():
            rest.drain()
            for k in range(2):
                to_relay(k).wait_send()
                for step in range(1, RING):
                    relayed_to_sibling(step, k).wait_send()

        for part in range(2):
            own_sibling_map(part).wait_send()
        for number, (step, to) in enumerate(partners):
            tip_copy(step, to, number).wait_send()

        @pl.when(row < PRODUCT_ROW - 1)
        def _():
            onward_rows(0).wait_send()

        @pl.when(jnp.logical_and(row == PRODUCT_ROW - 1, jnp.logical_not(final_row)))
        def _():
            for to in range(2):
                onward_pair(to).wait_send()

        @pl.when(jnp.logical_and(row >= PRODUCT_ROW, jnp.logical_not(final_row)))
        def _():
            for to in range(2):
                onward_columns(to).wait_send()

        for step in range(RING):
            for to in range(2):
                @pl.when(jnp.logical_or(x != step, tip != to))
                def _():
                    home_copy(step, to).wait_send()

    own_spikes.wait()
    spikes_out.wait()
    count = full.shape[0]
    parts = split_rows(full[...])
    fresh = jnp.dot(parts, maps[x, tip], preferred_element_type=jnp.float32)
    interface_ref[0] = fresh[:count] + fresh[count:]
    middle = spikes.shape[1]
    product = jnp.dot(parts[:count, :middle], spikes[0], preferred_element_type=jnp.float32)
    product_ref[0] = product + jnp.dot(parts[:count, middle:], spikes[1], preferred_element_type=jnp.float32)


def on_device(band_maps, right_tips, spikes, local_parts):
    rows_total = lax.axis_size("dom") // RING
    _, depth, half = band_maps.shape
    count = right_tips.shape[1]
    many = count // 2
    few = many // RING
    _, spike_rows, spike_columns = spikes.shape
    width = spike_columns // 2
    f32, b16, dma = jnp.float32, jnp.bfloat16, pltpu.SemaphoreType.DMA
    interface, product = pl.pallas_call(
        functools.partial(sweep, rows_total),
        out_shape=(
            jax.ShapeDtypeStruct((1, count, half), f32),
            jax.ShapeDtypeStruct((1, count, width), f32),
        ),
        in_specs=[
            pl.BlockSpec(memory_space=pltpu.HBM),
            pl.BlockSpec(memory_space=pltpu.HBM),
            pl.BlockSpec(memory_space=pltpu.HBM),
        ],
        out_specs=(pl.BlockSpec(memory_space=pltpu.VMEM),) * 2,
        scratch_shapes=[
            pltpu.VMEM((RING, 2, depth, half), b16),
            pltpu.VMEM((count, half), f32),
            pltpu.VMEM((RING, 2 * few, half), f32),
            pltpu.VMEM((RING, 2, 2 * few, half), f32),
            pltpu.VMEM((RING, 2, few, half), f32),
            pltpu.VMEM((2, many, half), f32),
            pltpu.VMEM((few, depth), f32),
            pltpu.VMEM((2, few, depth), f32),
            pltpu.VMEM((2, 2 * few, half), f32),
            pltpu.VMEM((2 * few, half), f32),
            pltpu.VMEM((2 * few, half), f32),
            pltpu.VMEM((2, depth, half), b16),
            pltpu.VMEM((2, depth, half), b16),
            pltpu.VMEM((2, many, half), f32),
            pltpu.VMEM((2, many, half), f32),
            pltpu.VMEM((RING, few, depth), f32),
            pltpu.VMEM((2 * RING, few, depth), f32),
            pltpu.VMEM((2, many, half), f32),
            pltpu.VMEM((count, depth), f32),
            pltpu.VMEM((2, spike_rows, width), b16),
            dma((3,)),
            dma((RING, 2)),
            dma((RING, 2)),
            dma((2, 2)),
            dma((2, 2)),
            pltpu.VMEM((2, depth // 8, half), b16),
            dma((RING, 2)),
            dma((RING, 2)),
            dma((RING, 2)),
            dma((RING, 2)),
            dma((2, 2)),
            dma((2, 2)),
            dma((2, 2)),
            dma((2, 2)),
            dma((2 * RING - 1,)),
            dma((RING, 2)),
            dma((2,)),
            dma((7,)),
            dma((RING, 2)),
            dma((2 * RING,)),
            dma((2,)),
            dma((2,)),
        ],
        compiler_params=pltpu.CompilerParams(
            collective_id=0, has_side_effects=True, vmem_limit_bytes=53 << 20
        ),
    )(band_maps, right_tips, spikes)
    return right_tips + interface, local_parts - product


def solution(mesh):
    return jax.shard_map(
        on_device,
        mesh=mesh,
        in_specs=(
            P("dom", None, "tip"),
            P("dom", None, "tip"),
            P("dom", "tip", None),
            P("dom", None, "tip"),
        ),
        out_specs=(P("dom", None, "tip"), P("dom", None, "tip")),
        check_vma=False,
    )
```

```python
import functools

import jax
import jax.numpy as jnp
from jax import lax
from jax.experimental import pallas as pl
from jax.experimental.pallas import tpu as pltpu
from jax.sharding import PartitionSpec as P

MESH = pl.DeviceIdType.MESH
RING = 4
CHAIN_ROWS = 2
HELPED_ROWS = 4
PRODUCT_ROW = 4


def split_rows(value):
    high = value.astype(jnp.bfloat16)
    low = value - high.astype(jnp.float32)
    return jnp.concatenate([high.astype(jnp.float32), low], 0).astype(jnp.bfloat16)


def times_map(value, left, right):
    rows = value.shape[0]
    parts = split_rows(value)
    out = [jnp.dot(parts, half, preferred_element_type=jnp.float32) for half in (left, right)]
    return [piece[:rows] + piece[rows:] for piece in out]


def four_maps(maps, tip, high, low):
    half = maps.shape[3]
    block = min(256, half)
    for turn, step in enumerate((2, 1, 0)):
        factor = jnp.concatenate([maps[step, 0], maps[step, 1]], 1)
        for start in range(0, half, block):
            columns = slice(start, start + block)
            if turn == 0:
                total = jnp.dot(factor, maps[3, tip, :, columns], preferred_element_type=jnp.float32)
            else:
                total = jnp.dot(factor, high[(turn - 1) % 2, :, columns], preferred_element_type=jnp.float32)
                total += jnp.dot(factor, low[(turn - 1) % 2, :, columns], preferred_element_type=jnp.float32)
            top = total.astype(jnp.bfloat16)
            high[turn % 2, :, columns] = top
            low[turn % 2, :, columns] = (total - top.astype(jnp.float32)).astype(jnp.bfloat16)


def sweep(
    rows_total, maps_hbm, tips_hbm, spikes_hbm, interface_ref, product_ref,
    maps, tips_ref, tips_out, tips_both, tips_few, tips_many, few_in, pair_in, columns_in, columns_out, local,
    high, low, many_in, many_out, states, prior, prior_many, full, spikes,
    local_sem, sib_send, sib_recv, quarter_send, quarter_recv, relay, relay_send, relay_recv, relay_sib_send, relay_sib_recv,
    link_send, link_recv, fwd_send, opp_recv,
    tip_send, tip_recv, wave_send, wave_recv, home_send, home_recv, side_send, side_recv,
):
    me, tip = lax.axis_index("dom"), lax.axis_index("tip")
    x, row = lax.rem(me, RING), lax.div(me, RING)
    other = 1 - tip
    base = me - x
    depth = maps_hbm.shape[1]
    half = maps_hbm.shape[2]
    cut = depth // 2
    width = spikes_hbm.shape[2] // 2
    chained = row < CHAIN_ROWS
    ringed = row >= CHAIN_ROWS
    helped = jnp.logical_and(ringed, row < CHAIN_ROWS + HELPED_ROWS)
    alone = row >= CHAIN_ROWS + HELPED_ROWS
    helping = rows_total - 4
    served = CHAIN_ROWS + lax.rem(row - helping + 4 * rows_total - CHAIN_ROWS, 4)
    helper = jnp.logical_and(row >= helping, served < CHAIN_ROWS + HELPED_ROWS)
    mirrored = jnp.where(helped, helping + lax.rem(row, 4), served) * RING
    relayed = maps_hbm.shape[1] // 4
    last_chain = CHAIN_ROWS * RING - 1
    right, left = base + lax.rem(x + 1, RING), base + lax.rem(x + 3, RING)
    opposite = base + lax.rem(x + 2, RING)
    many = full.shape[0] // 2
    few = many // RING

    def remote(src, dst, send, recv, dom, to):
        return pltpu.make_async_remote_copy(
            src_ref=src, dst_ref=dst, send_sem=send, recv_sem=recv, device_id=(dom, to), device_id_type=MESH
        )

    barrier = pltpu.get_barrier_semaphore()

    def greet(dom, to):
        pl.semaphore_signal(barrier, inc=1, device_id=(dom, to), device_id_type=MESH)

    greet(me, other)

    @pl.when(chained)
    def _():
        @pl.when(me > 0)
        def _():
            greet(me - 1, tip)

        @pl.when(me == 1)
        def _():
            greet(0, other)

    @pl.when(ringed)
    def _():
        for step in range(1, RING):
            for to in range(2):
                greet(base + lax.rem(x + step, RING), to)
        before = jnp.where(row == CHAIN_ROWS, last_chain, me - RING)
        greet(before, tip)

        @pl.when(row >= PRODUCT_ROW)
        def _():
            greet(before, other)

        @pl.when(helper)
        def _():
            greet(mirrored + x, tip)

    own_map = pltpu.make_async_copy(maps_hbm.at[0], maps.at[x, tip], local_sem.at[0])
    own_map.start()
    own_columns = pl.ds(pl.multiple_of(tip * width, width), width)
    other_columns = pl.ds(pl.multiple_of(other * width, width), width)
    own_spikes = pltpu.make_async_copy(spikes_hbm.at[0, :, own_columns], spikes.at[tip], local_sem.at[1])
    own_spikes.start()
    own_tips = pltpu.make_async_copy(tips_hbm.at[0], tips_ref, local_sem.at[2])
    own_tips.start()
    @pl.when(chained)
    def _():
        pl.semaphore_wait(barrier, jnp.where(me == last_chain, 1 + RING, jnp.where(me == 0, 3, 2)))

    @pl.when(ringed)
    def _():
        after = jnp.where(row == rows_total - 1, 0, jnp.where(row >= PRODUCT_ROW - 1, 2, 1))
        pl.semaphore_wait(barrier, 2 * RING - 1 + after + jnp.where(helped, 1, 0))

    pieces = [slice(0, cut), slice(cut, depth)]

    def sibling_map_arrives(step, part):
        slot = lax.rem(x + step, RING)
        block = maps.at[slot, other, pieces[part]]
        remote(block, block, sib_send.at[step, part], sib_recv.at[step, part], me, other).wait_recv()

    def own_sibling_map(part):
        src = maps_hbm.at[0, pieces[part]]
        return remote(src, maps.at[x, tip, pieces[part]], sib_send.at[0, part], sib_recv.at[0, part], me, other)

    spikes_out = remote(
        spikes_hbm.at[0, :, other_columns], spikes.at[tip], side_send.at[0], side_recv.at[0], me, other
    )

    def first_rows(to):
        rows = slice(to * many, (to + 1) * many)
        return remote(tips_hbm.at[0, rows, :], many_in.at[tip], wave_send.at[to], wave_recv.at[tip], 1, to)

    def relay_rows(k):
        start = depth - relayed + k * (relayed // 2)
        return slice(start, start + relayed // 2)

    def to_relay(k):
        src = maps_hbm.at[0, relay_rows(k)]
        return remote(src, relay.at[k], relay_send.at[0, k], relay_recv.at[0, k], mirrored + x, tip)

    def from_relay(step, k):
        dst = maps.at[x, tip, relay_rows(k)]
        dom = mirrored + lax.rem(x + step, RING)
        return remote(relay.at[k], dst, relay_send.at[step, k], relay_recv.at[step, k], dom, tip)

    def pass_on():
        for k in range(2):
            remote(relay.at[k], relay.at[k], relay_send.at[0, k], relay_recv.at[0, k], me, other).wait_recv()
            for step in range(1, RING):
                from_relay(step, k).start()

    @pl.when(chained)
    def _():
        @pl.when(me == 0)
        def _():
            for to in range(2):
                first_rows(to).start()

        own_tips.wait()
        for part in range(2):
            own_sibling_map(part).start()
        tip_rows = pl.ds(pl.multiple_of(other * many, many), many)
        tips_copy = remote(
            tips_ref.at[tip_rows, :], tips_many.at[tip], tip_send.at[0], tip_recv.at[0, 1], me, other
        )
        tips_copy.start()
        spikes_out.start()
        own_map.wait()
        for part in range(2):
            sibling_map_arrives(0, part)
        tips_copy.wait_recv()

        def many_send(h, dom):
            return remote(many_out.at[h], many_in.at[h], wave_send.at[h], wave_recv.at[h], dom, tip)

        own_rows = pl.ds(pl.multiple_of(tip * many, many), many)
        tips_many[tip] = tips_ref[own_rows, :]

        @pl.when(me == 0)
        def _():
            many_in[...] = jnp.zeros_like(many_in)

        total = [None, None]
        for k in range(2):
            @pl.when(me > 0)
            def _():
                remote(many_in.at[k], many_in.at[k], wave_send.at[k], wave_recv.at[k], me, other).wait_recv()

            parts = split_rows(many_in[k])
            for h in range(2):
                term = jnp.dot(parts, maps[x, h, k * half : (k + 1) * half, :], preferred_element_type=jnp.float32)
                total[h] = term if k == 0 else total[h] + term
                if k == 1:
                    fresh = total[h][:many] + total[h][many:] + tips_many[h]
                    many_out[h] = fresh

                    @pl.when(jnp.logical_and(me > 0, me < last_chain))
                    def _():
                        many_send(h, me + 1).start()

        @pl.when(me == last_chain)
        def _():
            for piece in range(RING):
                for h in range(2):
                    states[piece, :, h * half : (h + 1) * half] = many_out[h, piece * few : (piece + 1) * few, :]
            for piece in range(RING):
                remote(
                    states.at[piece], few_in, home_send.at[piece, 0], wave_recv.at[2], last_chain + 1 + piece, tip
                ).start()

        to_sibling = remote(many_in, prior_many, side_send.at[1], side_recv.at[1], me, other)
        to_sibling.start()
        for h in range(2):
            full[own_rows, h * half : (h + 1) * half] = many_in[h]
        to_sibling.wait_recv()
        for h in range(2):
            full[tip_rows, h * half : (h + 1) * half] = prior_many[h]

        to_sibling.wait_send()
        tips_copy.wait_send()
        for part in range(2):
            own_sibling_map(part).wait_send()

        @pl.when(me == 0)
        def _():
            for to in range(2):
                first_rows(to).wait_send()

        @pl.when(jnp.logical_and(me > 0, me < last_chain))
        def _():
            for h in range(2):
                many_send(h, me + 1).wait_send()

        @pl.when(me == last_chain)
        def _():
            for piece in range(RING):
                remote(
                    states.at[piece], few_in, home_send.at[piece, 0], wave_recv.at[2], last_chain + 1 + piece, tip
                ).wait_send()

    @pl.when(ringed)
    def _():
        class Gather:
            def __init__(self, count):
                self.cut = count // 2

            def rows(self, part, k=None):
                if k is None:
                    return slice(part * self.cut, (part + 1) * self.cut)
                size = self.cut // 2
                return slice(part * self.cut + k * size, part * self.cut + (k + 1) * size)

            def own(self, part, side):
                rows = self.rows(part)
                return remote(
                    maps_hbm.at[0, rows], maps.at[x, tip, rows],
                    link_send.at[side, part], link_recv.at[side, part], right if side == 0 else left, tip,
                )

            def neighbour_arrives(self, part, side):
                block = maps.at[lax.rem(x + (3 if side == 0 else 1), RING), tip, self.rows(part)]
                remote(block, block, link_send.at[side, part], link_recv.at[side, part], right, tip).wait_recv()

            def forward(self, side, k):
                block = maps.at[lax.rem(x + (3 if side == 0 else 1), RING), tip, self.rows(side, k)]
                dom = right if side == 0 else left
                return remote(block, block, fwd_send.at[side, k], opp_recv.at[side, k], dom, tip)

            def opposite_arrives(self, side, k):
                block = maps.at[lax.rem(x + 2, RING), tip, self.rows(side, k)]
                remote(block, block, fwd_send.at[side, k], opp_recv.at[side, k], right, tip).wait_recv()

            def to_sibling(self, step, part):
                block = maps.at[lax.rem(x + step, RING), tip, self.rows(part)]
                return remote(block, block, sib_send.at[step, part], sib_recv.at[step, part], me, other)

            def sibling_arrives(self, step, part):
                block = maps.at[lax.rem(x + step, RING), other, self.rows(part)]
                remote(block, block, sib_send.at[step, part], sib_recv.at[step, part], me, other).wait_recv()

            def quarter_to_sibling(self, side, k):
                block = maps.at[lax.rem(x + 2, RING), tip, self.rows(side, k)]
                return remote(block, block, quarter_send.at[side, k], quarter_recv.at[side, k], me, other)

            def sibling_quarter_arrives(self, side, k):
                block = maps.at[lax.rem(x + 2, RING), other, self.rows(side, k)]
                remote(block, block, quarter_send.at[side, k], quarter_recv.at[side, k], me, other).wait_recv()

            def start(self):
                for part, side in ((0, 0), (1, 1), (1, 0), (0, 1)):
                    self.own(part, side).start()

            def middle(self):
                for part, side in ((0, 0), (1, 1)):
                    self.neighbour_arrives(part, side)
                    for k in range(2):
                        self.forward(side, k).start()
                    self.to_sibling(3 if side == 0 else 1, part).start()
                for part, side in ((1, 0), (0, 1)):
                    self.neighbour_arrives(part, side)
                    self.to_sibling(3 if side == 0 else 1, part).start()

            def last(self):
                for k in range(2):
                    for side in range(2):
                        self.opposite_arrives(side, k)
                        self.quarter_to_sibling(side, k).start()
                for step in (1, 3):
                    for part in range(2):
                        self.sibling_arrives(step, part)
                for k in range(2):
                    for side in range(2):
                        self.sibling_quarter_arrives(side, k)

            def drain(self):
                for part in range(2):
                    for side in range(2):
                        self.own(part, side).wait_send()
                    for k in range(2):
                        self.forward(part, k).wait_send()
                        self.quarter_to_sibling(part, k).wait_send()
                    for step in (1, 3):
                        self.to_sibling(step, part).wait_send()

        whole, rest = Gather(depth), Gather(depth - relayed)

        def relayed_to_sibling(step, k):
            block = maps.at[lax.rem(x + RING - step, RING), tip, relay_rows(k)]
            return remote(block, block, relay_sib_send.at[step, k], relay_sib_recv.at[step, k], me, other)

        @pl.when(helped)
        def _():
            for k in range(2):
                to_relay(k).start()
            rest.start()

        @pl.when(alone)
        def _():
            whole.start()

        own_tips.wait()
        for piece in range(RING):
            for to in range(2):
                start = to * many + piece * few
                tips_out[piece, to * few : (to + 1) * few, :] = tips_ref[start : start + few, :]

        def tip_copy(step, to, number):
            dst_x = lax.rem(x + step, RING)
            return remote(
                tips_out.at[dst_x], tips_both.at[x, tip],
                tip_send.at[number], tip_recv.at[step, jnp.where(to == tip, 0, 1)], base + dst_x, to,
            )

        partners = [(0, other), (1, tip), (1, other), (2, tip), (2, other), (3, tip), (3, other)]
        for number, (step, to) in enumerate(partners):
            tip_copy(step, to, number).start()
        tips_both[x, tip] = tips_out[x]
        for part in range(2):
            own_sibling_map(part).start()
        spikes_out.start()

        @pl.when(helper)
        def _():
            pass_on()

        @pl.when(alone)
        def _():
            whole.middle()
            whole.last()

        @pl.when(helped)
        def _():
            rest.middle()
            for k in range(2):
                for step in range(1, RING):
                    block = maps.at[lax.rem(x + RING - step, RING), tip, relay_rows(k)]
                    remote(block, block, relay_send.at[step, k], relay_recv.at[step, k], me, other).wait_recv()
                    relayed_to_sibling(step, k).start()
            rest.last()
            for k in range(2):
                for step in range(1, RING):
                    block = maps.at[lax.rem(x + RING - step, RING), other, relay_rows(k)]
                    remote(block, block, relay_sib_send.at[step, k], relay_sib_recv.at[step, k], me, other).wait_recv()

        own_map.wait()
        for part in range(2):
            sibling_map_arrives(0, part)
        for step, to in partners:
            remote(
                tips_both.at[0, 0], tips_both.at[0, 0], tip_send.at[0],
                tip_recv.at[step, jnp.where(to == tip, 0, 1)], me, other,
            ).wait_recv()

        mine = tip * RING + x

        def home_copy(step, to):
            src = few_in if step == 0 else states.at[step - 1]
            return remote(src, prior.at[mine], home_send.at[step, to], home_recv.at[mine], base + step, to)

        def send_home(step):
            for to in range(2):
                @pl.when(jnp.logical_or(x != step, tip != to))
                def _():
                    home_copy(step, to).start()

            @pl.when(x == step)
            def _():
                prior[mine] = few_in[...] if step == 0 else states[step - 1]

        def next_state(step, state):
            fresh = times_map(state, maps[step, 0], maps[step, 1])
            for h in range(2):
                states[step, :, h * half : (h + 1) * half] = fresh[h] + tips_few[step, h]
            return states[step]

        def own_of(pair):
            return jnp.where(tip == 0, pair[:few], pair[few:])

        for step in range(RING):
            for h in range(2):
                tips_few[step, h] = own_of(tips_both[step, h])

        final_row = row == rows_total - 1
        direct = row < PRODUCT_ROW

        def onward_rows(to):
            return remote(states.at[RING - 1], few_in, wave_send.at[to], wave_recv.at[2], me + RING, tip)

        def onward_pair(to):
            return remote(
                states.at[RING - 1], pair_in.at[tip], wave_send.at[to], wave_recv.at[3 + tip], me + RING, to
            )

        def onward_columns(to):
            return remote(columns_out, columns_in.at[tip], wave_send.at[to], wave_recv.at[5 + tip], me + RING, to)

        @pl.when(direct)
        def _():
            remote(few_in, few_in, wave_send.at[0], wave_recv.at[2], me, other).wait_recv()
            state = few_in[...]
            for step in range(RING):
                state = next_state(step, state)

            @pl.when(row < PRODUCT_ROW - 1)
            def _():
                onward_rows(0).start()

            @pl.when(jnp.logical_and(row == PRODUCT_ROW - 1, jnp.logical_not(final_row)))
            def _():
                for to in range(2):
                    onward_pair(to).start()

            for step in range(RING):
                send_home(step)

        @pl.when(jnp.logical_not(direct))
        def _():
            @pl.when(jnp.logical_not(final_row))
            def _():
                four_maps(maps, tip, high, low)
                state = jnp.concatenate([tips_both[0, 0], tips_both[0, 1]], 1)
                for step in (1, 2):
                    fresh = times_map(state, maps[step, 0], maps[step, 1])
                    state = jnp.concatenate([fresh[h] + tips_both[step, h] for h in range(2)], 1)
                parts = split_rows(state)
                fresh = jnp.dot(parts, maps[3, tip], preferred_element_type=jnp.float32)
                local[...] = fresh[: 2 * few] + fresh[2 * few :] + tips_both[3, tip]

            @pl.when(row == PRODUCT_ROW)
            def _():
                for core in range(2):
                    remote(
                        pair_in.at[core], pair_in.at[core], wave_send.at[0], wave_recv.at[3 + core], me, other
                    ).wait_recv()
                for core in range(2):
                    for h in range(2):
                        columns_in[h, core * few : (core + 1) * few, :] = pair_in[core, :, h * half : (h + 1) * half]

            def columns_arrive(core):
                remote(
                    columns_in.at[core], columns_in.at[core], wave_send.at[0], wave_recv.at[5 + core], me, other
                ).wait_recv()

            @pl.when(final_row)
            def _():
                for core in range(2):
                    columns_arrive(core)

            @pl.when(jnp.logical_not(final_row))
            def _():
                @pl.when(row > PRODUCT_ROW)
                def _():
                    for core in range(2):
                        columns_arrive(core)

                parts = split_rows(jnp.concatenate([columns_in[0], columns_in[1]], 1))
                fresh = jnp.dot(parts, high[0], preferred_element_type=jnp.float32)
                fresh = fresh + jnp.dot(parts, low[0], preferred_element_type=jnp.float32)
                columns_out[...] = fresh[: 2 * few] + fresh[2 * few :] + local[...]
                for to in range(2):
                    onward_columns(to).start()

            for h in range(2):
                few_in[:, h * half : (h + 1) * half] = own_of(columns_in[h])
            send_home(0)
            state = few_in[...]
            for step in range(RING - 1):
                state = next_state(step, state)
                send_home(step + 1)

        for piece in range(2 * RING):
            @pl.when(piece != mine)
            def _():
                remote(
                    prior.at[piece], prior.at[piece], home_send.at[0, 0], home_recv.at[piece], me, other
                ).wait_recv()
        for piece in range(2 * RING):
            full[piece * few : (piece + 1) * few, :] = prior[piece]

        @pl.when(alone)
        def _():
            whole.drain()

        @pl.when(helper)
        def _():
            for k in range(2):
                for step in range(1, RING):
                    from_relay(step, k).wait_send()

        @pl.when(helped)
        def _():
            rest.drain()
            for k in range(2):
                to_relay(k).wait_send()
                for step in range(1, RING):
                    relayed_to_sibling(step, k).wait_send()

        for part in range(2):
            own_sibling_map(part).wait_send()
        for number, (step, to) in enumerate(partners):
            tip_copy(step, to, number).wait_send()

        @pl.when(row < PRODUCT_ROW - 1)
        def _():
            onward_rows(0).wait_send()

        @pl.when(jnp.logical_and(row == PRODUCT_ROW - 1, jnp.logical_not(final_row)))
        def _():
            for to in range(2):
                onward_pair(to).wait_send()

        @pl.when(jnp.logical_and(row >= PRODUCT_ROW, jnp.logical_not(final_row)))
        def _():
            for to in range(2):
                onward_columns(to).wait_send()

        for step in range(RING):
            for to in range(2):
                @pl.when(jnp.logical_or(x != step, tip != to))
                def _():
                    home_copy(step, to).wait_send()

    own_spikes.wait()
    spikes_out.wait()
    count = full.shape[0]
    parts = split_rows(full[...])
    fresh = jnp.dot(parts, maps[x, tip], preferred_element_type=jnp.float32)
    interface_ref[0] = fresh[:count] + fresh[count:]
    middle = spikes.shape[1]
    product = jnp.dot(parts[:count, :middle], spikes[0], preferred_element_type=jnp.float32)
    product_ref[0] = product + jnp.dot(parts[:count, middle:], spikes[1], preferred_element_type=jnp.float32)


def on_device(band_maps, right_tips, spikes, local_parts):
    rows_total = lax.axis_size("dom") // RING
    _, depth, half = band_maps.shape
    count = right_tips.shape[1]
    many = count // 2
    few = many // RING
    _, spike_rows, spike_columns = spikes.shape
    width = spike_columns // 2
    f32, b16, dma = jnp.float32, jnp.bfloat16, pltpu.SemaphoreType.DMA
    interface, product = pl.pallas_call(
        functools.partial(sweep, rows_total),
        out_shape=(
            jax.ShapeDtypeStruct((1, count, half), f32),
            jax.ShapeDtypeStruct((1, count, width), f32),
        ),
        in_specs=[
            pl.BlockSpec(memory_space=pltpu.HBM),
            pl.BlockSpec(memory_space=pltpu.HBM),
            pl.BlockSpec(memory_space=pltpu.HBM),
        ],
        out_specs=(pl.BlockSpec(memory_space=pltpu.VMEM),) * 2,
        scratch_shapes=[
            pltpu.VMEM((RING, 2, depth, half), b16),
            pltpu.VMEM((count, half), f32),
            pltpu.VMEM((RING, 2 * few, half), f32),
            pltpu.VMEM((RING, 2, 2 * few, half), f32),
            pltpu.VMEM((RING, 2, few, half), f32),
            pltpu.VMEM((2, many, half), f32),
            pltpu.VMEM((few, depth), f32),
            pltpu.VMEM((2, few, depth), f32),
            pltpu.VMEM((2, 2 * few, half), f32),
            pltpu.VMEM((2 * few, half), f32),
            pltpu.VMEM((2 * few, half), f32),
            pltpu.VMEM((2, depth, half), b16),
            pltpu.VMEM((2, depth, half), b16),
            pltpu.VMEM((2, many, half), f32),
            pltpu.VMEM((2, many, half), f32),
            pltpu.VMEM((RING, few, depth), f32),
            pltpu.VMEM((2 * RING, few, depth), f32),
            pltpu.VMEM((2, many, half), f32),
            pltpu.VMEM((count, depth), f32),
            pltpu.VMEM((2, spike_rows, width), b16),
            dma((3,)),
            dma((RING, 2)),
            dma((RING, 2)),
            dma((2, 2)),
            dma((2, 2)),
            pltpu.VMEM((2, depth // 8, half), b16),
            dma((RING, 2)),
            dma((RING, 2)),
            dma((RING, 2)),
            dma((RING, 2)),
            dma((2, 2)),
            dma((2, 2)),
            dma((2, 2)),
            dma((2, 2)),
            dma((2 * RING - 1,)),
            dma((RING, 2)),
            dma((2,)),
            dma((7,)),
            dma((RING, 2)),
            dma((2 * RING,)),
            dma((2,)),
            dma((2,)),
        ],
        compiler_params=pltpu.CompilerParams(
            collective_id=0, has_side_effects=True, vmem_limit_bytes=53 << 20
        ),
    )(band_maps, right_tips, spikes)
    return right_tips + interface, local_parts - product


def solution(mesh):
    return jax.shard_map(
        on_device,
        mesh=mesh,
        in_specs=(
            P("dom", None, "tip"),
            P("dom", None, "tip"),
            P("dom", "tip", None),
            P("dom", None, "tip"),
        ),
        out_specs=(P("dom", None, "tip"), P("dom", None, "tip")),
        check_vma=False,
    )
```

```python
import functools

import jax
import jax.numpy as jnp
from jax import lax
from jax.experimental import pallas as pl
from jax.experimental.pallas import tpu as pltpu
from jax.sharding import PartitionSpec as P

MESH = pl.DeviceIdType.MESH
RING = 4
CHAIN_ROWS = 2
HELPED_ROWS = 4
PRODUCT_ROW = 4


def split_rows(value):
    high = value.astype(jnp.bfloat16)
    low = value - high.astype(jnp.float32)
    return jnp.concatenate([high.astype(jnp.float32), low], 0).astype(jnp.bfloat16)


def times_map(value, left, right):
    rows = value.shape[0]
    parts = split_rows(value)
    out = [jnp.dot(parts, half, preferred_element_type=jnp.float32) for half in (left, right)]
    return [piece[:rows] + piece[rows:] for piece in out]


def four_maps(maps, tip, high, low):
    half = maps.shape[3]
    block = min(256, half)
    for turn, step in enumerate((2, 1, 0)):
        factor = jnp.concatenate([maps[step, 0], maps[step, 1]], 1)
        for start in range(0, half, block):
            columns = slice(start, start + block)
            if turn == 0:
                total = jnp.dot(factor, maps[3, tip, :, columns], preferred_element_type=jnp.float32)
            else:
                total = jnp.dot(factor, high[(turn - 1) % 2, :, columns], preferred_element_type=jnp.float32)
                total += jnp.dot(factor, low[(turn - 1) % 2, :, columns], preferred_element_type=jnp.float32)
            top = total.astype(jnp.bfloat16)
            high[turn % 2, :, columns] = top
            low[turn % 2, :, columns] = (total - top.astype(jnp.float32)).astype(jnp.bfloat16)


def sweep(
    rows_total, maps_hbm, tips_hbm, spikes_hbm, interface_ref, product_ref,
    maps, tips_ref, tips_out, tips_both, tips_few, tips_many, few_in, pair_in, columns_in, columns_out, local,
    high, low, many_in, many_out, states, prior, prior_many, full, spikes,
    local_sem, sib_send, sib_recv, quarter_send, quarter_recv, relay, relay_send, relay_recv, relay_sib_send, relay_sib_recv,
    link_send, link_recv, fwd_send, opp_recv,
    tip_send, tip_recv, wave_send, wave_recv, home_send, home_recv, side_send, side_recv,
):
    me, tip = lax.axis_index("dom"), lax.axis_index("tip")
    x, row = lax.rem(me, RING), lax.div(me, RING)
    other = 1 - tip
    base = me - x
    depth = maps_hbm.shape[1]
    half = maps_hbm.shape[2]
    cut = depth // 2
    width = spikes_hbm.shape[2] // 2
    chained = row < CHAIN_ROWS
    ringed = row >= CHAIN_ROWS
    helped = jnp.logical_and(ringed, row < CHAIN_ROWS + HELPED_ROWS)
    alone = row >= CHAIN_ROWS + HELPED_ROWS
    helping = rows_total - 4
    served = CHAIN_ROWS + lax.rem(row - helping + 4 * rows_total - CHAIN_ROWS, 4)
    helper = jnp.logical_and(row >= helping, served < CHAIN_ROWS + HELPED_ROWS)
    mirrored = jnp.where(helped, helping + lax.rem(row, 4), served) * RING
    relayed = maps_hbm.shape[1] // 4
    last_chain = CHAIN_ROWS * RING - 1
    right, left = base + lax.rem(x + 1, RING), base + lax.rem(x + 3, RING)
    opposite = base + lax.rem(x + 2, RING)
    many = full.shape[0] // 2
    few = many // RING

    def remote(src, dst, send, recv, dom, to):
        return pltpu.make_async_remote_copy(
            src_ref=src, dst_ref=dst, send_sem=send, recv_sem=recv, device_id=(dom, to), device_id_type=MESH
        )

    barrier = pltpu.get_barrier_semaphore()

    def greet(dom, to):
        pl.semaphore_signal(barrier, inc=1, device_id=(dom, to), device_id_type=MESH)

    greet(me, other)

    @pl.when(chained)
    def _():
        @pl.when(me > 0)
        def _():
            greet(me - 1, tip)

        @pl.when(me == 1)
        def _():
            greet(0, other)

    @pl.when(ringed)
    def _():
        for step in range(1, RING):
            for to in range(2):
                greet(base + lax.rem(x + step, RING), to)
        before = jnp.where(row == CHAIN_ROWS, last_chain, me - RING)
        greet(before, tip)

        @pl.when(row >= PRODUCT_ROW)
        def _():
            greet(before, other)

        @pl.when(helper)
        def _():
            greet(mirrored + x, tip)

    own_map = pltpu.make_async_copy(maps_hbm.at[0], maps.at[x, tip], local_sem.at[0])
    own_map.start()
    own_columns = pl.ds(pl.multiple_of(tip * width, width), width)
    other_columns = pl.ds(pl.multiple_of(other * width, width), width)
    own_spikes = pltpu.make_async_copy(spikes_hbm.at[0, :, own_columns], spikes.at[tip], local_sem.at[1])
    own_spikes.start()
    own_tips = pltpu.make_async_copy(tips_hbm.at[0], tips_ref, local_sem.at[2])
    own_tips.start()
    @pl.when(chained)
    def _():
        pl.semaphore_wait(barrier, jnp.where(me == last_chain, 1 + RING, jnp.where(me == 0, 3, 2)))

    @pl.when(ringed)
    def _():
        after = jnp.where(row == rows_total - 1, 0, jnp.where(row >= PRODUCT_ROW - 1, 2, 1))
        pl.semaphore_wait(barrier, 2 * RING - 1 + after + jnp.where(helped, 1, 0))

    pieces = [slice(0, cut), slice(cut, depth)]

    def sibling_map_arrives(step, part):
        slot = lax.rem(x + step, RING)
        block = maps.at[slot, other, pieces[part]]
        remote(block, block, sib_send.at[step, part], sib_recv.at[step, part], me, other).wait_recv()

    def own_sibling_map(part):
        src = maps_hbm.at[0, pieces[part]]
        return remote(src, maps.at[x, tip, pieces[part]], sib_send.at[0, part], sib_recv.at[0, part], me, other)

    spikes_out = remote(
        spikes_hbm.at[0, :, other_columns], spikes.at[tip], side_send.at[0], side_recv.at[0], me, other
    )

    def first_rows(to):
        rows = slice(to * many, (to + 1) * many)
        return remote(tips_hbm.at[0, rows, :], many_in.at[tip], wave_send.at[to], wave_recv.at[tip], 1, to)

    def relay_rows(k):
        start = depth - relayed + k * (relayed // 2)
        return slice(start, start + relayed // 2)

    def to_relay(k):
        src = maps_hbm.at[0, relay_rows(k)]
        return remote(src, relay.at[k], relay_send.at[0, k], relay_recv.at[0, k], mirrored + x, tip)

    def from_relay(step, k):
        dst = maps.at[x, tip, relay_rows(k)]
        dom = mirrored + lax.rem(x + step, RING)
        return remote(relay.at[k], dst, relay_send.at[step, k], relay_recv.at[step, k], dom, tip)

    def pass_on():
        for k in range(2):
            remote(relay.at[k], relay.at[k], relay_send.at[0, k], relay_recv.at[0, k], me, other).wait_recv()
            for step in range(1, RING):
                from_relay(step, k).start()

    @pl.when(chained)
    def _():
        @pl.when(me == 0)
        def _():
            for to in range(2):
                first_rows(to).start()

        own_tips.wait()
        for part in range(2):
            own_sibling_map(part).start()
        tip_rows = pl.ds(pl.multiple_of(other * many, many), many)
        tips_copy = remote(
            tips_ref.at[tip_rows, :], tips_many.at[tip], tip_send.at[0], tip_recv.at[0, 1], me, other
        )
        tips_copy.start()
        spikes_out.start()
        own_map.wait()
        for part in range(2):
            sibling_map_arrives(0, part)
        tips_copy.wait_recv()

        def many_send(h, dom):
            return remote(many_out.at[h], many_in.at[h], wave_send.at[h], wave_recv.at[h], dom, tip)

        own_rows = pl.ds(pl.multiple_of(tip * many, many), many)
        tips_many[tip] = tips_ref[own_rows, :]

        @pl.when(me == 0)
        def _():
            many_in[...] = jnp.zeros_like(many_in)

        total = [None, None]
        for k in range(2):
            @pl.when(me > 0)
            def _():
                remote(many_in.at[k], many_in.at[k], wave_send.at[k], wave_recv.at[k], me, other).wait_recv()

            parts = split_rows(many_in[k])
            for h in range(2):
                term = jnp.dot(parts, maps[x, h, k * half : (k + 1) * half, :], preferred_element_type=jnp.float32)
                total[h] = term if k == 0 else total[h] + term
                if k == 1:
                    fresh = total[h][:many] + total[h][many:] + tips_many[h]
                    many_out[h] = fresh

                    @pl.when(jnp.logical_and(me > 0, me < last_chain))
                    def _():
                        many_send(h, me + 1).start()

        @pl.when(me == last_chain)
        def _():
            for piece in range(RING):
                for h in range(2):
                    states[piece, :, h * half : (h + 1) * half] = many_out[h, piece * few : (piece + 1) * few, :]
            for piece in range(RING):
                remote(
                    states.at[piece], few_in, home_send.at[piece, 0], wave_recv.at[2], last_chain + 1 + piece, tip
                ).start()

        to_sibling = remote(many_in, prior_many, side_send.at[1], side_recv.at[1], me, other)
        to_sibling.start()
        for h in range(2):
            full[own_rows, h * half : (h + 1) * half] = many_in[h]
        to_sibling.wait_recv()
        for h in range(2):
            full[tip_rows, h * half : (h + 1) * half] = prior_many[h]

        to_sibling.wait_send()
        tips_copy.wait_send()
        for part in range(2):
            own_sibling_map(part).wait_send()

        @pl.when(me == 0)
        def _():
            for to in range(2):
                first_rows(to).wait_send()

        @pl.when(jnp.logical_and(me > 0, me < last_chain))
        def _():
            for h in range(2):
                many_send(h, me + 1).wait_send()

        @pl.when(me == last_chain)
        def _():
            for piece in range(RING):
                remote(
                    states.at[piece], few_in, home_send.at[piece, 0], wave_recv.at[2], last_chain + 1 + piece, tip
                ).wait_send()

    @pl.when(ringed)
    def _():
        class Gather:
            def __init__(self, count):
                self.cut = count // 2

            def rows(self, part, k=None):
                if k is None:
                    return slice(part * self.cut, (part + 1) * self.cut)
                size = self.cut // 2
                return slice(part * self.cut + k * size, part * self.cut + (k + 1) * size)

            def own(self, part, side):
                rows = self.rows(part)
                return remote(
                    maps_hbm.at[0, rows], maps.at[x, tip, rows],
                    link_send.at[side, part], link_recv.at[side, part], right if side == 0 else left, tip,
                )

            def neighbour_arrives(self, part, side):
                block = maps.at[lax.rem(x + (3 if side == 0 else 1), RING), tip, self.rows(part)]
                remote(block, block, link_send.at[side, part], link_recv.at[side, part], right, tip).wait_recv()

            def forward(self, side, k):
                block = maps.at[lax.rem(x + (3 if side == 0 else 1), RING), tip, self.rows(side, k)]
                dom = right if side == 0 else left
                return remote(block, block, fwd_send.at[side, k], opp_recv.at[side, k], dom, tip)

            def opposite_arrives(self, side, k):
                block = maps.at[lax.rem(x + 2, RING), tip, self.rows(side, k)]
                remote(block, block, fwd_send.at[side, k], opp_recv.at[side, k], right, tip).wait_recv()

            def to_sibling(self, step, part):
                block = maps.at[lax.rem(x + step, RING), tip, self.rows(part)]
                return remote(block, block, sib_send.at[step, part], sib_recv.at[step, part], me, other)

            def sibling_arrives(self, step, part):
                block = maps.at[lax.rem(x + step, RING), other, self.rows(part)]
                remote(block, block, sib_send.at[step, part], sib_recv.at[step, part], me, other).wait_recv()

            def quarter_to_sibling(self, side, k):
                block = maps.at[lax.rem(x + 2, RING), tip, self.rows(side, k)]
                return remote(block, block, quarter_send.at[side, k], quarter_recv.at[side, k], me, other)

            def sibling_quarter_arrives(self, side, k):
                block = maps.at[lax.rem(x + 2, RING), other, self.rows(side, k)]
                remote(block, block, quarter_send.at[side, k], quarter_recv.at[side, k], me, other).wait_recv()

            def start(self):
                for part, side in ((0, 0), (1, 1), (1, 0), (0, 1)):
                    self.own(part, side).start()

            def middle(self):
                for part, side in ((0, 0), (1, 1)):
                    self.neighbour_arrives(part, side)
                    for k in range(2):
                        self.forward(side, k).start()
                    self.to_sibling(3 if side == 0 else 1, part).start()
                for part, side in ((1, 0), (0, 1)):
                    self.neighbour_arrives(part, side)
                    self.to_sibling(3 if side == 0 else 1, part).start()

            def last(self):
                for k in range(2):
                    for side in range(2):
                        self.opposite_arrives(side, k)
                        self.quarter_to_sibling(side, k).start()
                for step in (1, 3):
                    for part in range(2):
                        self.sibling_arrives(step, part)
                for k in range(2):
                    for side in range(2):
                        self.sibling_quarter_arrives(side, k)

            def drain(self):
                for part in range(2):
                    for side in range(2):
                        self.own(part, side).wait_send()
                    for k in range(2):
                        self.forward(part, k).wait_send()
                        self.quarter_to_sibling(part, k).wait_send()
                    for step in (1, 3):
                        self.to_sibling(step, part).wait_send()

        whole, rest = Gather(depth), Gather(depth - relayed)

        def relayed_to_sibling(step, k):
            block = maps.at[lax.rem(x + RING - step, RING), tip, relay_rows(k)]
            return remote(block, block, relay_sib_send.at[step, k], relay_sib_recv.at[step, k], me, other)

        @pl.when(helped)
        def _():
            for k in range(2):
                to_relay(k).start()
            rest.start()

        @pl.when(jnp.logical_and(alone, jnp.logical_not(helper)))
        def _():
            whole.start()

        own_tips.wait()
        for piece in range(RING):
            for to in range(2):
                start = to * many + piece * few
                tips_out[piece, to * few : (to + 1) * few, :] = tips_ref[start : start + few, :]

        def tip_copy(step, to, number):
            dst_x = lax.rem(x + step, RING)
            return remote(
                tips_out.at[dst_x], tips_both.at[x, tip],
                tip_send.at[number], tip_recv.at[step, jnp.where(to == tip, 0, 1)], base + dst_x, to,
            )

        partners = [(0, other), (1, tip), (1, other), (2, tip), (2, other), (3, tip), (3, other)]
        for number, (step, to) in enumerate(partners):
            tip_copy(step, to, number).start()
        tips_both[x, tip] = tips_out[x]
        for part in range(2):
            own_sibling_map(part).start()
        spikes_out.start()

        @pl.when(helper)
        def _():
            pass_on()

        @pl.when(jnp.logical_and(alone, helper))
        def _():
            whole.start()

        @pl.when(alone)
        def _():
            whole.middle()
            whole.last()

        @pl.when(helped)
        def _():
            rest.middle()
            for k in range(2):
                for step in range(1, RING):
                    block = maps.at[lax.rem(x + RING - step, RING), tip, relay_rows(k)]
                    remote(block, block, relay_send.at[step, k], relay_recv.at[step, k], me, other).wait_recv()
                    relayed_to_sibling(step, k).start()
            rest.last()
            for k in range(2):
                for step in range(1, RING):
                    block = maps.at[lax.rem(x + RING - step, RING), other, relay_rows(k)]
                    remote(block, block, relay_sib_send.at[step, k], relay_sib_recv.at[step, k], me, other).wait_recv()

        own_map.wait()
        for part in range(2):
            sibling_map_arrives(0, part)
        for step, to in partners:
            remote(
                tips_both.at[0, 0], tips_both.at[0, 0], tip_send.at[0],
                tip_recv.at[step, jnp.where(to == tip, 0, 1)], me, other,
            ).wait_recv()

        mine = tip * RING + x

        def home_copy(step, to):
            src = few_in if step == 0 else states.at[step - 1]
            return remote(src, prior.at[mine], home_send.at[step, to], home_recv.at[mine], base + step, to)

        def send_home(step):
            for to in range(2):
                @pl.when(jnp.logical_or(x != step, tip != to))
                def _():
                    home_copy(step, to).start()

            @pl.when(x == step)
            def _():
                prior[mine] = few_in[...] if step == 0 else states[step - 1]

        def next_state(step, state):
            fresh = times_map(state, maps[step, 0], maps[step, 1])
            for h in range(2):
                states[step, :, h * half : (h + 1) * half] = fresh[h] + tips_few[step, h]
            return states[step]

        def own_of(pair):
            return jnp.where(tip == 0, pair[:few], pair[few:])

        for step in range(RING):
            for h in range(2):
                tips_few[step, h] = own_of(tips_both[step, h])

        final_row = row == rows_total - 1
        direct = row < PRODUCT_ROW

        def onward_rows(to):
            return remote(states.at[RING - 1], few_in, wave_send.at[to], wave_recv.at[2], me + RING, tip)

        def onward_pair(to):
            return remote(
                states.at[RING - 1], pair_in.at[tip], wave_send.at[to], wave_recv.at[3 + tip], me + RING, to
            )

        def onward_columns(to):
            return remote(columns_out, columns_in.at[tip], wave_send.at[to], wave_recv.at[5 + tip], me + RING, to)

        @pl.when(direct)
        def _():
            remote(few_in, few_in, wave_send.at[0], wave_recv.at[2], me, other).wait_recv()
            state = few_in[...]
            for step in range(RING):
                state = next_state(step, state)

            @pl.when(row < PRODUCT_ROW - 1)
            def _():
                onward_rows(0).start()

            @pl.when(jnp.logical_and(row == PRODUCT_ROW - 1, jnp.logical_not(final_row)))
            def _():
                for to in range(2):
                    onward_pair(to).start()

            for step in range(RING):
                send_home(step)

        @pl.when(jnp.logical_not(direct))
        def _():
            @pl.when(jnp.logical_not(final_row))
            def _():
                four_maps(maps, tip, high, low)
                state = jnp.concatenate([tips_both[0, 0], tips_both[0, 1]], 1)
                for step in (1, 2):
                    fresh = times_map(state, maps[step, 0], maps[step, 1])
                    state = jnp.concatenate([fresh[h] + tips_both[step, h] for h in range(2)], 1)
                parts = split_rows(state)
                fresh = jnp.dot(parts, maps[3, tip], preferred_element_type=jnp.float32)
                local[...] = fresh[: 2 * few] + fresh[2 * few :] + tips_both[3, tip]

            @pl.when(row == PRODUCT_ROW)
            def _():
                for core in range(2):
                    remote(
                        pair_in.at[core], pair_in.at[core], wave_send.at[0], wave_recv.at[3 + core], me, other
                    ).wait_recv()
                for core in range(2):
                    for h in range(2):
                        columns_in[h, core * few : (core + 1) * few, :] = pair_in[core, :, h * half : (h + 1) * half]

            def columns_arrive(core):
                remote(
                    columns_in.at[core], columns_in.at[core], wave_send.at[0], wave_recv.at[5 + core], me, other
                ).wait_recv()

            @pl.when(final_row)
            def _():
                for core in range(2):
                    columns_arrive(core)

            @pl.when(jnp.logical_not(final_row))
            def _():
                @pl.when(row > PRODUCT_ROW)
                def _():
                    for core in range(2):
                        columns_arrive(core)

                parts = split_rows(jnp.concatenate([columns_in[0], columns_in[1]], 1))
                fresh = jnp.dot(parts, high[0], preferred_element_type=jnp.float32)
                fresh = fresh + jnp.dot(parts, low[0], preferred_element_type=jnp.float32)
                columns_out[...] = fresh[: 2 * few] + fresh[2 * few :] + local[...]
                for to in range(2):
                    onward_columns(to).start()

            for h in range(2):
                few_in[:, h * half : (h + 1) * half] = own_of(columns_in[h])
            send_home(0)
            state = few_in[...]
            for step in range(RING - 1):
                state = next_state(step, state)
                send_home(step + 1)

        for piece in range(2 * RING):
            @pl.when(piece != mine)
            def _():
                remote(
                    prior.at[piece], prior.at[piece], home_send.at[0, 0], home_recv.at[piece], me, other
                ).wait_recv()
        for piece in range(2 * RING):
            full[piece * few : (piece + 1) * few, :] = prior[piece]

        @pl.when(alone)
        def _():
            whole.drain()

        @pl.when(helper)
        def _():
            for k in range(2):
                for step in range(1, RING):
                    from_relay(step, k).wait_send()

        @pl.when(helped)
        def _():
            rest.drain()
            for k in range(2):
                to_relay(k).wait_send()
                for step in range(1, RING):
                    relayed_to_sibling(step, k).wait_send()

        for part in range(2):
            own_sibling_map(part).wait_send()
        for number, (step, to) in enumerate(partners):
            tip_copy(step, to, number).wait_send()

        @pl.when(row < PRODUCT_ROW - 1)
        def _():
            onward_rows(0).wait_send()

        @pl.when(jnp.logical_and(row == PRODUCT_ROW - 1, jnp.logical_not(final_row)))
        def _():
            for to in range(2):
                onward_pair(to).wait_send()

        @pl.when(jnp.logical_and(row >= PRODUCT_ROW, jnp.logical_not(final_row)))
        def _():
            for to in range(2):
                onward_columns(to).wait_send()

        for step in range(RING):
            for to in range(2):
                @pl.when(jnp.logical_or(x != step, tip != to))
                def _():
                    home_copy(step, to).wait_send()

    own_spikes.wait()
    spikes_out.wait()
    count = full.shape[0]
    parts = split_rows(full[...])
    fresh = jnp.dot(parts, maps[x, tip], preferred_element_type=jnp.float32)
    interface_ref[0] = fresh[:count] + fresh[count:]
    middle = spikes.shape[1]
    product = jnp.dot(parts[:count, :middle], spikes[0], preferred_element_type=jnp.float32)
    product_ref[0] = product + jnp.dot(parts[:count, middle:], spikes[1], preferred_element_type=jnp.float32)


def on_device(band_maps, right_tips, spikes, local_parts):
    rows_total = lax.axis_size("dom") // RING
    _, depth, half = band_maps.shape
    count = right_tips.shape[1]
    many = count // 2
    few = many // RING
    _, spike_rows, spike_columns = spikes.shape
    width = spike_columns // 2
    f32, b16, dma = jnp.float32, jnp.bfloat16, pltpu.SemaphoreType.DMA
    interface, product = pl.pallas_call(
        functools.partial(sweep, rows_total),
        out_shape=(
            jax.ShapeDtypeStruct((1, count, half), f32),
            jax.ShapeDtypeStruct((1, count, width), f32),
        ),
        in_specs=[
            pl.BlockSpec(memory_space=pltpu.HBM),
            pl.BlockSpec(memory_space=pltpu.HBM),
            pl.BlockSpec(memory_space=pltpu.HBM),
        ],
        out_specs=(pl.BlockSpec(memory_space=pltpu.VMEM),) * 2,
        scratch_shapes=[
            pltpu.VMEM((RING, 2, depth, half), b16),
            pltpu.VMEM((count, half), f32),
            pltpu.VMEM((RING, 2 * few, half), f32),
            pltpu.VMEM((RING, 2, 2 * few, half), f32),
            pltpu.VMEM((RING, 2, few, half), f32),
            pltpu.VMEM((2, many, half), f32),
            pltpu.VMEM((few, depth), f32),
            pltpu.VMEM((2, few, depth), f32),
            pltpu.VMEM((2, 2 * few, half), f32),
            pltpu.VMEM((2 * few, half), f32),
            pltpu.VMEM((2 * few, half), f32),
            pltpu.VMEM((2, depth, half), b16),
            pltpu.VMEM((2, depth, half), b16),
            pltpu.VMEM((2, many, half), f32),
            pltpu.VMEM((2, many, half), f32),
            pltpu.VMEM((RING, few, depth), f32),
            pltpu.VMEM((2 * RING, few, depth), f32),
            pltpu.VMEM((2, many, half), f32),
            pltpu.VMEM((count, depth), f32),
            pltpu.VMEM((2, spike_rows, width), b16),
            dma((3,)),
            dma((RING, 2)),
            dma((RING, 2)),
            dma((2, 2)),
            dma((2, 2)),
            pltpu.VMEM((2, depth // 8, half), b16),
            dma((RING, 2)),
            dma((RING, 2)),
            dma((RING, 2)),
            dma((RING, 2)),
            dma((2, 2)),
            dma((2, 2)),
            dma((2, 2)),
            dma((2, 2)),
            dma((2 * RING - 1,)),
            dma((RING, 2)),
            dma((2,)),
            dma((7,)),
            dma((RING, 2)),
            dma((2 * RING,)),
            dma((2,)),
            dma((2,)),
        ],
        compiler_params=pltpu.CompilerParams(
            collective_id=0, has_side_effects=True, vmem_limit_bytes=53 << 20
        ),
    )(band_maps, right_tips, spikes)
    return right_tips + interface, local_parts - product


def solution(mesh):
    return jax.shard_map(
        on_device,
        mesh=mesh,
        in_specs=(
            P("dom", None, "tip"),
            P("dom", None, "tip"),
            P("dom", "tip", None),
            P("dom", None, "tip"),
        ),
        out_specs=(P("dom", None, "tip"), P("dom", None, "tip")),
        check_vma=False,
    )
```

```python
import functools

import jax
import jax.numpy as jnp
from jax import lax
from jax.experimental import pallas as pl
from jax.experimental.pallas import tpu as pltpu
from jax.sharding import PartitionSpec as P

MESH = pl.DeviceIdType.MESH
RING = 4
CHAIN_ROWS = 2
HELPED_ROWS = 4
PRODUCT_ROW = 4


def split_rows(value):
    high = value.astype(jnp.bfloat16)
    low = value - high.astype(jnp.float32)
    return jnp.concatenate([high.astype(jnp.float32), low], 0).astype(jnp.bfloat16)


def times_map(value, left, right):
    rows = value.shape[0]
    parts = split_rows(value)
    out = [jnp.dot(parts, half, preferred_element_type=jnp.float32) for half in (left, right)]
    return [piece[:rows] + piece[rows:] for piece in out]


def leading_maps(last, maps, tip, high, low):
    half = maps.shape[3]
    block = min(256, half)
    for turn, step in enumerate(range(last - 1, -1, -1)):
        factor = jnp.concatenate([maps[step, 0], maps[step, 1]], 1)
        for start in range(0, half, block):
            columns = slice(start, start + block)
            if turn == 0:
                total = jnp.dot(factor, maps[last, tip, :, columns], preferred_element_type=jnp.float32)
            else:
                total = jnp.dot(factor, high[(turn - 1) % 2, :, columns], preferred_element_type=jnp.float32)
                total += jnp.dot(factor, low[(turn - 1) % 2, :, columns], preferred_element_type=jnp.float32)
            top = total.astype(jnp.bfloat16)
            high[turn % 2, :, columns] = top
            low[turn % 2, :, columns] = (total - top.astype(jnp.float32)).astype(jnp.bfloat16)
    return (last - 1) % 2


def sweep(
    rows_total, maps_hbm, tips_hbm, spikes_hbm, interface_ref, product_ref,
    maps, tips_ref, tips_out, tips_both, tips_few, tips_many, few_in, pair_in, columns_in, columns_out, local,
    high, low, many_in, many_out, states, prior, prior_many, full, spikes,
    local_sem, sib_send, sib_recv, quarter_send, quarter_recv, relay, relay_open, relay_send, relay_recv,
    relay_sib_send, relay_sib_recv,
    link_send, link_recv, fwd_send, opp_recv,
    tip_send, tip_recv, wave_send, wave_recv, home_send, home_recv, side_send, side_recv,
    last_in, last_send, last_recv,
):
    me, tip = lax.axis_index("dom"), lax.axis_index("tip")
    x, row = lax.rem(me, RING), lax.div(me, RING)
    other = 1 - tip
    base = me - x
    depth = maps_hbm.shape[1]
    half = maps_hbm.shape[2]
    cut = depth // 2
    width = spikes_hbm.shape[2] // 2
    chained = row < CHAIN_ROWS
    ringed = row >= CHAIN_ROWS
    helped = jnp.logical_and(ringed, row < CHAIN_ROWS + HELPED_ROWS)
    alone = row >= CHAIN_ROWS + HELPED_ROWS
    helping = rows_total - 4
    served = CHAIN_ROWS + lax.rem(row - helping + 4 * rows_total - CHAIN_ROWS, 4)
    helper = jnp.logical_and(row >= helping, served < CHAIN_ROWS + HELPED_ROWS)
    mirrored = jnp.where(helped, helping + lax.rem(row, 4), served) * RING
    relayed = maps_hbm.shape[1] // 4
    last_chain = CHAIN_ROWS * RING - 1
    right, left = base + lax.rem(x + 1, RING), base + lax.rem(x + 3, RING)
    opposite = base + lax.rem(x + 2, RING)
    many = full.shape[0] // 2
    few = many // RING

    def remote(src, dst, send, recv, dom, to):
        return pltpu.make_async_remote_copy(
            src_ref=src, dst_ref=dst, send_sem=send, recv_sem=recv, device_id=(dom, to), device_id_type=MESH
        )

    barrier = pltpu.get_barrier_semaphore()

    def greet(dom, to):
        pl.semaphore_signal(barrier, inc=1, device_id=(dom, to), device_id_type=MESH)

    greet(me, other)

    @pl.when(chained)
    def _():
        @pl.when(me > 0)
        def _():
            greet(me - 1, tip)

        @pl.when(me == 1)
        def _():
            greet(0, other)

    @pl.when(ringed)
    def _():
        for step in range(1, RING):
            for to in range(2):
                greet(base + lax.rem(x + step, RING), to)
        before = jnp.where(row == CHAIN_ROWS, last_chain, me - RING)
        greet(before, tip)

        @pl.when(row >= PRODUCT_ROW)
        def _():
            greet(before, other)

        @pl.when(helped)
        def _():
            greet(mirrored + x, tip)

    own_map = pltpu.make_async_copy(maps_hbm.at[0], maps.at[x, tip], local_sem.at[0])
    own_map.start()
    own_columns = pl.ds(pl.multiple_of(tip * width, width), width)
    other_columns = pl.ds(pl.multiple_of(other * width, width), width)
    own_spikes = pltpu.make_async_copy(spikes_hbm.at[0, :, own_columns], spikes.at[tip], local_sem.at[1])
    own_spikes.start()
    own_tips = pltpu.make_async_copy(tips_hbm.at[0], tips_ref, local_sem.at[2])
    own_tips.start()
    @pl.when(chained)
    def _():
        pl.semaphore_wait(barrier, jnp.where(me == last_chain, 1 + RING, jnp.where(me == 0, 3, 2)))

    @pl.when(ringed)
    def _():
        after = jnp.where(row == rows_total - 1, 0, jnp.where(row >= PRODUCT_ROW - 1, 2, 1))
        pl.semaphore_wait(barrier, 2 * RING - 1 + after + jnp.where(helper, 1, 0))

        @pl.when(helper)
        def _():
            pl.semaphore_signal(relay_open, inc=1, device_id=(mirrored + x, tip), device_id_type=MESH)

    pieces = [slice(0, cut), slice(cut, depth)]

    def sibling_map_arrives(step, part):
        slot = lax.rem(x + step, RING)
        block = maps.at[slot, other, pieces[part]]
        remote(block, block, sib_send.at[step, part], sib_recv.at[step, part], me, other).wait_recv()

    def own_sibling_map(part):
        src = maps_hbm.at[0, pieces[part]]
        return remote(src, maps.at[x, tip, pieces[part]], sib_send.at[0, part], sib_recv.at[0, part], me, other)

    spikes_out = remote(
        spikes_hbm.at[0, :, other_columns], spikes.at[tip], side_send.at[0], side_recv.at[0], me, other
    )

    def first_rows(to):
        rows = slice(to * many, (to + 1) * many)
        return remote(tips_hbm.at[0, rows, :], many_in.at[tip], wave_send.at[to], wave_recv.at[tip], 1, to)

    def relay_rows(k):
        start = depth - relayed + k * (relayed // 2)
        return slice(start, start + relayed // 2)

    def to_relay(k):
        src = maps_hbm.at[0, relay_rows(k)]
        return remote(src, relay.at[k], relay_send.at[0, k], relay_recv.at[0, k], mirrored + x, tip)

    def from_relay(step, k):
        dst = maps.at[x, tip, relay_rows(k)]
        dom = mirrored + lax.rem(x + step, RING)
        return remote(relay.at[k], dst, relay_send.at[step, k], relay_recv.at[step, k], dom, tip)

    def pass_on():
        for k in range(2):
            remote(relay.at[k], relay.at[k], relay_send.at[0, k], relay_recv.at[0, k], me, other).wait_recv()
            for step in range(1, RING):
                from_relay(step, k).start()

    @pl.when(chained)
    def _():
        @pl.when(me == 0)
        def _():
            for to in range(2):
                first_rows(to).start()

        own_tips.wait()
        for part in range(2):
            own_sibling_map(part).start()
        tip_rows = pl.ds(pl.multiple_of(other * many, many), many)
        tips_copy = remote(
            tips_ref.at[tip_rows, :], tips_many.at[tip], tip_send.at[0], tip_recv.at[0, 1], me, other
        )
        tips_copy.start()
        spikes_out.start()
        own_map.wait()
        for part in range(2):
            sibling_map_arrives(0, part)
        tips_copy.wait_recv()

        def many_send(h, dom):
            return remote(many_out.at[h], many_in.at[h], wave_send.at[h], wave_recv.at[h], dom, tip)

        own_rows = pl.ds(pl.multiple_of(tip * many, many), many)
        tips_many[tip] = tips_ref[own_rows, :]

        @pl.when(me == 0)
        def _():
            many_in[...] = jnp.zeros_like(many_in)

        total = [None, None]
        for k in range(2):
            @pl.when(me > 0)
            def _():
                remote(many_in.at[k], many_in.at[k], wave_send.at[k], wave_recv.at[k], me, other).wait_recv()

            parts = split_rows(many_in[k])
            for h in range(2):
                term = jnp.dot(parts, maps[x, h, k * half : (k + 1) * half, :], preferred_element_type=jnp.float32)
                total[h] = term if k == 0 else total[h] + term
                if k == 1:
                    fresh = total[h][:many] + total[h][many:] + tips_many[h]
                    many_out[h] = fresh

                    @pl.when(jnp.logical_and(me > 0, me < last_chain))
                    def _():
                        many_send(h, me + 1).start()

        @pl.when(me == last_chain)
        def _():
            for piece in range(RING):
                for h in range(2):
                    states[piece, :, h * half : (h + 1) * half] = many_out[h, piece * few : (piece + 1) * few, :]
            for piece in range(RING):
                remote(
                    states.at[piece], few_in, home_send.at[piece, 0], wave_recv.at[2], last_chain + 1 + piece, tip
                ).start()

        to_sibling = remote(many_in, prior_many, side_send.at[1], side_recv.at[1], me, other)
        to_sibling.start()
        for h in range(2):
            full[own_rows, h * half : (h + 1) * half] = many_in[h]
        to_sibling.wait_recv()
        for h in range(2):
            full[tip_rows, h * half : (h + 1) * half] = prior_many[h]

        to_sibling.wait_send()
        tips_copy.wait_send()
        for part in range(2):
            own_sibling_map(part).wait_send()

        @pl.when(me == 0)
        def _():
            for to in range(2):
                first_rows(to).wait_send()

        @pl.when(jnp.logical_and(me > 0, me < last_chain))
        def _():
            for h in range(2):
                many_send(h, me + 1).wait_send()

        @pl.when(me == last_chain)
        def _():
            for piece in range(RING):
                remote(
                    states.at[piece], few_in, home_send.at[piece, 0], wave_recv.at[2], last_chain + 1 + piece, tip
                ).wait_send()

    @pl.when(ringed)
    def _():
        class Gather:
            def __init__(self, count):
                self.cut = count // 2

            def rows(self, part, k=None):
                if k is None:
                    return slice(part * self.cut, (part + 1) * self.cut)
                size = self.cut // 2
                return slice(part * self.cut + k * size, part * self.cut + (k + 1) * size)

            def own(self, part, side):
                rows = self.rows(part)
                return remote(
                    maps_hbm.at[0, rows], maps.at[x, tip, rows],
                    link_send.at[side, part], link_recv.at[side, part], right if side == 0 else left, tip,
                )

            def neighbour_arrives(self, part, side):
                block = maps.at[lax.rem(x + (3 if side == 0 else 1), RING), tip, self.rows(part)]
                remote(block, block, link_send.at[side, part], link_recv.at[side, part], right, tip).wait_recv()

            def forward(self, side, k):
                block = maps.at[lax.rem(x + (3 if side == 0 else 1), RING), tip, self.rows(side, k)]
                dom = right if side == 0 else left
                return remote(block, block, fwd_send.at[side, k], opp_recv.at[side, k], dom, tip)

            def opposite_arrives(self, side, k):
                block = maps.at[lax.rem(x + 2, RING), tip, self.rows(side, k)]
                remote(block, block, fwd_send.at[side, k], opp_recv.at[side, k], right, tip).wait_recv()

            def to_sibling(self, step, part):
                block = maps.at[lax.rem(x + step, RING), tip, self.rows(part)]
                return remote(block, block, sib_send.at[step, part], sib_recv.at[step, part], me, other)

            def sibling_arrives(self, step, part):
                block = maps.at[lax.rem(x + step, RING), other, self.rows(part)]
                remote(block, block, sib_send.at[step, part], sib_recv.at[step, part], me, other).wait_recv()

            def quarter_to_sibling(self, side, k):
                block = maps.at[lax.rem(x + 2, RING), tip, self.rows(side, k)]
                return remote(block, block, quarter_send.at[side, k], quarter_recv.at[side, k], me, other)

            def sibling_quarter_arrives(self, side, k):
                block = maps.at[lax.rem(x + 2, RING), other, self.rows(side, k)]
                remote(block, block, quarter_send.at[side, k], quarter_recv.at[side, k], me, other).wait_recv()

            def start(self):
                for part, side in ((0, 0), (1, 1), (1, 0), (0, 1)):
                    self.own(part, side).start()

            def middle(self):
                for part, side in ((0, 0), (1, 1)):
                    self.neighbour_arrives(part, side)
                    for k in range(2):
                        self.forward(side, k).start()
                    self.to_sibling(3 if side == 0 else 1, part).start()
                for part, side in ((1, 0), (0, 1)):
                    self.neighbour_arrives(part, side)
                    self.to_sibling(3 if side == 0 else 1, part).start()

            def last(self):
                for k in range(2):
                    for side in range(2):
                        self.opposite_arrives(side, k)
                        self.quarter_to_sibling(side, k).start()
                for step in (1, 3):
                    for part in range(2):
                        self.sibling_arrives(step, part)
                for k in range(2):
                    for side in range(2):
                        self.sibling_quarter_arrives(side, k)

            def drain(self):
                for part in range(2):
                    for side in range(2):
                        self.own(part, side).wait_send()
                    for k in range(2):
                        self.forward(part, k).wait_send()
                        self.quarter_to_sibling(part, k).wait_send()
                    for step in (1, 3):
                        self.to_sibling(step, part).wait_send()

        whole, rest = Gather(depth), Gather(depth - relayed)

        def relayed_to_sibling(step, k):
            block = maps.at[lax.rem(x + RING - step, RING), tip, relay_rows(k)]
            return remote(block, block, relay_sib_send.at[step, k], relay_sib_recv.at[step, k], me, other)

        @pl.when(helped)
        def _():
            rest.start()

        @pl.when(jnp.logical_and(alone, jnp.logical_not(helper)))
        def _():
            whole.start()

        own_tips.wait()
        for piece in range(RING):
            for to in range(2):
                start = to * many + piece * few
                tips_out[piece, to * few : (to + 1) * few, :] = tips_ref[start : start + few, :]

        def tip_copy(step, to, number):
            dst_x = lax.rem(x + step, RING)
            return remote(
                tips_out.at[dst_x], tips_both.at[x, tip],
                tip_send.at[number], tip_recv.at[step, jnp.where(to == tip, 0, 1)], base + dst_x, to,
            )

        partners = [(0, other), (1, tip), (1, other), (2, tip), (2, other), (3, tip), (3, other)]
        for number, (step, to) in enumerate(partners):
            tip_copy(step, to, number).start()
        tips_both[x, tip] = tips_out[x]
        for part in range(2):
            own_sibling_map(part).start()
        spikes_out.start()

        @pl.when(helped)
        def _():
            pl.semaphore_wait(relay_open, 1)
            for k in range(2):
                to_relay(k).start()

        @pl.when(helper)
        def _():
            pass_on()

        @pl.when(jnp.logical_and(alone, helper))
        def _():
            whole.start()

        @pl.when(alone)
        def _():
            whole.middle()
            whole.last()

        @pl.when(helped)
        def _():
            rest.middle()
            for k in range(2):
                for step in range(1, RING):
                    block = maps.at[lax.rem(x + RING - step, RING), tip, relay_rows(k)]
                    remote(block, block, relay_send.at[step, k], relay_recv.at[step, k], me, other).wait_recv()
                    relayed_to_sibling(step, k).start()
            rest.last()
            for k in range(2):
                for step in range(1, RING):
                    block = maps.at[lax.rem(x + RING - step, RING), other, relay_rows(k)]
                    remote(block, block, relay_sib_send.at[step, k], relay_sib_recv.at[step, k], me, other).wait_recv()

        own_map.wait()
        for part in range(2):
            sibling_map_arrives(0, part)
        for step, to in partners:
            remote(
                tips_both.at[0, 0], tips_both.at[0, 0], tip_send.at[0],
                tip_recv.at[step, jnp.where(to == tip, 0, 1)], me, other,
            ).wait_recv()

        mine = tip * RING + x

        def home_copy(step, to):
            src = few_in if step == 0 else states.at[step - 1]
            return remote(src, prior.at[mine], home_send.at[step, to], home_recv.at[mine], base + step, to)

        def send_home(step):
            for to in range(2):
                @pl.when(jnp.logical_or(x != step, tip != to))
                def _():
                    home_copy(step, to).start()

            @pl.when(x == step)
            def _():
                prior[mine] = few_in[...] if step == 0 else states[step - 1]

        def next_state(step, state):
            fresh = times_map(state, maps[step, 0], maps[step, 1])
            for h in range(2):
                states[step, :, h * half : (h + 1) * half] = fresh[h] + tips_few[step, h]
            return states[step]

        def own_of(pair):
            return jnp.where(tip == 0, pair[:few], pair[few:])

        for step in range(RING):
            for h in range(2):
                tips_few[step, h] = own_of(tips_both[step, h])

        final_row = row == rows_total - 1
        to_the_end = jnp.logical_and(final_row, x == RING - 1)

        def to_last(to):
            dom = base + RING - 1
            return remote(columns_out, last_in.at[x, tip], last_send.at[to], last_recv.at[x, tip], dom, to)
        direct = row < PRODUCT_ROW

        def onward_rows(to):
            return remote(states.at[RING - 1], few_in, wave_send.at[to], wave_recv.at[2], me + RING, tip)

        def onward_pair(to):
            return remote(
                states.at[RING - 1], pair_in.at[tip], wave_send.at[to], wave_recv.at[3 + tip], me + RING, to
            )

        def onward_columns(to):
            return remote(columns_out, columns_in.at[tip], wave_send.at[to], wave_recv.at[5 + tip], me + RING, to)

        @pl.when(direct)
        def _():
            remote(few_in, few_in, wave_send.at[0], wave_recv.at[2], me, other).wait_recv()
            state = few_in[...]
            for step in range(RING):
                state = next_state(step, state)

            @pl.when(row < PRODUCT_ROW - 1)
            def _():
                onward_rows(0).start()

            @pl.when(jnp.logical_and(row == PRODUCT_ROW - 1, jnp.logical_not(final_row)))
            def _():
                for to in range(2):
                    onward_pair(to).start()

            for step in range(RING):
                send_home(step)

        @pl.when(jnp.logical_not(direct))
        def _():
            def prepare(last):
                leading_maps(last, maps, tip, high, low)
                state = jnp.concatenate([tips_both[0, 0], tips_both[0, 1]], 1)
                for step in range(1, last):
                    fresh = times_map(state, maps[step, 0], maps[step, 1])
                    state = jnp.concatenate([fresh[h] + tips_both[step, h] for h in range(2)], 1)
                parts = split_rows(state)
                fresh = jnp.dot(parts, maps[last, tip], preferred_element_type=jnp.float32)
                local[...] = fresh[: 2 * few] + fresh[2 * few :] + tips_both[last, tip]

            def product_step(last):
                slot = (last - 1) % 2
                parts = split_rows(jnp.concatenate([columns_in[0], columns_in[1]], 1))
                fresh = jnp.dot(parts, high[slot], preferred_element_type=jnp.float32)
                fresh = fresh + jnp.dot(parts, low[slot], preferred_element_type=jnp.float32)
                columns_out[...] = fresh[: 2 * few] + fresh[2 * few :] + local[...]

            @pl.when(jnp.logical_not(final_row))
            def _():
                prepare(RING - 1)

            @pl.when(final_row)
            def _():
                prepare(RING - 2)

            @pl.when(row == PRODUCT_ROW)
            def _():
                for core in range(2):
                    remote(
                        pair_in.at[core], pair_in.at[core], wave_send.at[0], wave_recv.at[3 + core], me, other
                    ).wait_recv()
                for core in range(2):
                    for h in range(2):
                        columns_in[h, core * few : (core + 1) * few, :] = pair_in[core, :, h * half : (h + 1) * half]

            def columns_arrive(core):
                remote(
                    columns_in.at[core], columns_in.at[core], wave_send.at[0], wave_recv.at[5 + core], me, other
                ).wait_recv()

            @pl.when(row > PRODUCT_ROW)
            def _():
                for core in range(2):
                    columns_arrive(core)

            @pl.when(jnp.logical_not(final_row))
            def _():
                product_step(RING - 1)
                for to in range(2):
                    onward_columns(to).start()

            @pl.when(final_row)
            def _():
                product_step(RING - 2)
                for to in range(2):
                    @pl.when(jnp.logical_or(x != RING - 1, tip != to))
                    def _():
                        to_last(to).start()

                @pl.when(x == RING - 1)
                def _():
                    last_in[x, tip] = columns_out[...]

            for h in range(2):
                few_in[:, h * half : (h + 1) * half] = own_of(columns_in[h])
            send_home(0)
            state = few_in[...]
            for step in range(RING - 2):
                state = next_state(step, state)
                send_home(step + 1)

            @pl.when(jnp.logical_not(final_row))
            def _():
                next_state(RING - 2, state)
                send_home(RING - 1)

        @pl.when(to_the_end)
        def _():
            for chip in range(RING):
                for core in range(2):
                    @pl.when(jnp.logical_or(chip != x, core != tip))
                    def _():
                        block = last_in.at[chip, core]
                        remote(block, block, last_send.at[0], last_recv.at[chip, core], me, other).wait_recv()
            for chip in range(RING):
                for core in range(2):
                    columns = slice(core * half, (core + 1) * half)
                    for group in range(2):
                        start = group * many + chip * few
                        block = last_in[chip, core, group * few : (group + 1) * few, :]
                        full[start : start + few, columns] = block

        @pl.when(jnp.logical_not(to_the_end))
        def _():
            for piece in range(2 * RING):
                @pl.when(piece != mine)
                def _():
                    remote(
                        prior.at[piece], prior.at[piece], home_send.at[0, 0], home_recv.at[piece], me, other
                    ).wait_recv()
            for piece in range(2 * RING):
                full[piece * few : (piece + 1) * few, :] = prior[piece]

        @pl.when(alone)
        def _():
            whole.drain()

        @pl.when(helper)
        def _():
            for k in range(2):
                for step in range(1, RING):
                    from_relay(step, k).wait_send()

        @pl.when(helped)
        def _():
            rest.drain()
            for k in range(2):
                to_relay(k).wait_send()
                for step in range(1, RING):
                    relayed_to_sibling(step, k).wait_send()

        for part in range(2):
            own_sibling_map(part).wait_send()
        for number, (step, to) in enumerate(partners):
            tip_copy(step, to, number).wait_send()

        @pl.when(row < PRODUCT_ROW - 1)
        def _():
            onward_rows(0).wait_send()

        @pl.when(jnp.logical_and(row == PRODUCT_ROW - 1, jnp.logical_not(final_row)))
        def _():
            for to in range(2):
                onward_pair(to).wait_send()

        @pl.when(jnp.logical_and(row >= PRODUCT_ROW, jnp.logical_not(final_row)))
        def _():
            for to in range(2):
                onward_columns(to).wait_send()

        for step in range(RING - 1):
            for to in range(2):
                @pl.when(jnp.logical_or(x != step, tip != to))
                def _():
                    home_copy(step, to).wait_send()

        for to in range(2):
            @pl.when(jnp.logical_or(x != RING - 1, tip != to))
            def _():
                @pl.when(final_row)
                def _():
                    to_last(to).wait_send()

                @pl.when(jnp.logical_not(final_row))
                def _():
                    home_copy(RING - 1, to).wait_send()

    own_spikes.wait()
    spikes_out.wait()
    count = full.shape[0]
    parts = split_rows(full[...])
    fresh = jnp.dot(parts, maps[x, tip], preferred_element_type=jnp.float32)
    interface_ref[0] = fresh[:count] + fresh[count:]
    middle = spikes.shape[1]
    product = jnp.dot(parts[:count, :middle], spikes[0], preferred_element_type=jnp.float32)
    product_ref[0] = product + jnp.dot(parts[:count, middle:], spikes[1], preferred_element_type=jnp.float32)


def on_device(band_maps, right_tips, spikes, local_parts):
    rows_total = lax.axis_size("dom") // RING
    _, depth, half = band_maps.shape
    count = right_tips.shape[1]
    many = count // 2
    few = many // RING
    _, spike_rows, spike_columns = spikes.shape
    width = spike_columns // 2
    f32, b16, dma = jnp.float32, jnp.bfloat16, pltpu.SemaphoreType.DMA
    interface, product = pl.pallas_call(
        functools.partial(sweep, rows_total),
        out_shape=(
            jax.ShapeDtypeStruct((1, count, half), f32),
            jax.ShapeDtypeStruct((1, count, width), f32),
        ),
        in_specs=[
            pl.BlockSpec(memory_space=pltpu.HBM),
            pl.BlockSpec(memory_space=pltpu.HBM),
            pl.BlockSpec(memory_space=pltpu.HBM),
        ],
        out_specs=(pl.BlockSpec(memory_space=pltpu.VMEM),) * 2,
        scratch_shapes=[
            pltpu.VMEM((RING, 2, depth, half), b16),
            pltpu.VMEM((count, half), f32),
            pltpu.VMEM((RING, 2 * few, half), f32),
            pltpu.VMEM((RING, 2, 2 * few, half), f32),
            pltpu.VMEM((RING, 2, few, half), f32),
            pltpu.VMEM((2, many, half), f32),
            pltpu.VMEM((few, depth), f32),
            pltpu.VMEM((2, few, depth), f32),
            pltpu.VMEM((2, 2 * few, half), f32),
            pltpu.VMEM((2 * few, half), f32),
            pltpu.VMEM((2 * few, half), f32),
            pltpu.VMEM((2, depth, half), b16),
            pltpu.VMEM((2, depth, half), b16),
            pltpu.VMEM((2, many, half), f32),
            pltpu.VMEM((2, many, half), f32),
            pltpu.VMEM((RING, few, depth), f32),
            pltpu.VMEM((2 * RING, few, depth), f32),
            pltpu.VMEM((2, many, half), f32),
            pltpu.VMEM((count, depth), f32),
            pltpu.VMEM((2, spike_rows, width), b16),
            dma((3,)),
            dma((RING, 2)),
            dma((RING, 2)),
            dma((2, 2)),
            dma((2, 2)),
            pltpu.VMEM((2, depth // 8, half), b16),
            pltpu.SemaphoreType.REGULAR,
            dma((RING, 2)),
            dma((RING, 2)),
            dma((RING, 2)),
            dma((RING, 2)),
            dma((2, 2)),
            dma((2, 2)),
            dma((2, 2)),
            dma((2, 2)),
            dma((2 * RING - 1,)),
            dma((RING, 2)),
            dma((2,)),
            dma((7,)),
            dma((RING, 2)),
            dma((2 * RING,)),
            dma((2,)),
            dma((2,)),
            pltpu.VMEM((RING, 2, 2 * few, half), f32),
            dma((2,)),
            dma((RING, 2)),
        ],
        compiler_params=pltpu.CompilerParams(
            collective_id=0, has_side_effects=True, vmem_limit_bytes=53 << 20
        ),
    )(band_maps, right_tips, spikes)
    return right_tips + interface, local_parts - product


def solution(mesh):
    return jax.shard_map(
        on_device,
        mesh=mesh,
        in_specs=(
            P("dom", None, "tip"),
            P("dom", None, "tip"),
            P("dom", "tip", None),
            P("dom", None, "tip"),
        ),
        out_specs=(P("dom", None, "tip"), P("dom", None, "tip")),
        check_vma=False,
    )
```

```python
import functools

import jax
import jax.numpy as jnp
from jax import lax
from jax.experimental import pallas as pl
from jax.experimental.pallas import tpu as pltpu
from jax.sharding import PartitionSpec as P

MESH = pl.DeviceIdType.MESH
RING = 4
CHAIN_ROWS = 2
HELPERS = {
    2: ((14, 3), (1, 2)),
    3: ((15, 4),),
    4: ((13, 4),),
    5: ((12, 3),),
    6: ((10, 2),),
    7: ((11, 2),),
}
PRODUCT_ROW = 4


def split_rows(value):
    high = value.astype(jnp.bfloat16)
    low = value - high.astype(jnp.float32)
    return jnp.concatenate([high.astype(jnp.float32), low], 0).astype(jnp.bfloat16)


def times_map(value, left, right):
    rows = value.shape[0]
    parts = split_rows(value)
    out = [jnp.dot(parts, half, preferred_element_type=jnp.float32) for half in (left, right)]
    return [piece[:rows] + piece[rows:] for piece in out]


def leading_maps(last, maps, tip, high, low):
    half = maps.shape[3]
    block = min(256, half)
    for turn, step in enumerate(range(last - 1, -1, -1)):
        factor = jnp.concatenate([maps[step, 0], maps[step, 1]], 1)
        for start in range(0, half, block):
            columns = slice(start, start + block)
            if turn == 0:
                total = jnp.dot(factor, maps[last, tip, :, columns], preferred_element_type=jnp.float32)
            else:
                total = jnp.dot(factor, high[(turn - 1) % 2, :, columns], preferred_element_type=jnp.float32)
                total += jnp.dot(factor, low[(turn - 1) % 2, :, columns], preferred_element_type=jnp.float32)
            top = total.astype(jnp.bfloat16)
            high[turn % 2, :, columns] = top
            low[turn % 2, :, columns] = (total - top.astype(jnp.float32)).astype(jnp.bfloat16)
    return (last - 1) % 2


def sweep(
    rows_total, maps_hbm, tips_hbm, spikes_hbm, interface_ref, product_ref,
    maps, tips_ref, tips_out, tips_both, tips_few, tips_many, few_in, pair_in, columns_in, columns_out, local,
    high, low, many_in, many_out, states, prior, prior_many, full, spikes,
    local_sem, sib_send, sib_recv, quarter_send, quarter_recv, relay, relay_open, relay_send, relay_recv,
    relay_sib_send, relay_sib_recv,
    link_send, link_recv, fwd_send, opp_recv,
    tip_send, tip_recv, wave_send, wave_recv, home_send, home_recv, side_send, side_recv,
    last_in, last_send, last_recv,
):
    me, tip = lax.axis_index("dom"), lax.axis_index("tip")
    x, row = lax.rem(me, RING), lax.div(me, RING)
    other = 1 - tip
    base = me - x
    depth = maps_hbm.shape[1]
    half = maps_hbm.shape[2]
    cut = depth // 2
    width = spikes_hbm.shape[2] // 2
    chained = row < CHAIN_ROWS
    ringed = row >= CHAIN_ROWS
    def among(rows):
        return functools.reduce(jnp.logical_or, [row == r for r in rows])

    def first_chip(pairs):
        value = pairs[0][1]
        for this, that in pairs[1:]:
            value = jnp.where(row == this, that, value)
        return value * RING

    by_shares, by_part = {}, {}
    for r, helpers in HELPERS.items():
        by_shares.setdefault(tuple(n for _, n in helpers), []).append(r)
        first = 0
        for which, (h, n) in enumerate(helpers):
            by_part.setdefault((first, n, which, h < CHAIN_ROWS), []).append((h, r))
            first += n
    helped = []
    for shares, rows in by_shares.items():
        parts = [
            (sum(shares[:which]), shares[which], first_chip([(r, HELPERS[r][which][0]) for r in rows]))
            for which in range(len(shares))
        ]
        helped.append((among(rows), sum(shares), parts))
    helping = [
        (among([h for h, _ in pairs]), first, n, which, first_chip(pairs), in_chain)
        for (first, n, which, in_chain), pairs in by_part.items()
    ]
    all_helped = among(list(HELPERS))
    all_helping = among([h for helpers in HELPERS.values() for h, _ in helpers])
    unit = maps_hbm.shape[1] // 16
    last_chain = CHAIN_ROWS * RING - 1
    right, left = base + lax.rem(x + 1, RING), base + lax.rem(x + 3, RING)
    opposite = base + lax.rem(x + 2, RING)
    many = full.shape[0] // 2
    few = many // RING

    def remote(src, dst, send, recv, dom, to):
        return pltpu.make_async_remote_copy(
            src_ref=src, dst_ref=dst, send_sem=send, recv_sem=recv, device_id=(dom, to), device_id_type=MESH
        )

    barrier = pltpu.get_barrier_semaphore()

    def greet(dom, to):
        pl.semaphore_signal(barrier, inc=1, device_id=(dom, to), device_id_type=MESH)

    greet(me, other)

    @pl.when(chained)
    def _():
        @pl.when(me > 0)
        def _():
            greet(me - 1, tip)

        @pl.when(me == 1)
        def _():
            greet(0, other)

    @pl.when(ringed)
    def _():
        for step in range(1, RING):
            for to in range(2):
                greet(base + lax.rem(x + step, RING), to)
        before = jnp.where(row == CHAIN_ROWS, last_chain, me - RING)
        greet(before, tip)

        @pl.when(row >= PRODUCT_ROW)
        def _():
            greet(before, other)

        for those, _, parts in helped:
            @pl.when(those)
            def _():
                for _, _, chip in parts:
                    greet(chip + x, tip)

    own_map = pltpu.make_async_copy(maps_hbm.at[0], maps.at[x, tip], local_sem.at[0])
    own_map.start()
    own_columns = pl.ds(pl.multiple_of(tip * width, width), width)
    other_columns = pl.ds(pl.multiple_of(other * width, width), width)
    own_spikes = pltpu.make_async_copy(spikes_hbm.at[0, :, own_columns], spikes.at[tip], local_sem.at[1])
    own_spikes.start()
    own_tips = pltpu.make_async_copy(tips_hbm.at[0], tips_ref, local_sem.at[2])
    own_tips.start()
    asked = jnp.where(all_helping, 1, 0)

    @pl.when(chained)
    def _():
        pl.semaphore_wait(barrier, jnp.where(me == last_chain, 1 + RING, jnp.where(me == 0, 3, 2)) + asked)

    @pl.when(ringed)
    def _():
        after = jnp.where(row == rows_total - 1, 0, jnp.where(row >= PRODUCT_ROW - 1, 2, 1))
        pl.semaphore_wait(barrier, 2 * RING - 1 + after + asked)

    for those, _, _, which, chip, _ in helping:
        @pl.when(those)
        def _():
            pl.semaphore_signal(relay_open.at[which], inc=1, device_id=(chip + x, tip), device_id_type=MESH)

    pieces = [slice(0, cut), slice(cut, depth)]

    def sibling_map_arrives(step, part):
        slot = lax.rem(x + step, RING)
        block = maps.at[slot, other, pieces[part]]
        remote(block, block, sib_send.at[step, part], sib_recv.at[step, part], me, other).wait_recv()

    def own_sibling_map(part):
        src = maps_hbm.at[0, pieces[part]]
        return remote(src, maps.at[x, tip, pieces[part]], sib_send.at[0, part], sib_recv.at[0, part], me, other)

    spikes_out = remote(
        spikes_hbm.at[0, :, other_columns], spikes.at[tip], side_send.at[0], side_recv.at[0], me, other
    )

    def first_rows(to):
        rows = slice(to * many, (to + 1) * many)
        return remote(tips_hbm.at[0, rows, :], many_in.at[tip], wave_send.at[to], wave_recv.at[tip], 1, to)

    def relay_rows(k):
        return slice(depth - (k + 1) * unit, depth - k * unit)

    def to_relay(k, chip):
        src = maps_hbm.at[0, relay_rows(k)]
        return remote(src, relay.at[k], relay_send.at[0, k], relay_recv.at[0, k], chip + x, tip)

    def from_relay(step, k, chip):
        dst = maps.at[x, tip, relay_rows(k)]
        dom = chip + lax.rem(x + step, RING)
        return remote(relay.at[k], dst, relay_send.at[step, k], relay_recv.at[step, k], dom, tip)

    def pass_on(first, n, chip):
        for k in range(first, first + n):
            remote(relay.at[k], relay.at[k], relay_send.at[0, k], relay_recv.at[0, k], me, other).wait_recv()
            for step in range(1, RING):
                from_relay(step, k, chip).start()

    def relay_drain(first, n, chip):
        for k in range(first, first + n):
            for step in range(1, RING):
                from_relay(step, k, chip).wait_send()

    @pl.when(chained)
    def _():
        @pl.when(me == 0)
        def _():
            for to in range(2):
                first_rows(to).start()

        own_tips.wait()
        for part in range(2):
            own_sibling_map(part).start()
        tip_rows = pl.ds(pl.multiple_of(other * many, many), many)
        tips_copy = remote(
            tips_ref.at[tip_rows, :], tips_many.at[tip], tip_send.at[0], tip_recv.at[0, 1], me, other
        )
        tips_copy.start()
        spikes_out.start()
        own_map.wait()
        for part in range(2):
            sibling_map_arrives(0, part)
        tips_copy.wait_recv()

        def many_send(h, dom):
            return remote(many_out.at[h], many_in.at[h], wave_send.at[h], wave_recv.at[h], dom, tip)

        own_rows = pl.ds(pl.multiple_of(tip * many, many), many)
        tips_many[tip] = tips_ref[own_rows, :]

        @pl.when(me == 0)
        def _():
            many_in[...] = jnp.zeros_like(many_in)

        for those, first, n, _, chip, in_chain in helping:
            if in_chain:
                @pl.when(those)
                def _():
                    pass_on(first, n, chip)

        total = [None, None]
        for k in range(2):
            @pl.when(me > 0)
            def _():
                remote(many_in.at[k], many_in.at[k], wave_send.at[k], wave_recv.at[k], me, other).wait_recv()

            parts = split_rows(many_in[k])
            for h in range(2):
                term = jnp.dot(parts, maps[x, h, k * half : (k + 1) * half, :], preferred_element_type=jnp.float32)
                total[h] = term if k == 0 else total[h] + term
                if k == 1:
                    fresh = total[h][:many] + total[h][many:] + tips_many[h]
                    many_out[h] = fresh

                    @pl.when(jnp.logical_and(me > 0, me < last_chain))
                    def _():
                        many_send(h, me + 1).start()

        @pl.when(me == last_chain)
        def _():
            for piece in range(RING):
                for h in range(2):
                    states[piece, :, h * half : (h + 1) * half] = many_out[h, piece * few : (piece + 1) * few, :]
            for piece in range(RING):
                remote(
                    states.at[piece], few_in, home_send.at[piece, 0], wave_recv.at[2], last_chain + 1 + piece, tip
                ).start()

        to_sibling = remote(many_in, prior_many, side_send.at[1], side_recv.at[1], me, other)
        to_sibling.start()
        for h in range(2):
            full[own_rows, h * half : (h + 1) * half] = many_in[h]
        to_sibling.wait_recv()
        for h in range(2):
            full[tip_rows, h * half : (h + 1) * half] = prior_many[h]

        for those, first, n, _, chip, in_chain in helping:
            if in_chain:
                @pl.when(those)
                def _():
                    relay_drain(first, n, chip)

        to_sibling.wait_send()
        tips_copy.wait_send()
        for part in range(2):
            own_sibling_map(part).wait_send()

        @pl.when(me == 0)
        def _():
            for to in range(2):
                first_rows(to).wait_send()

        @pl.when(jnp.logical_and(me > 0, me < last_chain))
        def _():
            for h in range(2):
                many_send(h, me + 1).wait_send()

        @pl.when(me == last_chain)
        def _():
            for piece in range(RING):
                remote(
                    states.at[piece], few_in, home_send.at[piece, 0], wave_recv.at[2], last_chain + 1 + piece, tip
                ).wait_send()

    @pl.when(ringed)
    def _():
        class Gather:
            def __init__(self, count):
                self.cut = count // 2

            def rows(self, part, k=None):
                if k is None:
                    return slice(part * self.cut, (part + 1) * self.cut)
                size = self.cut // 2
                return slice(part * self.cut + k * size, part * self.cut + (k + 1) * size)

            def own(self, part, side):
                rows = self.rows(part)
                return remote(
                    maps_hbm.at[0, rows], maps.at[x, tip, rows],
                    link_send.at[side, part], link_recv.at[side, part], right if side == 0 else left, tip,
                )

            def neighbour_arrives(self, part, side):
                block = maps.at[lax.rem(x + (3 if side == 0 else 1), RING), tip, self.rows(part)]
                remote(block, block, link_send.at[side, part], link_recv.at[side, part], right, tip).wait_recv()

            def forward(self, side, k):
                block = maps.at[lax.rem(x + (3 if side == 0 else 1), RING), tip, self.rows(side, k)]
                dom = right if side == 0 else left
                return remote(block, block, fwd_send.at[side, k], opp_recv.at[side, k], dom, tip)

            def opposite_arrives(self, side, k):
                block = maps.at[lax.rem(x + 2, RING), tip, self.rows(side, k)]
                remote(block, block, fwd_send.at[side, k], opp_recv.at[side, k], right, tip).wait_recv()

            def to_sibling(self, step, part):
                block = maps.at[lax.rem(x + step, RING), tip, self.rows(part)]
                return remote(block, block, sib_send.at[step, part], sib_recv.at[step, part], me, other)

            def sibling_arrives(self, step, part):
                block = maps.at[lax.rem(x + step, RING), other, self.rows(part)]
                remote(block, block, sib_send.at[step, part], sib_recv.at[step, part], me, other).wait_recv()

            def quarter_to_sibling(self, side, k):
                block = maps.at[lax.rem(x + 2, RING), tip, self.rows(side, k)]
                return remote(block, block, quarter_send.at[side, k], quarter_recv.at[side, k], me, other)

            def sibling_quarter_arrives(self, side, k):
                block = maps.at[lax.rem(x + 2, RING), other, self.rows(side, k)]
                remote(block, block, quarter_send.at[side, k], quarter_recv.at[side, k], me, other).wait_recv()

            def start(self, which=(0, 1)):
                for turn in which:
                    for part, side in (((0, 0), (1, 1)), ((1, 0), (0, 1)))[turn]:
                        self.own(part, side).start()

            def middle(self):
                for part, side in ((0, 0), (1, 1)):
                    self.neighbour_arrives(part, side)
                    for k in range(2):
                        self.forward(side, k).start()
                    self.to_sibling(3 if side == 0 else 1, part).start()
                for part, side in ((1, 0), (0, 1)):
                    self.neighbour_arrives(part, side)
                    self.to_sibling(3 if side == 0 else 1, part).start()

            def last(self):
                for k in range(2):
                    for side in range(2):
                        self.opposite_arrives(side, k)
                        self.quarter_to_sibling(side, k).start()
                for step in (1, 3):
                    for part in range(2):
                        self.sibling_arrives(step, part)
                for k in range(2):
                    for side in range(2):
                        self.sibling_quarter_arrives(side, k)

            def drain(self):
                for part in range(2):
                    for side in range(2):
                        self.own(part, side).wait_send()
                    for k in range(2):
                        self.forward(part, k).wait_send()
                        self.quarter_to_sibling(part, k).wait_send()
                    for step in (1, 3):
                        self.to_sibling(step, part).wait_send()

        whole = Gather(depth)
        gathers = [Gather(depth - count * unit) for _, count, _ in helped]

        def relayed_to_sibling(step, k):
            block = maps.at[lax.rem(x + RING - step, RING), tip, relay_rows(k)]
            return remote(block, block, relay_sib_send.at[step, k], relay_sib_recv.at[step, k], me, other)

        for (those, _, _), gather in zip(helped, gathers):
            @pl.when(those)
            def _():
                gather.start()

        @pl.when(jnp.logical_not(jnp.logical_or(all_helped, all_helping)))
        def _():
            whole.start()

        for those, _, n, _, _, in_chain in helping:
            if not in_chain and n < 3:
                @pl.when(those)
                def _():
                    whole.start((0,))

        own_tips.wait()
        for piece in range(RING):
            for to in range(2):
                start = to * many + piece * few
                tips_out[piece, to * few : (to + 1) * few, :] = tips_ref[start : start + few, :]

        def tip_copy(step, to, number):
            dst_x = lax.rem(x + step, RING)
            return remote(
                tips_out.at[dst_x], tips_both.at[x, tip],
                tip_send.at[number], tip_recv.at[step, jnp.where(to == tip, 0, 1)], base + dst_x, to,
            )

        partners = [(0, other), (1, tip), (1, other), (2, tip), (2, other), (3, tip), (3, other)]
        for number, (step, to) in enumerate(partners):
            tip_copy(step, to, number).start()
        tips_both[x, tip] = tips_out[x]
        for part in range(2):
            own_sibling_map(part).start()
        spikes_out.start()

        for those, _, parts in helped:
            @pl.when(those)
            def _():
                for which, (first, n, chip) in reversed(list(enumerate(parts))):
                    pl.semaphore_wait(relay_open.at[which], 1)
                    for k in range(first, first + n):
                        to_relay(k, chip).start()

        for those, first, n, _, chip, in_chain in helping:
            if not in_chain:
                @pl.when(those)
                def _():
                    pass_on(first, n, chip)
                    whole.start((1,) if n < 3 else (0, 1))

        @pl.when(jnp.logical_not(all_helped))
        def _():
            whole.middle()
            whole.last()

        for (those, count, _), gather in zip(helped, gathers):
            @pl.when(those)
            def _():
                gather.middle()
                for k in range(count):
                    for step in range(1, RING):
                        block = maps.at[lax.rem(x + RING - step, RING), tip, relay_rows(k)]
                        remote(block, block, relay_send.at[step, k], relay_recv.at[step, k], me, other).wait_recv()
                        relayed_to_sibling(step, k).start()
                gather.last()
                for k in range(count):
                    for step in range(1, RING):
                        block = maps.at[lax.rem(x + RING - step, RING), other, relay_rows(k)]
                        remote(
                            block, block, relay_sib_send.at[step, k], relay_sib_recv.at[step, k], me, other
                        ).wait_recv()

        own_map.wait()
        for part in range(2):
            sibling_map_arrives(0, part)
        for step, to in partners:
            remote(
                tips_both.at[0, 0], tips_both.at[0, 0], tip_send.at[0],
                tip_recv.at[step, jnp.where(to == tip, 0, 1)], me, other,
            ).wait_recv()

        mine = tip * RING + x

        def home_copy(step, to):
            src = few_in if step == 0 else states.at[step - 1]
            return remote(src, prior.at[mine], home_send.at[step, to], home_recv.at[mine], base + step, to)

        def send_home(step):
            for to in range(2):
                @pl.when(jnp.logical_or(x != step, tip != to))
                def _():
                    home_copy(step, to).start()

            @pl.when(x == step)
            def _():
                prior[mine] = few_in[...] if step == 0 else states[step - 1]

        def next_state(step, state):
            fresh = times_map(state, maps[step, 0], maps[step, 1])
            for h in range(2):
                states[step, :, h * half : (h + 1) * half] = fresh[h] + tips_few[step, h]
            return states[step]

        def own_of(pair):
            return jnp.where(tip == 0, pair[:few], pair[few:])

        for step in range(RING):
            for h in range(2):
                tips_few[step, h] = own_of(tips_both[step, h])

        final_row = row == rows_total - 1
        to_the_end = jnp.logical_and(final_row, x == RING - 1)

        def to_last(to):
            dom = base + RING - 1
            return remote(columns_out, last_in.at[x, tip], last_send.at[to], last_recv.at[x, tip], dom, to)
        direct = row < PRODUCT_ROW

        def onward_rows(to):
            return remote(states.at[RING - 1], few_in, wave_send.at[to], wave_recv.at[2], me + RING, tip)

        def onward_pair(to):
            return remote(
                states.at[RING - 1], pair_in.at[tip], wave_send.at[to], wave_recv.at[3 + tip], me + RING, to
            )

        def onward_columns(to):
            return remote(columns_out, columns_in.at[tip], wave_send.at[to], wave_recv.at[5 + tip], me + RING, to)

        @pl.when(direct)
        def _():
            remote(few_in, few_in, wave_send.at[0], wave_recv.at[2], me, other).wait_recv()
            state = few_in[...]
            for step in range(RING):
                state = next_state(step, state)

            @pl.when(row < PRODUCT_ROW - 1)
            def _():
                onward_rows(0).start()

            @pl.when(jnp.logical_and(row == PRODUCT_ROW - 1, jnp.logical_not(final_row)))
            def _():
                for to in range(2):
                    onward_pair(to).start()

            for step in range(RING):
                send_home(step)

        @pl.when(jnp.logical_not(direct))
        def _():
            def prepare(last):
                leading_maps(last, maps, tip, high, low)
                state = jnp.concatenate([tips_both[0, 0], tips_both[0, 1]], 1)
                for step in range(1, last):
                    fresh = times_map(state, maps[step, 0], maps[step, 1])
                    state = jnp.concatenate([fresh[h] + tips_both[step, h] for h in range(2)], 1)
                parts = split_rows(state)
                fresh = jnp.dot(parts, maps[last, tip], preferred_element_type=jnp.float32)
                local[...] = fresh[: 2 * few] + fresh[2 * few :] + tips_both[last, tip]

            def start_state():
                for h in range(2):
                    few_in[:, h * half : (h + 1) * half] = own_of(columns_in[h])
                send_home(0)

            def product_step(last):
                slot = (last - 1) % 2
                parts = split_rows(jnp.concatenate([columns_in[0], columns_in[1]], 1))
                fresh = jnp.dot(parts, high[slot], preferred_element_type=jnp.float32)
                fresh = fresh + jnp.dot(parts, low[slot], preferred_element_type=jnp.float32)
                columns_out[...] = fresh[: 2 * few] + fresh[2 * few :] + local[...]

            @pl.when(jnp.logical_not(final_row))
            def _():
                prepare(RING - 1)

            @pl.when(final_row)
            def _():
                prepare(RING - 2)

            @pl.when(row == PRODUCT_ROW)
            def _():
                for core in range(2):
                    remote(
                        pair_in.at[core], pair_in.at[core], wave_send.at[0], wave_recv.at[3 + core], me, other
                    ).wait_recv()
                for core in range(2):
                    for h in range(2):
                        columns_in[h, core * few : (core + 1) * few, :] = pair_in[core, :, h * half : (h + 1) * half]

            def columns_arrive(core):
                remote(
                    columns_in.at[core], columns_in.at[core], wave_send.at[0], wave_recv.at[5 + core], me, other
                ).wait_recv()

            @pl.when(row > PRODUCT_ROW)
            def _():
                for core in range(2):
                    columns_arrive(core)

            @pl.when(jnp.logical_not(final_row))
            def _():
                product_step(RING - 1)
                for to in range(2):
                    onward_columns(to).start()

            @pl.when(final_row)
            def _():
                start_state()
                product_step(RING - 2)
                for to in range(2):
                    @pl.when(jnp.logical_or(x != RING - 1, tip != to))
                    def _():
                        to_last(to).start()

                @pl.when(x == RING - 1)
                def _():
                    last_in[x, tip] = columns_out[...]

            @pl.when(jnp.logical_not(final_row))
            def _():
                start_state()

            state = few_in[...]
            for step in range(RING - 2):
                state = next_state(step, state)
                send_home(step + 1)

            @pl.when(jnp.logical_not(final_row))
            def _():
                next_state(RING - 2, state)
                send_home(RING - 1)

        @pl.when(to_the_end)
        def _():
            for chip in range(RING):
                for core in range(2):
                    @pl.when(jnp.logical_or(chip != x, core != tip))
                    def _():
                        block = last_in.at[chip, core]
                        remote(block, block, last_send.at[0], last_recv.at[chip, core], me, other).wait_recv()
            for chip in range(RING):
                for core in range(2):
                    columns = slice(core * half, (core + 1) * half)
                    for group in range(2):
                        start = group * many + chip * few
                        block = last_in[chip, core, group * few : (group + 1) * few, :]
                        full[start : start + few, columns] = block

        @pl.when(jnp.logical_not(to_the_end))
        def _():
            for piece in range(2 * RING):
                @pl.when(piece != mine)
                def _():
                    remote(
                        prior.at[piece], prior.at[piece], home_send.at[0, 0], home_recv.at[piece], me, other
                    ).wait_recv()
            for piece in range(2 * RING):
                full[piece * few : (piece + 1) * few, :] = prior[piece]

        @pl.when(jnp.logical_not(all_helped))
        def _():
            whole.drain()

        for those, first, n, _, chip, in_chain in helping:
            if not in_chain:
                @pl.when(those)
                def _():
                    relay_drain(first, n, chip)

        for (those, _, parts), gather in zip(helped, gathers):
            @pl.when(those)
            def _():
                gather.drain()
                for first, n, chip in parts:
                    for k in range(first, first + n):
                        to_relay(k, chip).wait_send()
                        for step in range(1, RING):
                            relayed_to_sibling(step, k).wait_send()

        for part in range(2):
            own_sibling_map(part).wait_send()
        for number, (step, to) in enumerate(partners):
            tip_copy(step, to, number).wait_send()

        @pl.when(row < PRODUCT_ROW - 1)
        def _():
            onward_rows(0).wait_send()

        @pl.when(jnp.logical_and(row == PRODUCT_ROW - 1, jnp.logical_not(final_row)))
        def _():
            for to in range(2):
                onward_pair(to).wait_send()

        @pl.when(jnp.logical_and(row >= PRODUCT_ROW, jnp.logical_not(final_row)))
        def _():
            for to in range(2):
                onward_columns(to).wait_send()

        for step in range(RING - 1):
            for to in range(2):
                @pl.when(jnp.logical_or(x != step, tip != to))
                def _():
                    home_copy(step, to).wait_send()

        for to in range(2):
            @pl.when(jnp.logical_or(x != RING - 1, tip != to))
            def _():
                @pl.when(final_row)
                def _():
                    to_last(to).wait_send()

                @pl.when(jnp.logical_not(final_row))
                def _():
                    home_copy(RING - 1, to).wait_send()

    own_spikes.wait()
    spikes_out.wait()
    count = full.shape[0]
    parts = split_rows(full[...])
    fresh = jnp.dot(parts, maps[x, tip], preferred_element_type=jnp.float32)
    interface_ref[0] = fresh[:count] + fresh[count:]
    middle = spikes.shape[1]
    product = jnp.dot(parts[:count, :middle], spikes[0], preferred_element_type=jnp.float32)
    product_ref[0] = product + jnp.dot(parts[:count, middle:], spikes[1], preferred_element_type=jnp.float32)


def on_device(band_maps, right_tips, spikes, local_parts):
    rows_total = lax.axis_size("dom") // RING
    _, depth, half = band_maps.shape
    count = right_tips.shape[1]
    many = count // 2
    few = many // RING
    _, spike_rows, spike_columns = spikes.shape
    width = spike_columns // 2
    f32, b16, dma = jnp.float32, jnp.bfloat16, pltpu.SemaphoreType.DMA
    interface, product = pl.pallas_call(
        functools.partial(sweep, rows_total),
        out_shape=(
            jax.ShapeDtypeStruct((1, count, half), f32),
            jax.ShapeDtypeStruct((1, count, width), f32),
        ),
        in_specs=[
            pl.BlockSpec(memory_space=pltpu.HBM),
            pl.BlockSpec(memory_space=pltpu.HBM),
            pl.BlockSpec(memory_space=pltpu.HBM),
        ],
        out_specs=(pl.BlockSpec(memory_space=pltpu.VMEM),) * 2,
        scratch_shapes=[
            pltpu.VMEM((RING, 2, depth, half), b16),
            pltpu.VMEM((count, half), f32),
            pltpu.VMEM((RING, 2 * few, half), f32),
            pltpu.VMEM((RING, 2, 2 * few, half), f32),
            pltpu.VMEM((RING, 2, few, half), f32),
            pltpu.VMEM((2, many, half), f32),
            pltpu.VMEM((few, depth), f32),
            pltpu.VMEM((2, few, depth), f32),
            pltpu.VMEM((2, 2 * few, half), f32),
            pltpu.VMEM((2 * few, half), f32),
            pltpu.VMEM((2 * few, half), f32),
            pltpu.VMEM((2, depth, half), b16),
            pltpu.VMEM((2, depth, half), b16),
            pltpu.VMEM((2, many, half), f32),
            pltpu.VMEM((2, many, half), f32),
            pltpu.VMEM((RING, few, depth), f32),
            pltpu.VMEM((2 * RING, few, depth), f32),
            pltpu.VMEM((2, many, half), f32),
            pltpu.VMEM((count, depth), f32),
            pltpu.VMEM((2, spike_rows, width), b16),
            dma((3,)),
            dma((RING, 2)),
            dma((RING, 2)),
            dma((2, 2)),
            dma((2, 2)),
            pltpu.VMEM((5, depth // 16, half), b16),
            pltpu.SemaphoreType.REGULAR((2,)),
            dma((RING, 5)),
            dma((RING, 5)),
            dma((RING, 5)),
            dma((RING, 5)),
            dma((2, 2)),
            dma((2, 2)),
            dma((2, 2)),
            dma((2, 2)),
            dma((2 * RING - 1,)),
            dma((RING, 2)),
            dma((2,)),
            dma((7,)),
            dma((RING, 2)),
            dma((2 * RING,)),
            dma((2,)),
            dma((2,)),
            pltpu.VMEM((RING, 2, 2 * few, half), f32),
            dma((2,)),
            dma((RING, 2)),
        ],
        compiler_params=pltpu.CompilerParams(
            collective_id=0, has_side_effects=True, vmem_limit_bytes=53 << 20
        ),
    )(band_maps, right_tips, spikes)
    return right_tips + interface, local_parts - product


def solution(mesh):
    return jax.shard_map(
        on_device,
        mesh=mesh,
        in_specs=(
            P("dom", None, "tip"),
            P("dom", None, "tip"),
            P("dom", "tip", None),
            P("dom", None, "tip"),
        ),
        out_specs=(P("dom", None, "tip"), P("dom", None, "tip")),
        check_vma=False,
    )
```

```python
import functools

import jax
import jax.numpy as jnp
from jax import lax
from jax.experimental import pallas as pl
from jax.experimental.pallas import tpu as pltpu
from jax.sharding import PartitionSpec as P

MESH = pl.DeviceIdType.MESH
RING = 4
CHAIN_ROWS = 2
HELPERS = {
    2: ((14, 3), (1, 2)),
    3: ((15, 4),),
    4: ((13, 4),),
    5: ((12, 3),),
    6: ((10, 2),),
    7: ((11, 2),),
}
PRODUCT_ROW = 4


def split_rows(value):
    high = value.astype(jnp.bfloat16)
    low = value - high.astype(jnp.float32)
    return jnp.concatenate([high.astype(jnp.float32), low], 0).astype(jnp.bfloat16)


def times_map(value, left, right):
    rows = value.shape[0]
    parts = split_rows(value)
    out = [jnp.dot(parts, half, preferred_element_type=jnp.float32) for half in (left, right)]
    return [piece[:rows] + piece[rows:] for piece in out]


def leading_maps(last, maps, tip, high, low):
    half = maps.shape[3]
    block = min(256, half)
    for turn, step in enumerate(range(last - 1, -1, -1)):
        factor = jnp.concatenate([maps[step, 0], maps[step, 1]], 1)
        for start in range(0, half, block):
            columns = slice(start, start + block)
            if turn == 0:
                total = jnp.dot(factor, maps[last, tip, :, columns], preferred_element_type=jnp.float32)
            else:
                total = jnp.dot(factor, high[(turn - 1) % 2, :, columns], preferred_element_type=jnp.float32)
                total += jnp.dot(factor, low[(turn - 1) % 2, :, columns], preferred_element_type=jnp.float32)
            top = total.astype(jnp.bfloat16)
            high[turn % 2, :, columns] = top
            low[turn % 2, :, columns] = (total - top.astype(jnp.float32)).astype(jnp.bfloat16)
    return (last - 1) % 2


def sweep(
    rows_total, maps_hbm, tips_hbm, spikes_hbm, interface_ref, product_ref,
    maps, tips_ref, tips_out, tips_both, tips_few, tips_many, few_in, pair_in, columns_in, columns_out, local,
    high, low, many_in, many_out, states, prior, prior_many, full, spikes,
    local_sem, sib_send, sib_recv, quarter_send, quarter_recv, relay, relay_open, relay_send, relay_recv,
    relay_sib_send, relay_sib_recv,
    link_send, link_recv, fwd_send, opp_recv,
    tip_send, tip_recv, wave_send, wave_recv, home_send, home_recv, side_send, side_recv,
    last_in, last_send, last_recv,
):
    me, tip = lax.axis_index("dom"), lax.axis_index("tip")
    x, row = lax.rem(me, RING), lax.div(me, RING)
    other = 1 - tip
    base = me - x
    depth = maps_hbm.shape[1]
    half = maps_hbm.shape[2]
    cut = depth // 2
    width = spikes_hbm.shape[2] // 2
    chained = row < CHAIN_ROWS
    ringed = row >= CHAIN_ROWS
    def among(rows):
        return functools.reduce(jnp.logical_or, [row == r for r in rows])

    def first_chip(pairs):
        value = pairs[0][1]
        for this, that in pairs[1:]:
            value = jnp.where(row == this, that, value)
        return value * RING

    by_shares, by_part = {}, {}
    for r, helpers in HELPERS.items():
        by_shares.setdefault(tuple(n for _, n in helpers), []).append(r)
        first = 0
        for which, (h, n) in enumerate(helpers):
            by_part.setdefault((first, n, which, h < CHAIN_ROWS), []).append((h, r))
            first += n
    helped = []
    for shares, rows in by_shares.items():
        parts = [
            (sum(shares[:which]), shares[which], first_chip([(r, HELPERS[r][which][0]) for r in rows]))
            for which in range(len(shares))
        ]
        helped.append((among(rows), sum(shares), parts))
    helping = [
        (among([h for h, _ in pairs]), first, n, which, first_chip(pairs), in_chain)
        for (first, n, which, in_chain), pairs in by_part.items()
    ]
    all_helped = among(list(HELPERS))
    all_helping = among([h for helpers in HELPERS.values() for h, _ in helpers])
    unit = maps_hbm.shape[1] // 16
    last_chain = CHAIN_ROWS * RING - 1
    right, left = base + lax.rem(x + 1, RING), base + lax.rem(x + 3, RING)
    opposite = base + lax.rem(x + 2, RING)
    many = full.shape[0] // 2
    few = many // RING

    def remote(src, dst, send, recv, dom, to):
        return pltpu.make_async_remote_copy(
            src_ref=src, dst_ref=dst, send_sem=send, recv_sem=recv, device_id=(dom, to), device_id_type=MESH
        )

    barrier = pltpu.get_barrier_semaphore()

    def greet(dom, to):
        pl.semaphore_signal(barrier, inc=1, device_id=(dom, to), device_id_type=MESH)

    greet(me, other)

    @pl.when(chained)
    def _():
        @pl.when(me > 0)
        def _():
            greet(me - 1, tip)

        @pl.when(me == 1)
        def _():
            greet(0, other)

    @pl.when(ringed)
    def _():
        for step in range(1, RING):
            for to in range(2):
                greet(base + lax.rem(x + step, RING), to)
        before = jnp.where(row == CHAIN_ROWS, last_chain, me - RING)
        greet(before, tip)

        @pl.when(row >= PRODUCT_ROW)
        def _():
            greet(before, other)

        for those, _, parts in helped:
            @pl.when(those)
            def _():
                for _, _, chip in parts:
                    greet(chip + x, tip)

    own_map = pltpu.make_async_copy(maps_hbm.at[0], maps.at[x, tip], local_sem.at[0])
    own_map.start()
    own_columns = pl.ds(pl.multiple_of(tip * width, width), width)
    other_columns = pl.ds(pl.multiple_of(other * width, width), width)
    own_spikes = pltpu.make_async_copy(spikes_hbm.at[0, :, own_columns], spikes.at[tip], local_sem.at[1])
    own_spikes.start()
    own_tips = pltpu.make_async_copy(tips_hbm.at[0], tips_ref, local_sem.at[2])
    own_tips.start()
    asked = jnp.where(all_helping, 1, 0)

    @pl.when(chained)
    def _():
        pl.semaphore_wait(barrier, jnp.where(me == last_chain, 1 + RING, jnp.where(me == 0, 3, 2)) + asked)

    @pl.when(ringed)
    def _():
        after = jnp.where(row == rows_total - 1, 0, jnp.where(row >= PRODUCT_ROW - 1, 2, 1))
        pl.semaphore_wait(barrier, 2 * RING - 1 + after + asked)

    for those, _, _, which, chip, _ in helping:
        @pl.when(those)
        def _():
            pl.semaphore_signal(relay_open.at[which], inc=1, device_id=(chip + x, tip), device_id_type=MESH)

    pieces = [slice(0, cut), slice(cut, depth)]

    def sibling_map_arrives(step, part):
        slot = lax.rem(x + step, RING)
        block = maps.at[slot, other, pieces[part]]
        remote(block, block, sib_send.at[step, part], sib_recv.at[step, part], me, other).wait_recv()

    def own_sibling_map(part):
        src = maps_hbm.at[0, pieces[part]]
        return remote(src, maps.at[x, tip, pieces[part]], sib_send.at[0, part], sib_recv.at[0, part], me, other)

    spikes_out = remote(
        spikes_hbm.at[0, :, other_columns], spikes.at[tip], side_send.at[0], side_recv.at[0], me, other
    )

    def first_rows(to):
        rows = slice(to * many, (to + 1) * many)
        return remote(tips_hbm.at[0, rows, :], many_in.at[tip], wave_send.at[to], wave_recv.at[tip], 1, to)

    def relay_rows(k):
        return slice(depth - (k + 1) * unit, depth - k * unit)

    def to_relay(k, chip):
        src = maps_hbm.at[0, relay_rows(k)]
        return remote(src, relay.at[k], relay_send.at[0, k], relay_recv.at[0, k], chip + x, tip)

    def from_relay(step, k, chip):
        dst = maps.at[x, tip, relay_rows(k)]
        dom = chip + lax.rem(x + step, RING)
        return remote(relay.at[k], dst, relay_send.at[step, k], relay_recv.at[step, k], dom, tip)

    def pass_on(first, n, chip):
        for k in range(first, first + n):
            remote(relay.at[k], relay.at[k], relay_send.at[0, k], relay_recv.at[0, k], me, other).wait_recv()
            for step in range(1, RING):
                from_relay(step, k, chip).start()

    def relay_drain(first, n, chip):
        for k in range(first, first + n):
            for step in range(1, RING):
                from_relay(step, k, chip).wait_send()

    @pl.when(chained)
    def _():
        @pl.when(me == 0)
        def _():
            for to in range(2):
                first_rows(to).start()

        own_tips.wait()
        for part in range(2):
            own_sibling_map(part).start()
        tip_rows = pl.ds(pl.multiple_of(other * many, many), many)
        tips_copy = remote(
            tips_ref.at[tip_rows, :], tips_many.at[tip], tip_send.at[0], tip_recv.at[0, 1], me, other
        )
        tips_copy.start()
        spikes_out.start()
        own_map.wait()
        for part in range(2):
            sibling_map_arrives(0, part)
        tips_copy.wait_recv()

        def many_send(h, dom):
            return remote(many_out.at[h], many_in.at[h], wave_send.at[h], wave_recv.at[h], dom, tip)

        own_rows = pl.ds(pl.multiple_of(tip * many, many), many)
        tips_many[tip] = tips_ref[own_rows, :]

        @pl.when(me == 0)
        def _():
            many_in[...] = jnp.zeros_like(many_in)

        for those, first, n, _, chip, in_chain in helping:
            if in_chain:
                @pl.when(those)
                def _():
                    pass_on(first, n, chip)

        total = [None, None]
        for k in range(2):
            @pl.when(me > 0)
            def _():
                remote(many_in.at[k], many_in.at[k], wave_send.at[k], wave_recv.at[k], me, other).wait_recv()

            parts = split_rows(many_in[k])
            for h in range(2):
                term = jnp.dot(parts, maps[x, h, k * half : (k + 1) * half, :], preferred_element_type=jnp.float32)
                total[h] = term if k == 0 else total[h] + term
                if k == 1:
                    fresh = total[h][:many] + total[h][many:] + tips_many[h]
                    many_out[h] = fresh

                    @pl.when(jnp.logical_and(me > 0, me < last_chain))
                    def _():
                        many_send(h, me + 1).start()

        @pl.when(me == last_chain)
        def _():
            for piece in range(RING):
                for h in range(2):
                    states[piece, :, h * half : (h + 1) * half] = many_out[h, piece * few : (piece + 1) * few, :]
            for piece in range(RING):
                remote(
                    states.at[piece], few_in, home_send.at[piece, 0], wave_recv.at[2], last_chain + 1 + piece, tip
                ).start()

        to_sibling = remote(many_in, prior_many, side_send.at[1], side_recv.at[1], me, other)
        to_sibling.start()
        for h in range(2):
            full[own_rows, h * half : (h + 1) * half] = many_in[h]
        to_sibling.wait_recv()
        for h in range(2):
            full[tip_rows, h * half : (h + 1) * half] = prior_many[h]

        for those, first, n, _, chip, in_chain in helping:
            if in_chain:
                @pl.when(those)
                def _():
                    relay_drain(first, n, chip)

        to_sibling.wait_send()
        tips_copy.wait_send()
        for part in range(2):
            own_sibling_map(part).wait_send()

        @pl.when(me == 0)
        def _():
            for to in range(2):
                first_rows(to).wait_send()

        @pl.when(jnp.logical_and(me > 0, me < last_chain))
        def _():
            for h in range(2):
                many_send(h, me + 1).wait_send()

        @pl.when(me == last_chain)
        def _():
            for piece in range(RING):
                remote(
                    states.at[piece], few_in, home_send.at[piece, 0], wave_recv.at[2], last_chain + 1 + piece, tip
                ).wait_send()

    @pl.when(ringed)
    def _():
        class Gather:
            def __init__(self, count):
                self.cut = count // 2

            def rows(self, part, k=None):
                if k is None:
                    return slice(part * self.cut, (part + 1) * self.cut)
                size = self.cut // 2
                return slice(part * self.cut + k * size, part * self.cut + (k + 1) * size)

            def own(self, part, side):
                rows = self.rows(part)
                return remote(
                    maps_hbm.at[0, rows], maps.at[x, tip, rows],
                    link_send.at[side, part], link_recv.at[side, part], right if side == 0 else left, tip,
                )

            def neighbour_arrives(self, part, side):
                block = maps.at[lax.rem(x + (3 if side == 0 else 1), RING), tip, self.rows(part)]
                remote(block, block, link_send.at[side, part], link_recv.at[side, part], right, tip).wait_recv()

            def forward(self, side, k):
                block = maps.at[lax.rem(x + (3 if side == 0 else 1), RING), tip, self.rows(side, k)]
                dom = right if side == 0 else left
                return remote(block, block, fwd_send.at[side, k], opp_recv.at[side, k], dom, tip)

            def opposite_arrives(self, side, k):
                block = maps.at[lax.rem(x + 2, RING), tip, self.rows(side, k)]
                remote(block, block, fwd_send.at[side, k], opp_recv.at[side, k], right, tip).wait_recv()

            def to_sibling(self, step, part):
                block = maps.at[lax.rem(x + step, RING), tip, self.rows(part)]
                return remote(block, block, sib_send.at[step, part], sib_recv.at[step, part], me, other)

            def sibling_arrives(self, step, part):
                block = maps.at[lax.rem(x + step, RING), other, self.rows(part)]
                remote(block, block, sib_send.at[step, part], sib_recv.at[step, part], me, other).wait_recv()

            def quarter_to_sibling(self, side, k):
                block = maps.at[lax.rem(x + 2, RING), tip, self.rows(side, k)]
                return remote(block, block, quarter_send.at[side, k], quarter_recv.at[side, k], me, other)

            def sibling_quarter_arrives(self, side, k):
                block = maps.at[lax.rem(x + 2, RING), other, self.rows(side, k)]
                remote(block, block, quarter_send.at[side, k], quarter_recv.at[side, k], me, other).wait_recv()

            def start(self, which=(0, 1)):
                for turn in which:
                    for part, side in (((0, 0), (1, 1)), ((1, 0), (0, 1)))[turn]:
                        self.own(part, side).start()

            def middle(self):
                for part, side in ((0, 0), (1, 1)):
                    self.neighbour_arrives(part, side)
                    for k in range(2):
                        self.forward(side, k).start()
                    self.to_sibling(3 if side == 0 else 1, part).start()
                for part, side in ((1, 0), (0, 1)):
                    self.neighbour_arrives(part, side)
                    self.to_sibling(3 if side == 0 else 1, part).start()

            def last(self):
                for k in range(2):
                    for side in range(2):
                        self.opposite_arrives(side, k)
                        self.quarter_to_sibling(side, k).start()
                for step in (1, 3):
                    for part in range(2):
                        self.sibling_arrives(step, part)
                for k in range(2):
                    for side in range(2):
                        self.sibling_quarter_arrives(side, k)

            def drain(self):
                for part in range(2):
                    for side in range(2):
                        self.own(part, side).wait_send()
                    for k in range(2):
                        self.forward(part, k).wait_send()
                        self.quarter_to_sibling(part, k).wait_send()
                    for step in (1, 3):
                        self.to_sibling(step, part).wait_send()

        whole = Gather(depth)
        gathers = [Gather(depth - count * unit) for _, count, _ in helped]

        def relayed_to_sibling(step, k):
            block = maps.at[lax.rem(x + RING - step, RING), tip, relay_rows(k)]
            return remote(block, block, relay_sib_send.at[step, k], relay_sib_recv.at[step, k], me, other)

        for (those, _, _), gather in zip(helped, gathers):
            @pl.when(those)
            def _():
                gather.start()

        @pl.when(jnp.logical_not(jnp.logical_or(all_helped, all_helping)))
        def _():
            whole.start()

        for those, _, n, _, _, in_chain in helping:
            if not in_chain and n < 3:
                @pl.when(those)
                def _():
                    whole.start((0,))

        own_tips.wait()
        for piece in range(RING):
            for to in range(2):
                start = to * many + piece * few
                tips_out[piece, to * few : (to + 1) * few, :] = tips_ref[start : start + few, :]

        def tip_copy(step, to, number):
            dst_x = lax.rem(x + step, RING)
            return remote(
                tips_out.at[dst_x], tips_both.at[x, tip],
                tip_send.at[number], tip_recv.at[step, jnp.where(to == tip, 0, 1)], base + dst_x, to,
            )

        partners = [(0, other), (1, tip), (1, other), (2, tip), (2, other), (3, tip), (3, other)]
        for number, (step, to) in enumerate(partners):
            tip_copy(step, to, number).start()
        tips_both[x, tip] = tips_out[x]
        for part in range(2):
            own_sibling_map(part).start()
        spikes_out.start()

        for those, _, parts in helped:
            @pl.when(those)
            def _():
                for which, (first, n, chip) in reversed(list(enumerate(parts))):
                    pl.semaphore_wait(relay_open.at[which], 1)
                    for k in range(first, first + n):
                        to_relay(k, chip).start()

        for those, first, n, _, chip, in_chain in helping:
            if not in_chain:
                @pl.when(those)
                def _():
                    pass_on(first, n, chip)
                    whole.start((1,) if n < 3 else (0, 1))

        @pl.when(jnp.logical_not(all_helped))
        def _():
            whole.middle()
            whole.last()

        for (those, count, _), gather in zip(helped, gathers):
            @pl.when(those)
            def _():
                gather.middle()
                for k in range(count):
                    for step in range(1, RING):
                        block = maps.at[lax.rem(x + RING - step, RING), tip, relay_rows(k)]
                        remote(block, block, relay_send.at[step, k], relay_recv.at[step, k], me, other).wait_recv()
                        relayed_to_sibling(step, k).start()
                gather.last()
                for k in range(count):
                    for step in range(1, RING):
                        block = maps.at[lax.rem(x + RING - step, RING), other, relay_rows(k)]
                        remote(
                            block, block, relay_sib_send.at[step, k], relay_sib_recv.at[step, k], me, other
                        ).wait_recv()

        own_map.wait()
        for part in range(2):
            sibling_map_arrives(0, part)
        for step, to in partners:
            remote(
                tips_both.at[0, 0], tips_both.at[0, 0], tip_send.at[0],
                tip_recv.at[step, jnp.where(to == tip, 0, 1)], me, other,
            ).wait_recv()

        mine = tip * RING + x

        def home_copy(step, to):
            src = few_in if step == 0 else states.at[step - 1]
            return remote(src, prior.at[mine], home_send.at[step, to], home_recv.at[mine], base + step, to)

        def send_home(step):
            for to in range(2):
                @pl.when(jnp.logical_or(x != step, tip != to))
                def _():
                    home_copy(step, to).start()

            @pl.when(x == step)
            def _():
                prior[mine] = few_in[...] if step == 0 else states[step - 1]

        def next_state(step, state):
            fresh = times_map(state, maps[step, 0], maps[step, 1])
            for h in range(2):
                states[step, :, h * half : (h + 1) * half] = fresh[h] + tips_few[step, h]
            return states[step]

        def own_of(pair):
            return jnp.where(tip == 0, pair[:few], pair[few:])

        for step in range(RING):
            for h in range(2):
                tips_few[step, h] = own_of(tips_both[step, h])

        final_row = row == rows_total - 1
        to_the_end = jnp.logical_and(final_row, x == RING - 1)

        def to_last(to):
            dom = base + RING - 1
            return remote(columns_out, last_in.at[x, tip], last_send.at[to], last_recv.at[x, tip], dom, to)
        direct = row < PRODUCT_ROW

        def onward_rows(to):
            return remote(states.at[RING - 1], few_in, wave_send.at[to], wave_recv.at[2], me + RING, tip)

        def onward_pair(to):
            return remote(
                states.at[RING - 1], pair_in.at[tip], wave_send.at[to], wave_recv.at[3 + tip], me + RING, to
            )

        def onward_columns(to):
            return remote(columns_out, columns_in.at[tip], wave_send.at[to], wave_recv.at[5 + tip], me + RING, to)

        @pl.when(direct)
        def _():
            remote(few_in, few_in, wave_send.at[0], wave_recv.at[2], me, other).wait_recv()
            state = few_in[...]
            for step in range(RING):
                state = next_state(step, state)

            @pl.when(row < PRODUCT_ROW - 1)
            def _():
                onward_rows(0).start()

            @pl.when(jnp.logical_and(row == PRODUCT_ROW - 1, jnp.logical_not(final_row)))
            def _():
                for to in range(2):
                    onward_pair(to).start()

            for step in range(RING):
                send_home(step)

        @pl.when(jnp.logical_not(direct))
        def _():
            def prepare(last):
                leading_maps(last, maps, tip, high, low)
                state = jnp.concatenate([tips_both[0, 0], tips_both[0, 1]], 1)
                for step in range(1, last):
                    fresh = times_map(state, maps[step, 0], maps[step, 1])
                    state = jnp.concatenate([fresh[h] + tips_both[step, h] for h in range(2)], 1)
                parts = split_rows(state)
                fresh = jnp.dot(parts, maps[last, tip], preferred_element_type=jnp.float32)
                local[...] = fresh[: 2 * few] + fresh[2 * few :] + tips_both[last, tip]

            def start_state():
                for h in range(2):
                    few_in[:, h * half : (h + 1) * half] = own_of(columns_in[h])
                send_home(0)

            def product_step(last):
                slot = (last - 1) % 2
                parts = split_rows(jnp.concatenate([columns_in[0], columns_in[1]], 1))
                fresh = jnp.dot(parts, high[slot], preferred_element_type=jnp.float32)
                fresh = fresh + jnp.dot(parts, low[slot], preferred_element_type=jnp.float32)
                columns_out[...] = fresh[: 2 * few] + fresh[2 * few :] + local[...]

            @pl.when(jnp.logical_not(final_row))
            def _():
                prepare(RING - 1)

            @pl.when(final_row)
            def _():
                prepare(RING - 2)

            @pl.when(row == PRODUCT_ROW)
            def _():
                for core in range(2):
                    remote(
                        pair_in.at[core], pair_in.at[core], wave_send.at[0], wave_recv.at[3 + core], me, other
                    ).wait_recv()
                for core in range(2):
                    for h in range(2):
                        columns_in[h, core * few : (core + 1) * few, :] = pair_in[core, :, h * half : (h + 1) * half]

            def columns_arrive(core):
                remote(
                    columns_in.at[core], columns_in.at[core], wave_send.at[0], wave_recv.at[5 + core], me, other
                ).wait_recv()

            @pl.when(row > PRODUCT_ROW)
            def _():
                for core in range(2):
                    columns_arrive(core)

            @pl.when(jnp.logical_not(final_row))
            def _():
                product_step(RING - 1)
                for to in range(2):
                    onward_columns(to).start()

            @pl.when(final_row)
            def _():
                start_state()
                product_step(RING - 2)
                for to in range(2):
                    @pl.when(jnp.logical_or(x != RING - 1, tip != to))
                    def _():
                        to_last(to).start()

                @pl.when(x == RING - 1)
                def _():
                    last_in[x, tip] = columns_out[...]

            @pl.when(jnp.logical_not(final_row))
            def _():
                start_state()

            state = few_in[...]
            for step in range(RING - 2):
                state = next_state(step, state)
                send_home(step + 1)

            @pl.when(jnp.logical_not(final_row))
            def _():
                next_state(RING - 2, state)
                send_home(RING - 1)

        @pl.when(to_the_end)
        def _():
            for chip in range(RING):
                for core in range(2):
                    @pl.when(jnp.logical_or(chip != x, core != tip))
                    def _():
                        block = last_in.at[chip, core]
                        remote(block, block, last_send.at[0], last_recv.at[chip, core], me, other).wait_recv()
            for chip in range(RING):
                for core in range(2):
                    columns = slice(core * half, (core + 1) * half)
                    for group in range(2):
                        start = group * many + chip * few
                        block = last_in[chip, core, group * few : (group + 1) * few, :]
                        full[start : start + few, columns] = block

        @pl.when(jnp.logical_not(to_the_end))
        def _():
            for piece in range(2 * RING):
                @pl.when(piece != mine)
                def _():
                    remote(
                        prior.at[piece], prior.at[piece], home_send.at[0, 0], home_recv.at[piece], me, other
                    ).wait_recv()
            for piece in range(2 * RING):
                full[piece * few : (piece + 1) * few, :] = prior[piece]

        @pl.when(jnp.logical_not(all_helped))
        def _():
            whole.drain()

        for those, first, n, _, chip, in_chain in helping:
            if not in_chain:
                @pl.when(those)
                def _():
                    relay_drain(first, n, chip)

        for (those, _, parts), gather in zip(helped, gathers):
            @pl.when(those)
            def _():
                gather.drain()
                for first, n, chip in parts:
                    for k in range(first, first + n):
                        to_relay(k, chip).wait_send()
                        for step in range(1, RING):
                            relayed_to_sibling(step, k).wait_send()

        for part in range(2):
            own_sibling_map(part).wait_send()
        for number, (step, to) in enumerate(partners):
            tip_copy(step, to, number).wait_send()

        @pl.when(row < PRODUCT_ROW - 1)
        def _():
            onward_rows(0).wait_send()

        @pl.when(jnp.logical_and(row == PRODUCT_ROW - 1, jnp.logical_not(final_row)))
        def _():
            for to in range(2):
                onward_pair(to).wait_send()

        @pl.when(jnp.logical_and(row >= PRODUCT_ROW, jnp.logical_not(final_row)))
        def _():
            for to in range(2):
                onward_columns(to).wait_send()

        for step in range(RING - 1):
            for to in range(2):
                @pl.when(jnp.logical_or(x != step, tip != to))
                def _():
                    home_copy(step, to).wait_send()

        for to in range(2):
            @pl.when(jnp.logical_or(x != RING - 1, tip != to))
            def _():
                @pl.when(final_row)
                def _():
                    to_last(to).wait_send()

                @pl.when(jnp.logical_not(final_row))
                def _():
                    home_copy(RING - 1, to).wait_send()

    own_spikes.wait()
    spikes_out.wait()
    count = full.shape[0]
    parts = split_rows(full[...])
    fresh = jnp.dot(parts, maps[x, tip], preferred_element_type=jnp.float32)
    interface_ref[0] = fresh[:count] + fresh[count:]
    middle = spikes.shape[1]
    product = jnp.dot(parts[:count, :middle], spikes[0], preferred_element_type=jnp.float32)
    product_ref[0] = product + jnp.dot(parts[:count, middle:], spikes[1], preferred_element_type=jnp.float32)


def on_device(band_maps, right_tips, spikes, local_parts):
    rows_total = lax.axis_size("dom") // RING
    _, depth, half = band_maps.shape
    count = right_tips.shape[1]
    many = count // 2
    few = many // RING
    _, spike_rows, spike_columns = spikes.shape
    width = spike_columns // 2
    f32, b16, dma = jnp.float32, jnp.bfloat16, pltpu.SemaphoreType.DMA
    interface, product = pl.pallas_call(
        functools.partial(sweep, rows_total),
        out_shape=(
            jax.ShapeDtypeStruct((1, count, half), f32),
            jax.ShapeDtypeStruct((1, count, width), f32),
        ),
        in_specs=[
            pl.BlockSpec(memory_space=pltpu.HBM),
            pl.BlockSpec(memory_space=pltpu.HBM),
            pl.BlockSpec(memory_space=pltpu.HBM),
        ],
        out_specs=(pl.BlockSpec(memory_space=pltpu.VMEM),) * 2,
        scratch_shapes=[
            pltpu.VMEM((RING, 2, depth, half), b16),
            pltpu.VMEM((count, half), f32),
            pltpu.VMEM((RING, 2 * few, half), f32),
            pltpu.VMEM((RING, 2, 2 * few, half), f32),
            pltpu.VMEM((RING, 2, few, half), f32),
            pltpu.VMEM((2, many, half), f32),
            pltpu.VMEM((few, depth), f32),
            pltpu.VMEM((2, few, depth), f32),
            pltpu.VMEM((2, 2 * few, half), f32),
            pltpu.VMEM((2 * few, half), f32),
            pltpu.VMEM((2 * few, half), f32),
            pltpu.VMEM((2, depth, half), b16),
            pltpu.VMEM((2, depth, half), b16),
            pltpu.VMEM((2, many, half), f32),
            pltpu.VMEM((2, many, half), f32),
            pltpu.VMEM((RING, few, depth), f32),
            pltpu.VMEM((2 * RING, few, depth), f32),
            pltpu.VMEM((2, many, half), f32),
            pltpu.VMEM((count, depth), f32),
            pltpu.VMEM((2, spike_rows, width), b16),
            dma((3,)),
            dma((RING, 2)),
            dma((RING, 2)),
            dma((2, 2)),
            dma((2, 2)),
            pltpu.VMEM((5, depth // 16, half), b16),
            pltpu.SemaphoreType.REGULAR((2,)),
            dma((RING, 5)),
            dma((RING, 5)),
            dma((RING, 5)),
            dma((RING, 5)),
            dma((2, 2)),
            dma((2, 2)),
            dma((2, 2)),
            dma((2, 2)),
            dma((2 * RING - 1,)),
            dma((RING, 2)),
            dma((2,)),
            dma((7,)),
            dma((RING, 2)),
            dma((2 * RING,)),
            dma((2,)),
            dma((2,)),
            pltpu.VMEM((RING, 2, 2 * few, half), f32),
            dma((2,)),
            dma((RING, 2)),
        ],
        compiler_params=pltpu.CompilerParams(
            collective_id=0, has_side_effects=True, vmem_limit_bytes=53 << 20
        ),
    )(band_maps, pltpu.with_memory_space_constraint(right_tips, pltpu.HBM), spikes)
    return right_tips + interface, local_parts - product


def solution(mesh):
    return jax.shard_map(
        on_device,
        mesh=mesh,
        in_specs=(
            P("dom", None, "tip"),
            P("dom", None, "tip"),
            P("dom", "tip", None),
            P("dom", None, "tip"),
        ),
        out_specs=(P("dom", None, "tip"), P("dom", None, "tip")),
        check_vma=False,
    )
```

```python
import functools

import jax
import jax.numpy as jnp
from jax import lax
from jax.experimental import pallas as pl
from jax.experimental.pallas import tpu as pltpu
from jax.sharding import PartitionSpec as P

MESH = pl.DeviceIdType.MESH
RING = 4
CHAIN_ROWS = 2
HELPERS = {
    2: ((14, 3), (1, 2)),
    3: ((15, 4),),
    4: ((13, 4),),
    5: ((12, 3),),
    6: ((10, 2),),
    7: ((11, 2),),
}
PRODUCT_ROW = 4


def split_rows(value):
    high = value.astype(jnp.bfloat16)
    low = value - high.astype(jnp.float32)
    return jnp.concatenate([high.astype(jnp.float32), low], 0).astype(jnp.bfloat16)


def times_map(value, left, right):
    rows = value.shape[0]
    parts = split_rows(value)
    out = [jnp.dot(parts, half, preferred_element_type=jnp.float32) for half in (left, right)]
    return [piece[:rows] + piece[rows:] for piece in out]


def leading_maps(last, maps, tips, tip, high, low, local):
    depth, half = maps.shape[2], maps.shape[3]
    count = local.shape[0]
    local[...] = tips[last, tip]
    block = min(256, half)
    for turn, step in enumerate(range(last - 1, -1, -1)):
        rows = split_rows(jnp.concatenate([tips[step, 0], tips[step, 1]], 1))
        factor = jnp.concatenate([jnp.concatenate([maps[step, 0], maps[step, 1]], 1), rows], 0)
        for start in range(0, half, block):
            columns = slice(start, start + block)
            if turn == 0:
                total = jnp.dot(factor, maps[last, tip, :, columns], preferred_element_type=jnp.float32)
            else:
                total = jnp.dot(factor, high[(turn - 1) % 2, :, columns], preferred_element_type=jnp.float32)
                total += jnp.dot(factor, low[(turn - 1) % 2, :, columns], preferred_element_type=jnp.float32)
            local[:, columns] += total[depth : depth + count] + total[depth + count :]
            total = total[:depth]
            top = total.astype(jnp.bfloat16)
            high[turn % 2, :, columns] = top
            low[turn % 2, :, columns] = (total - top.astype(jnp.float32)).astype(jnp.bfloat16)


def sweep(
    rows_total, maps_hbm, tips_hbm, spikes_hbm, interface_ref, product_ref,
    maps, tips_ref, tips_out, tips_both, tips_few, tips_many, few_in, pair_in, columns_in, columns_out, local,
    high, low, many_in, many_out, states, prior, prior_many, full, spikes,
    local_sem, sib_send, sib_recv, quarter_send, quarter_recv, relay, relay_open, relay_send, relay_recv,
    relay_sib_send, relay_sib_recv,
    link_send, link_recv, fwd_send, opp_recv,
    tip_send, tip_recv, wave_send, wave_recv, home_send, home_recv, side_send, side_recv,
    last_in, last_send, last_recv,
):
    me, tip = lax.axis_index("dom"), lax.axis_index("tip")
    x, row = lax.rem(me, RING), lax.div(me, RING)
    other = 1 - tip
    base = me - x
    depth = maps_hbm.shape[1]
    half = maps_hbm.shape[2]
    cut = depth // 2
    width = spikes_hbm.shape[2] // 2
    chained = row < CHAIN_ROWS
    ringed = row >= CHAIN_ROWS
    def among(rows):
        return functools.reduce(jnp.logical_or, [row == r for r in rows])

    def first_chip(pairs):
        value = pairs[0][1]
        for this, that in pairs[1:]:
            value = jnp.where(row == this, that, value)
        return value * RING

    by_shares, by_part = {}, {}
    for r, helpers in HELPERS.items():
        by_shares.setdefault(tuple(n for _, n in helpers), []).append(r)
        first = 0
        for which, (h, n) in enumerate(helpers):
            by_part.setdefault((first, n, which, h < CHAIN_ROWS), []).append((h, r))
            first += n
    helped = []
    for shares, rows in by_shares.items():
        parts = [
            (sum(shares[:which]), shares[which], first_chip([(r, HELPERS[r][which][0]) for r in rows]))
            for which in range(len(shares))
        ]
        helped.append((among(rows), sum(shares), parts))
    helping = [
        (among([h for h, _ in pairs]), first, n, which, first_chip(pairs), in_chain)
        for (first, n, which, in_chain), pairs in by_part.items()
    ]
    all_helped = among(list(HELPERS))
    all_helping = among([h for helpers in HELPERS.values() for h, _ in helpers])
    unit = maps_hbm.shape[1] // 16
    last_chain = CHAIN_ROWS * RING - 1
    right, left = base + lax.rem(x + 1, RING), base + lax.rem(x + 3, RING)
    opposite = base + lax.rem(x + 2, RING)
    many = full.shape[0] // 2
    few = many // RING

    def remote(src, dst, send, recv, dom, to):
        return pltpu.make_async_remote_copy(
            src_ref=src, dst_ref=dst, send_sem=send, recv_sem=recv, device_id=(dom, to), device_id_type=MESH
        )

    barrier = pltpu.get_barrier_semaphore()

    def greet(dom, to):
        pl.semaphore_signal(barrier, inc=1, device_id=(dom, to), device_id_type=MESH)

    greet(me, other)

    @pl.when(chained)
    def _():
        @pl.when(me > 0)
        def _():
            greet(me - 1, tip)

        @pl.when(me == 1)
        def _():
            greet(0, other)

    @pl.when(ringed)
    def _():
        for step in range(1, RING):
            for to in range(2):
                greet(base + lax.rem(x + step, RING), to)
        before = jnp.where(row == CHAIN_ROWS, last_chain, me - RING)
        greet(before, tip)

        @pl.when(row >= PRODUCT_ROW)
        def _():
            greet(before, other)

        for those, _, parts in helped:
            @pl.when(those)
            def _():
                for _, _, chip in parts:
                    greet(chip + x, tip)

    own_map = pltpu.make_async_copy(maps_hbm.at[0], maps.at[x, tip], local_sem.at[0])
    own_map.start()
    own_columns = pl.ds(pl.multiple_of(tip * width, width), width)
    other_columns = pl.ds(pl.multiple_of(other * width, width), width)
    own_spikes = pltpu.make_async_copy(spikes_hbm.at[0, :, own_columns], spikes.at[tip], local_sem.at[1])
    own_spikes.start()
    own_tips = pltpu.make_async_copy(tips_hbm.at[0], tips_ref, local_sem.at[2])
    own_tips.start()
    asked = jnp.where(all_helping, 1, 0)

    @pl.when(chained)
    def _():
        pl.semaphore_wait(barrier, jnp.where(me == last_chain, 1 + RING, jnp.where(me == 0, 3, 2)) + asked)

    @pl.when(ringed)
    def _():
        after = jnp.where(row == rows_total - 1, 0, jnp.where(row >= PRODUCT_ROW - 1, 2, 1))
        pl.semaphore_wait(barrier, 2 * RING - 1 + after + asked)

    for those, _, _, which, chip, _ in helping:
        @pl.when(those)
        def _():
            pl.semaphore_signal(relay_open.at[which], inc=1, device_id=(chip + x, tip), device_id_type=MESH)

    pieces = [slice(0, cut), slice(cut, depth)]

    def sibling_map_arrives(step, part):
        slot = lax.rem(x + step, RING)
        block = maps.at[slot, other, pieces[part]]
        remote(block, block, sib_send.at[step, part], sib_recv.at[step, part], me, other).wait_recv()

    def own_sibling_map(part):
        src = maps_hbm.at[0, pieces[part]]
        return remote(src, maps.at[x, tip, pieces[part]], sib_send.at[0, part], sib_recv.at[0, part], me, other)

    spikes_out = remote(
        spikes_hbm.at[0, :, other_columns], spikes.at[tip], side_send.at[0], side_recv.at[0], me, other
    )

    def first_rows(to):
        rows = slice(to * many, (to + 1) * many)
        return remote(tips_hbm.at[0, rows, :], many_in.at[tip], wave_send.at[to], wave_recv.at[tip], 1, to)

    def relay_rows(k):
        return slice(depth - (k + 1) * unit, depth - k * unit)

    def to_relay(k, chip):
        src = maps_hbm.at[0, relay_rows(k)]
        return remote(src, relay.at[k], relay_send.at[0, k], relay_recv.at[0, k], chip + x, tip)

    def from_relay(step, k, chip):
        dst = maps.at[x, tip, relay_rows(k)]
        dom = chip + lax.rem(x + step, RING)
        return remote(relay.at[k], dst, relay_send.at[step, k], relay_recv.at[step, k], dom, tip)

    def pass_on(first, n, chip):
        for k in range(first, first + n):
            remote(relay.at[k], relay.at[k], relay_send.at[0, k], relay_recv.at[0, k], me, other).wait_recv()
            for step in range(1, RING):
                from_relay(step, k, chip).start()

    def relay_drain(first, n, chip):
        for k in range(first, first + n):
            for step in range(1, RING):
                from_relay(step, k, chip).wait_send()

    @pl.when(chained)
    def _():
        @pl.when(me == 0)
        def _():
            for to in range(2):
                first_rows(to).start()

        own_tips.wait()
        for part in range(2):
            own_sibling_map(part).start()
        tip_rows = pl.ds(pl.multiple_of(other * many, many), many)
        tips_copy = remote(
            tips_ref.at[tip_rows, :], tips_many.at[tip], tip_send.at[0], tip_recv.at[0, 1], me, other
        )
        tips_copy.start()
        spikes_out.start()
        tips_copy.wait_recv()

        def many_send(h, dom):
            return remote(many_out.at[h], many_in.at[h], wave_send.at[h], wave_recv.at[h], dom, tip)

        own_rows = pl.ds(pl.multiple_of(tip * many, many), many)
        tips_many[tip] = tips_ref[own_rows, :]

        @pl.when(me == 0)
        def _():
            many_in[...] = jnp.zeros_like(many_in)

        for those, first, n, _, chip, in_chain in helping:
            if in_chain:
                @pl.when(those)
                def _():
                    pass_on(first, n, chip)

        total = [None, None]
        for k in range(2):
            @pl.when(me > 0)
            def _():
                remote(many_in.at[k], many_in.at[k], wave_send.at[k], wave_recv.at[k], me, other).wait_recv()

            if k == 0:
                own_map.wait()
            sibling_map_arrives(0, k)
            parts = split_rows(many_in[k])
            for h in range(2):
                term = jnp.dot(parts, maps[x, h, k * half : (k + 1) * half, :], preferred_element_type=jnp.float32)
                total[h] = term if k == 0 else total[h] + term
                if k == 1:
                    fresh = total[h][:many] + total[h][many:] + tips_many[h]
                    many_out[h] = fresh

                    @pl.when(jnp.logical_and(me > 0, me < last_chain))
                    def _():
                        many_send(h, me + 1).start()

        @pl.when(me == last_chain)
        def _():
            for piece in range(RING):
                for h in range(2):
                    states[piece, :, h * half : (h + 1) * half] = many_out[h, piece * few : (piece + 1) * few, :]
            for piece in range(RING):
                remote(
                    states.at[piece], few_in, home_send.at[piece, 0], wave_recv.at[2], last_chain + 1 + piece, tip
                ).start()

        to_sibling = remote(many_in, prior_many, side_send.at[1], side_recv.at[1], me, other)
        to_sibling.start()
        for h in range(2):
            full[own_rows, h * half : (h + 1) * half] = many_in[h]
        to_sibling.wait_recv()
        for h in range(2):
            full[tip_rows, h * half : (h + 1) * half] = prior_many[h]

        for those, first, n, _, chip, in_chain in helping:
            if in_chain:
                @pl.when(those)
                def _():
                    relay_drain(first, n, chip)

        to_sibling.wait_send()
        tips_copy.wait_send()
        for part in range(2):
            own_sibling_map(part).wait_send()

        @pl.when(me == 0)
        def _():
            for to in range(2):
                first_rows(to).wait_send()

        @pl.when(jnp.logical_and(me > 0, me < last_chain))
        def _():
            for h in range(2):
                many_send(h, me + 1).wait_send()

        @pl.when(me == last_chain)
        def _():
            for piece in range(RING):
                remote(
                    states.at[piece], few_in, home_send.at[piece, 0], wave_recv.at[2], last_chain + 1 + piece, tip
                ).wait_send()

    @pl.when(ringed)
    def _():
        class Gather:
            def __init__(self, count):
                self.cut = count // 2

            def rows(self, part, k=None):
                if k is None:
                    return slice(part * self.cut, (part + 1) * self.cut)
                size = self.cut // 2
                return slice(part * self.cut + k * size, part * self.cut + (k + 1) * size)

            def own(self, part, side):
                rows = self.rows(part)
                return remote(
                    maps_hbm.at[0, rows], maps.at[x, tip, rows],
                    link_send.at[side, part], link_recv.at[side, part], right if side == 0 else left, tip,
                )

            def neighbour_arrives(self, part, side):
                block = maps.at[lax.rem(x + (3 if side == 0 else 1), RING), tip, self.rows(part)]
                remote(block, block, link_send.at[side, part], link_recv.at[side, part], right, tip).wait_recv()

            def forward(self, side, k):
                block = maps.at[lax.rem(x + (3 if side == 0 else 1), RING), tip, self.rows(side, k)]
                dom = right if side == 0 else left
                return remote(block, block, fwd_send.at[side, k], opp_recv.at[side, k], dom, tip)

            def opposite_arrives(self, side, k):
                block = maps.at[lax.rem(x + 2, RING), tip, self.rows(side, k)]
                remote(block, block, fwd_send.at[side, k], opp_recv.at[side, k], right, tip).wait_recv()

            def to_sibling(self, step, part):
                block = maps.at[lax.rem(x + step, RING), tip, self.rows(part)]
                return remote(block, block, sib_send.at[step, part], sib_recv.at[step, part], me, other)

            def sibling_arrives(self, step, part):
                block = maps.at[lax.rem(x + step, RING), other, self.rows(part)]
                remote(block, block, sib_send.at[step, part], sib_recv.at[step, part], me, other).wait_recv()

            def quarter_to_sibling(self, side, k):
                block = maps.at[lax.rem(x + 2, RING), tip, self.rows(side, k)]
                return remote(block, block, quarter_send.at[side, k], quarter_recv.at[side, k], me, other)

            def sibling_quarter_arrives(self, side, k):
                block = maps.at[lax.rem(x + 2, RING), other, self.rows(side, k)]
                remote(block, block, quarter_send.at[side, k], quarter_recv.at[side, k], me, other).wait_recv()

            def start(self, which=(0, 1)):
                for turn in which:
                    for part, side in (((0, 0), (1, 1)), ((1, 0), (0, 1)))[turn]:
                        self.own(part, side).start()

            def middle(self):
                for part, side in ((0, 0), (1, 1)):
                    self.neighbour_arrives(part, side)
                    for k in range(2):
                        self.forward(side, k).start()
                    self.to_sibling(3 if side == 0 else 1, part).start()
                for part, side in ((1, 0), (0, 1)):
                    self.neighbour_arrives(part, side)
                    self.to_sibling(3 if side == 0 else 1, part).start()

            def last(self):
                for k in range(2):
                    for side in range(2):
                        self.opposite_arrives(side, k)
                        self.quarter_to_sibling(side, k).start()
                for step in (1, 3):
                    for part in range(2):
                        self.sibling_arrives(step, part)
                for k in range(2):
                    for side in range(2):
                        self.sibling_quarter_arrives(side, k)

            def drain(self):
                for part in range(2):
                    for side in range(2):
                        self.own(part, side).wait_send()
                    for k in range(2):
                        self.forward(part, k).wait_send()
                        self.quarter_to_sibling(part, k).wait_send()
                    for step in (1, 3):
                        self.to_sibling(step, part).wait_send()

        whole = Gather(depth)
        gathers = [Gather(depth - count * unit) for _, count, _ in helped]

        def relayed_to_sibling(step, k):
            block = maps.at[lax.rem(x + RING - step, RING), tip, relay_rows(k)]
            return remote(block, block, relay_sib_send.at[step, k], relay_sib_recv.at[step, k], me, other)

        for (those, _, _), gather in zip(helped, gathers):
            @pl.when(those)
            def _():
                gather.start()

        @pl.when(jnp.logical_not(jnp.logical_or(all_helped, all_helping)))
        def _():
            whole.start()

        for those, _, n, _, _, in_chain in helping:
            if not in_chain and n < 3:
                @pl.when(those)
                def _():
                    whole.start((0,))

        own_tips.wait()
        for piece in range(RING):
            for to in range(2):
                start = to * many + piece * few
                tips_out[piece, to * few : (to + 1) * few, :] = tips_ref[start : start + few, :]

        def tip_copy(step, to, number):
            dst_x = lax.rem(x + step, RING)
            return remote(
                tips_out.at[dst_x], tips_both.at[x, tip],
                tip_send.at[number], tip_recv.at[step, jnp.where(to == tip, 0, 1)], base + dst_x, to,
            )

        partners = [(0, other), (1, tip), (1, other), (2, tip), (2, other), (3, tip), (3, other)]
        for number, (step, to) in enumerate(partners):
            tip_copy(step, to, number).start()
        tips_both[x, tip] = tips_out[x]

        for those, _, parts in helped:
            @pl.when(those)
            def _():
                for which, (first, n, chip) in reversed(list(enumerate(parts))):
                    pl.semaphore_wait(relay_open.at[which], 1)
                    for k in range(first, first + n):
                        to_relay(k, chip).start()

        for those, first, n, _, chip, in_chain in helping:
            if not in_chain:
                @pl.when(those)
                def _():
                    pass_on(first, n, chip)
                    whole.start((1,) if n < 3 else (0, 1))

        for part in range(2):
            own_sibling_map(part).start()
        spikes_out.start()

        @pl.when(jnp.logical_not(all_helped))
        def _():
            whole.middle()
            whole.last()

        for (those, count, _), gather in zip(helped, gathers):
            @pl.when(those)
            def _():
                gather.middle()
                for k in range(count):
                    for step in range(1, RING):
                        block = maps.at[lax.rem(x + RING - step, RING), tip, relay_rows(k)]
                        remote(block, block, relay_send.at[step, k], relay_recv.at[step, k], me, other).wait_recv()
                        relayed_to_sibling(step, k).start()
                gather.last()
                for k in range(count):
                    for step in range(1, RING):
                        block = maps.at[lax.rem(x + RING - step, RING), other, relay_rows(k)]
                        remote(
                            block, block, relay_sib_send.at[step, k], relay_sib_recv.at[step, k], me, other
                        ).wait_recv()

        own_map.wait()
        for part in range(2):
            sibling_map_arrives(0, part)
        for step, to in partners:
            remote(
                tips_both.at[0, 0], tips_both.at[0, 0], tip_send.at[0],
                tip_recv.at[step, jnp.where(to == tip, 0, 1)], me, other,
            ).wait_recv()

        mine = tip * RING + x

        def home_copy(step, to):
            src = few_in if step == 0 else states.at[step - 1]
            return remote(src, prior.at[mine], home_send.at[step, to], home_recv.at[mine], base + step, to)

        def send_home(step):
            for to in range(2):
                @pl.when(jnp.logical_or(x != step, tip != to))
                def _():
                    home_copy(step, to).start()

            @pl.when(x == step)
            def _():
                prior[mine] = few_in[...] if step == 0 else states[step - 1]

        def next_state(step, state):
            fresh = times_map(state, maps[step, 0], maps[step, 1])
            for h in range(2):
                states[step, :, h * half : (h + 1) * half] = fresh[h] + tips_few[step, h]
            return states[step]

        def own_of(pair):
            return jnp.where(tip == 0, pair[:few], pair[few:])

        for step in range(RING):
            for h in range(2):
                tips_few[step, h] = own_of(tips_both[step, h])

        final_row = row == rows_total - 1
        to_the_end = jnp.logical_and(final_row, x == RING - 1)

        def to_last(to):
            dom = base + RING - 1
            return remote(columns_out, last_in.at[x, tip], last_send.at[to], last_recv.at[x, tip], dom, to)
        direct = row < PRODUCT_ROW

        def onward_rows(to):
            return remote(states.at[RING - 1], few_in, wave_send.at[to], wave_recv.at[2], me + RING, tip)

        def onward_pair(to):
            return remote(
                states.at[RING - 1], pair_in.at[tip], wave_send.at[to], wave_recv.at[3 + tip], me + RING, to
            )

        def onward_columns(to):
            return remote(columns_out, columns_in.at[tip], wave_send.at[to], wave_recv.at[5 + tip], me + RING, to)

        @pl.when(direct)
        def _():
            remote(few_in, few_in, wave_send.at[0], wave_recv.at[2], me, other).wait_recv()
            state = few_in[...]
            for step in range(RING):
                state = next_state(step, state)

            @pl.when(row < PRODUCT_ROW - 1)
            def _():
                onward_rows(0).start()

            @pl.when(jnp.logical_and(row == PRODUCT_ROW - 1, jnp.logical_not(final_row)))
            def _():
                for to in range(2):
                    onward_pair(to).start()

            for step in range(RING):
                send_home(step)

        @pl.when(jnp.logical_not(direct))
        def _():
            def prepare(last):
                leading_maps(last, maps, tips_both, tip, high, low, local)

            def start_state():
                for h in range(2):
                    few_in[:, h * half : (h + 1) * half] = own_of(columns_in[h])
                send_home(0)

            def product_step(last):
                slot = (last - 1) % 2
                parts = split_rows(jnp.concatenate([columns_in[0], columns_in[1]], 1))
                fresh = jnp.dot(parts, high[slot], preferred_element_type=jnp.float32)
                fresh = fresh + jnp.dot(parts, low[slot], preferred_element_type=jnp.float32)
                columns_out[...] = fresh[: 2 * few] + fresh[2 * few :] + local[...]

            @pl.when(jnp.logical_not(final_row))
            def _():
                prepare(RING - 1)

            @pl.when(final_row)
            def _():
                prepare(RING - 2)

            @pl.when(row == PRODUCT_ROW)
            def _():
                for core in range(2):
                    remote(
                        pair_in.at[core], pair_in.at[core], wave_send.at[0], wave_recv.at[3 + core], me, other
                    ).wait_recv()
                for core in range(2):
                    for h in range(2):
                        columns_in[h, core * few : (core + 1) * few, :] = pair_in[core, :, h * half : (h + 1) * half]

            def columns_arrive(core):
                remote(
                    columns_in.at[core], columns_in.at[core], wave_send.at[0], wave_recv.at[5 + core], me, other
                ).wait_recv()

            @pl.when(row > PRODUCT_ROW)
            def _():
                for core in range(2):
                    columns_arrive(core)

            @pl.when(jnp.logical_not(final_row))
            def _():
                product_step(RING - 1)
                for to in range(2):
                    onward_columns(to).start()

            @pl.when(final_row)
            def _():
                start_state()
                product_step(RING - 2)
                for to in range(2):
                    @pl.when(jnp.logical_or(x != RING - 1, tip != to))
                    def _():
                        to_last(to).start()

                @pl.when(x == RING - 1)
                def _():
                    last_in[x, tip] = columns_out[...]

            @pl.when(jnp.logical_not(final_row))
            def _():
                start_state()

            state = few_in[...]
            for step in range(RING - 2):
                state = next_state(step, state)
                send_home(step + 1)

            @pl.when(jnp.logical_not(final_row))
            def _():
                next_state(RING - 2, state)
                send_home(RING - 1)

        @pl.when(to_the_end)
        def _():
            for chip in range(RING):
                for core in range(2):
                    @pl.when(jnp.logical_or(chip != x, core != tip))
                    def _():
                        block = last_in.at[chip, core]
                        remote(block, block, last_send.at[0], last_recv.at[chip, core], me, other).wait_recv()
            for chip in range(RING):
                for core in range(2):
                    columns = slice(core * half, (core + 1) * half)
                    for group in range(2):
                        start = group * many + chip * few
                        block = last_in[chip, core, group * few : (group + 1) * few, :]
                        full[start : start + few, columns] = block

        @pl.when(jnp.logical_not(to_the_end))
        def _():
            for piece in range(2 * RING):
                @pl.when(piece != mine)
                def _():
                    remote(
                        prior.at[piece], prior.at[piece], home_send.at[0, 0], home_recv.at[piece], me, other
                    ).wait_recv()
            for piece in range(2 * RING):
                full[piece * few : (piece + 1) * few, :] = prior[piece]

        @pl.when(jnp.logical_not(all_helped))
        def _():
            whole.drain()

        for those, first, n, _, chip, in_chain in helping:
            if not in_chain:
                @pl.when(those)
                def _():
                    relay_drain(first, n, chip)

        for (those, _, parts), gather in zip(helped, gathers):
            @pl.when(those)
            def _():
                gather.drain()
                for first, n, chip in parts:
                    for k in range(first, first + n):
                        to_relay(k, chip).wait_send()
                        for step in range(1, RING):
                            relayed_to_sibling(step, k).wait_send()

        for part in range(2):
            own_sibling_map(part).wait_send()
        for number, (step, to) in enumerate(partners):
            tip_copy(step, to, number).wait_send()

        @pl.when(row < PRODUCT_ROW - 1)
        def _():
            onward_rows(0).wait_send()

        @pl.when(jnp.logical_and(row == PRODUCT_ROW - 1, jnp.logical_not(final_row)))
        def _():
            for to in range(2):
                onward_pair(to).wait_send()

        @pl.when(jnp.logical_and(row >= PRODUCT_ROW, jnp.logical_not(final_row)))
        def _():
            for to in range(2):
                onward_columns(to).wait_send()

        for step in range(RING - 1):
            for to in range(2):
                @pl.when(jnp.logical_or(x != step, tip != to))
                def _():
                    home_copy(step, to).wait_send()

        for to in range(2):
            @pl.when(jnp.logical_or(x != RING - 1, tip != to))
            def _():
                @pl.when(final_row)
                def _():
                    to_last(to).wait_send()

                @pl.when(jnp.logical_not(final_row))
                def _():
                    home_copy(RING - 1, to).wait_send()

    own_spikes.wait()
    spikes_out.wait()
    count = full.shape[0]
    parts = split_rows(full[...])
    fresh = jnp.dot(parts, maps[x, tip], preferred_element_type=jnp.float32)
    interface_ref[0] = fresh[:count] + fresh[count:]
    middle = spikes.shape[1]
    product = jnp.dot(parts[:count, :middle], spikes[0], preferred_element_type=jnp.float32)
    product_ref[0] = product + jnp.dot(parts[:count, middle:], spikes[1], preferred_element_type=jnp.float32)


def on_device(band_maps, right_tips, spikes, local_parts):
    rows_total = lax.axis_size("dom") // RING
    _, depth, half = band_maps.shape
    count = right_tips.shape[1]
    many = count // 2
    few = many // RING
    _, spike_rows, spike_columns = spikes.shape
    width = spike_columns // 2
    f32, b16, dma = jnp.float32, jnp.bfloat16, pltpu.SemaphoreType.DMA
    interface, product = pl.pallas_call(
        functools.partial(sweep, rows_total),
        out_shape=(
            jax.ShapeDtypeStruct((1, count, half), f32),
            jax.ShapeDtypeStruct((1, count, width), f32),
        ),
        in_specs=[
            pl.BlockSpec(memory_space=pltpu.HBM),
            pl.BlockSpec(memory_space=pltpu.HBM),
            pl.BlockSpec(memory_space=pltpu.HBM),
        ],
        out_specs=(pl.BlockSpec(memory_space=pltpu.VMEM),) * 2,
        scratch_shapes=[
            pltpu.VMEM((RING, 2, depth, half), b16),
            pltpu.VMEM((count, half), f32),
            pltpu.VMEM((RING, 2 * few, half), f32),
            pltpu.VMEM((RING, 2, 2 * few, half), f32),
            pltpu.VMEM((RING, 2, few, half), f32),
            pltpu.VMEM((2, many, half), f32),
            pltpu.VMEM((few, depth), f32),
            pltpu.VMEM((2, few, depth), f32),
            pltpu.VMEM((2, 2 * few, half), f32),
            pltpu.VMEM((2 * few, half), f32),
            pltpu.VMEM((2 * few, half), f32),
            pltpu.VMEM((2, depth, half), b16),
            pltpu.VMEM((2, depth, half), b16),
            pltpu.VMEM((2, many, half), f32),
            pltpu.VMEM((2, many, half), f32),
            pltpu.VMEM((RING, few, depth), f32),
            pltpu.VMEM((2 * RING, few, depth), f32),
            pltpu.VMEM((2, many, half), f32),
            pltpu.VMEM((count, depth), f32),
            pltpu.VMEM((2, spike_rows, width), b16),
            dma((3,)),
            dma((RING, 2)),
            dma((RING, 2)),
            dma((2, 2)),
            dma((2, 2)),
            pltpu.VMEM((5, depth // 16, half), b16),
            pltpu.SemaphoreType.REGULAR((2,)),
            dma((RING, 5)),
            dma((RING, 5)),
            dma((RING, 5)),
            dma((RING, 5)),
            dma((2, 2)),
            dma((2, 2)),
            dma((2, 2)),
            dma((2, 2)),
            dma((2 * RING - 1,)),
            dma((RING, 2)),
            dma((2,)),
            dma((7,)),
            dma((RING, 2)),
            dma((2 * RING,)),
            dma((2,)),
            dma((2,)),
            pltpu.VMEM((RING, 2, 2 * few, half), f32),
            dma((2,)),
            dma((RING, 2)),
        ],
        compiler_params=pltpu.CompilerParams(
            collective_id=0, has_side_effects=True, vmem_limit_bytes=53 << 20
        ),
    )(band_maps, pltpu.with_memory_space_constraint(right_tips, pltpu.HBM), spikes)
    return right_tips + interface, local_parts - product


def solution(mesh):
    return jax.shard_map(
        on_device,
        mesh=mesh,
        in_specs=(
            P("dom", None, "tip"),
            P("dom", None, "tip"),
            P("dom", "tip", None),
            P("dom", None, "tip"),
        ),
        out_specs=(P("dom", None, "tip"), P("dom", None, "tip")),
        check_vma=False,
    )
```

```python
import functools

import jax
import jax.numpy as jnp
from jax import lax
from jax.experimental import pallas as pl
from jax.experimental.pallas import tpu as pltpu
from jax.sharding import PartitionSpec as P

MESH = pl.DeviceIdType.MESH
RING = 4
CHAIN_ROWS = 2
HELPERS = {
    2: ((14, 3), (1, 2)),
    3: ((15, 4),),
    4: ((13, 4),),
    5: ((12, 3),),
    6: ((10, 2),),
    7: ((11, 2),),
}
PRODUCT_ROW = 4


def split_rows(value):
    high = value.astype(jnp.bfloat16)
    low = value - high.astype(jnp.float32)
    return jnp.concatenate([high.astype(jnp.float32), low], 0).astype(jnp.bfloat16)


def times_map(value, left, right):
    rows = value.shape[0]
    parts = split_rows(value)
    out = [jnp.dot(parts, half, preferred_element_type=jnp.float32) for half in (left, right)]
    return [piece[:rows] + piece[rows:] for piece in out]


def leading_maps(last, maps, tips, tip, high, low, local):
    depth, half = maps.shape[2], maps.shape[3]
    count = local.shape[0]
    local[...] = tips[last, tip]
    block = min(256, half)
    for turn, step in enumerate(range(last - 1, -1, -1)):
        rows = split_rows(jnp.concatenate([tips[step, 0], tips[step, 1]], 1))
        factor = jnp.concatenate([jnp.concatenate([maps[step, 0], maps[step, 1]], 1), rows], 0)
        for start in range(0, half, block):
            columns = slice(start, start + block)
            if turn == 0:
                total = jnp.dot(factor, maps[last, tip, :, columns], preferred_element_type=jnp.float32)
            else:
                total = jnp.dot(factor, high[(turn - 1) % 2, :, columns], preferred_element_type=jnp.float32)
                total += jnp.dot(factor, low[(turn - 1) % 2, :, columns], preferred_element_type=jnp.float32)
            local[:, columns] += total[depth : depth + count] + total[depth + count :]
            total = total[:depth]
            top = total.astype(jnp.bfloat16)
            high[turn % 2, :, columns] = top
            low[turn % 2, :, columns] = (total - top.astype(jnp.float32)).astype(jnp.bfloat16)


def sweep(
    rows_total, maps_hbm, tips_hbm, spikes_hbm, interface_ref, product_ref,
    maps, tips_ref, tips_out, tips_both, tips_few, tips_many, few_in, pair_in, columns_in, columns_out, local,
    high, low, many_in, many_out, states, prior, prior_many, full, spikes,
    local_sem, sib_send, sib_recv, quarter_send, quarter_recv, relay, relay_open, relay_send, relay_recv,
    relay_sib_send, relay_sib_recv,
    link_send, link_recv, fwd_send, opp_recv,
    tip_send, tip_recv, wave_send, wave_recv, home_send, home_recv, side_send, side_recv,
    last_in, last_send, last_recv,
):
    me, tip = lax.axis_index("dom"), lax.axis_index("tip")
    x, row = lax.rem(me, RING), lax.div(me, RING)
    other = 1 - tip
    base = me - x
    depth = maps_hbm.shape[1]
    half = maps_hbm.shape[2]
    cut = depth // 2
    width = spikes_hbm.shape[2] // 2
    chained = row < CHAIN_ROWS
    ringed = row >= CHAIN_ROWS
    def among(rows):
        return functools.reduce(jnp.logical_or, [row == r for r in rows])

    def first_chip(pairs):
        value = pairs[0][1]
        for this, that in pairs[1:]:
            value = jnp.where(row == this, that, value)
        return value * RING

    by_shares, by_part = {}, {}
    for r, helpers in HELPERS.items():
        by_shares.setdefault(tuple(n for _, n in helpers), []).append(r)
        first = 0
        for which, (h, n) in enumerate(helpers):
            by_part.setdefault((first, n, which, h < CHAIN_ROWS), []).append((h, r))
            first += n
    helped = []
    for shares, rows in by_shares.items():
        parts = [
            (sum(shares[:which]), shares[which], first_chip([(r, HELPERS[r][which][0]) for r in rows]))
            for which in range(len(shares))
        ]
        helped.append((among(rows), sum(shares), parts))
    helping = [
        (among([h for h, _ in pairs]), first, n, which, first_chip(pairs), in_chain)
        for (first, n, which, in_chain), pairs in by_part.items()
    ]
    all_helped = among(list(HELPERS))
    all_helping = among([h for helpers in HELPERS.values() for h, _ in helpers])
    unit = maps_hbm.shape[1] // 16
    last_chain = CHAIN_ROWS * RING - 1
    right, left = base + lax.rem(x + 1, RING), base + lax.rem(x + 3, RING)
    opposite = base + lax.rem(x + 2, RING)
    many = full.shape[0] // 2
    few = many // RING

    def remote(src, dst, send, recv, dom, to):
        return pltpu.make_async_remote_copy(
            src_ref=src, dst_ref=dst, send_sem=send, recv_sem=recv, device_id=(dom, to), device_id_type=MESH
        )

    barrier = pltpu.get_barrier_semaphore()

    def greet(dom, to):
        pl.semaphore_signal(barrier, inc=1, device_id=(dom, to), device_id_type=MESH)

    greet(me, other)

    @pl.when(chained)
    def _():
        @pl.when(me > 0)
        def _():
            greet(me - 1, tip)

        @pl.when(me == 1)
        def _():
            greet(0, other)

    @pl.when(ringed)
    def _():
        for step in range(1, RING):
            for to in range(2):
                greet(base + lax.rem(x + step, RING), to)
        before = jnp.where(row == CHAIN_ROWS, last_chain, me - RING)
        greet(before, tip)

        @pl.when(row >= PRODUCT_ROW)
        def _():
            greet(before, other)

        for those, _, parts in helped:
            @pl.when(those)
            def _():
                for _, _, chip in parts:
                    greet(chip + x, tip)

    own_map = pltpu.make_async_copy(maps_hbm.at[0], maps.at[x, tip], local_sem.at[0])
    own_map.start()
    own_columns = pl.ds(pl.multiple_of(tip * width, width), width)
    other_columns = pl.ds(pl.multiple_of(other * width, width), width)
    own_spikes = pltpu.make_async_copy(spikes_hbm.at[0, :, own_columns], spikes.at[tip], local_sem.at[1])
    own_spikes.start()
    own_tips = pltpu.make_async_copy(tips_hbm.at[0], tips_ref, local_sem.at[2])
    own_tips.start()
    asked = jnp.where(all_helping, 1, 0)

    @pl.when(chained)
    def _():
        pl.semaphore_wait(barrier, jnp.where(me == last_chain, 1 + RING, jnp.where(me == 0, 3, 2)) + asked)

    @pl.when(ringed)
    def _():
        after = jnp.where(row == rows_total - 1, 0, jnp.where(row >= PRODUCT_ROW - 1, 2, 1))
        pl.semaphore_wait(barrier, 2 * RING - 1 + after + asked)

    for those, _, _, which, chip, _ in helping:
        @pl.when(those)
        def _():
            pl.semaphore_signal(relay_open.at[which], inc=1, device_id=(chip + x, tip), device_id_type=MESH)

    pieces = [slice(0, cut), slice(cut, depth)]

    def sibling_map_arrives(step, part):
        slot = lax.rem(x + step, RING)
        block = maps.at[slot, other, pieces[part]]
        remote(block, block, sib_send.at[step, part], sib_recv.at[step, part], me, other).wait_recv()

    def own_sibling_map(part):
        src = maps_hbm.at[0, pieces[part]]
        return remote(src, maps.at[x, tip, pieces[part]], sib_send.at[0, part], sib_recv.at[0, part], me, other)

    spikes_out = remote(
        spikes_hbm.at[0, :, other_columns], spikes.at[tip], side_send.at[0], side_recv.at[0], me, other
    )

    def first_rows(to):
        rows = slice(to * many, (to + 1) * many)
        return remote(tips_hbm.at[0, rows, :], many_in.at[tip], wave_send.at[to], wave_recv.at[tip], 1, to)

    def relay_rows(k):
        return slice(depth - (k + 1) * unit, depth - k * unit)

    def to_relay(k, chip):
        src = maps_hbm.at[0, relay_rows(k)]
        return remote(src, relay.at[k], relay_send.at[0, k], relay_recv.at[0, k], chip + x, tip)

    def from_relay(step, k, chip):
        dst = maps.at[x, tip, relay_rows(k)]
        dom = chip + lax.rem(x + step, RING)
        return remote(relay.at[k], dst, relay_send.at[step, k], relay_recv.at[step, k], dom, tip)

    def pass_on(first, n, chip):
        for k in range(first, first + n):
            remote(relay.at[k], relay.at[k], relay_send.at[0, k], relay_recv.at[0, k], me, other).wait_recv()
            for step in range(1, RING):
                from_relay(step, k, chip).start()

    def relay_drain(first, n, chip):
        for k in range(first, first + n):
            for step in range(1, RING):
                from_relay(step, k, chip).wait_send()

    @pl.when(chained)
    def _():
        @pl.when(me == 0)
        def _():
            for to in range(2):
                first_rows(to).start()

        own_tips.wait()
        for part in range(2):
            own_sibling_map(part).start()
        tip_rows = pl.ds(pl.multiple_of(other * many, many), many)
        tips_copy = remote(
            tips_ref.at[tip_rows, :], tips_many.at[tip], tip_send.at[0], tip_recv.at[0, 1], me, other
        )
        tips_copy.start()
        spikes_out.start()
        tips_copy.wait_recv()

        def many_send(h, dom):
            return remote(many_out.at[h], many_in.at[h], wave_send.at[h], wave_recv.at[h], dom, tip)

        own_rows = pl.ds(pl.multiple_of(tip * many, many), many)
        tips_many[tip] = tips_ref[own_rows, :]

        @pl.when(me == 0)
        def _():
            many_in[...] = jnp.zeros_like(many_in)

        for those, first, n, _, chip, in_chain in helping:
            if in_chain:
                @pl.when(those)
                def _():
                    pass_on(first, n, chip)

        total = [None, None]
        for k in range(2):
            @pl.when(me > 0)
            def _():
                remote(many_in.at[k], many_in.at[k], wave_send.at[k], wave_recv.at[k], me, other).wait_recv()

            if k == 0:
                own_map.wait()
            sibling_map_arrives(0, k)
            parts = split_rows(many_in[k])
            for h in range(2):
                term = jnp.dot(parts, maps[x, h, k * half : (k + 1) * half, :], preferred_element_type=jnp.float32)
                total[h] = term if k == 0 else total[h] + term
                if k == 1:
                    fresh = total[h][:many] + total[h][many:] + tips_many[h]
                    many_out[h] = fresh

                    @pl.when(jnp.logical_and(me > 0, me < last_chain))
                    def _():
                        many_send(h, me + 1).start()

        @pl.when(me == last_chain)
        def _():
            for piece in range(RING):
                for h in range(2):
                    states[piece, :, h * half : (h + 1) * half] = many_out[h, piece * few : (piece + 1) * few, :]
            for piece in range(RING):
                remote(
                    states.at[piece], few_in, home_send.at[piece, 0], wave_recv.at[2], last_chain + 1 + piece, tip
                ).start()

        to_sibling = remote(many_in, prior_many, side_send.at[1], side_recv.at[1], me, other)
        to_sibling.start()
        for h in range(2):
            full[own_rows, h * half : (h + 1) * half] = many_in[h]
        to_sibling.wait_recv()
        for h in range(2):
            full[tip_rows, h * half : (h + 1) * half] = prior_many[h]

        for those, first, n, _, chip, in_chain in helping:
            if in_chain:
                @pl.when(those)
                def _():
                    relay_drain(first, n, chip)

        to_sibling.wait_send()
        tips_copy.wait_send()
        for part in range(2):
            own_sibling_map(part).wait_send()

        @pl.when(me == 0)
        def _():
            for to in range(2):
                first_rows(to).wait_send()

        @pl.when(jnp.logical_and(me > 0, me < last_chain))
        def _():
            for h in range(2):
                many_send(h, me + 1).wait_send()

        @pl.when(me == last_chain)
        def _():
            for piece in range(RING):
                remote(
                    states.at[piece], few_in, home_send.at[piece, 0], wave_recv.at[2], last_chain + 1 + piece, tip
                ).wait_send()

    @pl.when(ringed)
    def _():
        class Gather:
            def __init__(self, count):
                self.cut = count // 2

            def rows(self, part, k=None):
                if k is None:
                    return slice(part * self.cut, (part + 1) * self.cut)
                size = self.cut // 2
                return slice(part * self.cut + k * size, part * self.cut + (k + 1) * size)

            def own(self, part, side):
                rows = self.rows(part)
                return remote(
                    maps_hbm.at[0, rows], maps.at[x, tip, rows],
                    link_send.at[side, part], link_recv.at[side, part], right if side == 0 else left, tip,
                )

            def neighbour_arrives(self, part, side):
                block = maps.at[lax.rem(x + (3 if side == 0 else 1), RING), tip, self.rows(part)]
                remote(block, block, link_send.at[side, part], link_recv.at[side, part], right, tip).wait_recv()

            def forward(self, side, k):
                block = maps.at[lax.rem(x + (3 if side == 0 else 1), RING), tip, self.rows(side, k)]
                dom = right if side == 0 else left
                return remote(block, block, fwd_send.at[side, k], opp_recv.at[side, k], dom, tip)

            def opposite_arrives(self, side, k):
                block = maps.at[lax.rem(x + 2, RING), tip, self.rows(side, k)]
                remote(block, block, fwd_send.at[side, k], opp_recv.at[side, k], right, tip).wait_recv()

            def to_sibling(self, step, part):
                block = maps.at[lax.rem(x + step, RING), tip, self.rows(part)]
                return remote(block, block, sib_send.at[step, part], sib_recv.at[step, part], me, other)

            def sibling_arrives(self, step, part):
                block = maps.at[lax.rem(x + step, RING), other, self.rows(part)]
                remote(block, block, sib_send.at[step, part], sib_recv.at[step, part], me, other).wait_recv()

            def quarter_to_sibling(self, side, k):
                block = maps.at[lax.rem(x + 2, RING), tip, self.rows(side, k)]
                return remote(block, block, quarter_send.at[side, k], quarter_recv.at[side, k], me, other)

            def sibling_quarter_arrives(self, side, k):
                block = maps.at[lax.rem(x + 2, RING), other, self.rows(side, k)]
                remote(block, block, quarter_send.at[side, k], quarter_recv.at[side, k], me, other).wait_recv()

            def start(self, which=(0, 1)):
                for turn in which:
                    for part, side in (((0, 0), (1, 1)), ((1, 0), (0, 1)))[turn]:
                        self.own(part, side).start()

            def middle(self):
                for part, side in ((0, 0), (1, 1)):
                    self.neighbour_arrives(part, side)
                    for k in range(2):
                        self.forward(side, k).start()
                    self.to_sibling(3 if side == 0 else 1, part).start()
                for part, side in ((1, 0), (0, 1)):
                    self.neighbour_arrives(part, side)
                    self.to_sibling(3 if side == 0 else 1, part).start()

            def last(self):
                for k in range(2):
                    for side in range(2):
                        self.opposite_arrives(side, k)
                        self.quarter_to_sibling(side, k).start()
                for step in (1, 3):
                    for part in range(2):
                        self.sibling_arrives(step, part)
                for k in range(2):
                    for side in range(2):
                        self.sibling_quarter_arrives(side, k)

            def drain(self):
                for part in range(2):
                    for side in range(2):
                        self.own(part, side).wait_send()
                    for k in range(2):
                        self.forward(part, k).wait_send()
                        self.quarter_to_sibling(part, k).wait_send()
                    for step in (1, 3):
                        self.to_sibling(step, part).wait_send()

        whole = Gather(depth)
        gathers = [Gather(depth - count * unit) for _, count, _ in helped]

        def relayed_to_sibling(step, k):
            block = maps.at[lax.rem(x + RING - step, RING), tip, relay_rows(k)]
            return remote(block, block, relay_sib_send.at[step, k], relay_sib_recv.at[step, k], me, other)

        for (those, _, _), gather in zip(helped, gathers):
            @pl.when(those)
            def _():
                gather.start()

        @pl.when(jnp.logical_not(jnp.logical_or(all_helped, all_helping)))
        def _():
            whole.start()

        for those, _, n, _, _, in_chain in helping:
            if not in_chain and n < 3:
                @pl.when(those)
                def _():
                    whole.start((0,))

        own_tips.wait()
        for piece in range(RING):
            for to in range(2):
                start = to * many + piece * few
                tips_out[piece, to * few : (to + 1) * few, :] = tips_ref[start : start + few, :]

        def tip_copy(step, to, number):
            dst_x = lax.rem(x + step, RING)
            return remote(
                tips_out.at[dst_x], tips_both.at[x, tip],
                tip_send.at[number], tip_recv.at[step, jnp.where(to == tip, 0, 1)], base + dst_x, to,
            )

        partners = [(0, other), (1, tip), (1, other), (2, tip), (2, other), (3, tip), (3, other)]
        for number, (step, to) in enumerate(partners):
            tip_copy(step, to, number).start()
        tips_both[x, tip] = tips_out[x]

        for those, _, parts in helped:
            @pl.when(those)
            def _():
                for which, (first, n, chip) in reversed(list(enumerate(parts))):
                    pl.semaphore_wait(relay_open.at[which], 1)
                    for k in range(first, first + n):
                        to_relay(k, chip).start()

        for those, first, n, _, chip, in_chain in helping:
            if not in_chain:
                @pl.when(those)
                def _():
                    pass_on(first, n, chip)
                    whole.start((1,) if n < 3 else (0, 1))

        for part in range(2):
            own_sibling_map(part).start()
        spikes_out.start()

        @pl.when(jnp.logical_not(all_helped))
        def _():
            whole.middle()
            whole.last()

        for (those, count, _), gather in zip(helped, gathers):
            @pl.when(those)
            def _():
                gather.middle()
                for k in range(count):
                    for step in range(1, RING):
                        block = maps.at[lax.rem(x + RING - step, RING), tip, relay_rows(k)]
                        remote(block, block, relay_send.at[step, k], relay_recv.at[step, k], me, other).wait_recv()
                        relayed_to_sibling(step, k).start()
                gather.last()
                for k in range(count):
                    for step in range(1, RING):
                        block = maps.at[lax.rem(x + RING - step, RING), other, relay_rows(k)]
                        remote(
                            block, block, relay_sib_send.at[step, k], relay_sib_recv.at[step, k], me, other
                        ).wait_recv()

        own_map.wait()
        for part in range(2):
            sibling_map_arrives(0, part)
        for step, to in partners:
            remote(
                tips_both.at[0, 0], tips_both.at[0, 0], tip_send.at[0],
                tip_recv.at[step, jnp.where(to == tip, 0, 1)], me, other,
            ).wait_recv()

        mine = tip * RING + x

        def home_copy(step, to):
            src = few_in if step == 0 else states.at[step - 1]
            return remote(src, prior.at[mine], home_send.at[step, to], home_recv.at[mine], base + step, to)

        def send_home(step):
            for to in (tip, other):
                @pl.when(jnp.logical_or(x != step, tip != to))
                def _():
                    home_copy(step, to).start()

            @pl.when(x == step)
            def _():
                prior[mine] = few_in[...] if step == 0 else states[step - 1]

        def next_state(step, state):
            fresh = times_map(state, maps[step, 0], maps[step, 1])
            for h in range(2):
                states[step, :, h * half : (h + 1) * half] = fresh[h] + tips_few[step, h]
            return states[step]

        def own_of(pair):
            return jnp.where(tip == 0, pair[:few], pair[few:])

        for step in range(RING):
            for h in range(2):
                tips_few[step, h] = own_of(tips_both[step, h])

        final_row = row == rows_total - 1
        to_the_end = jnp.logical_and(final_row, x == RING - 1)

        def to_last(to):
            dom = base + RING - 1
            return remote(columns_out, last_in.at[x, tip], last_send.at[to], last_recv.at[x, tip], dom, to)
        direct = row < PRODUCT_ROW

        def onward_rows(to):
            return remote(states.at[RING - 1], few_in, wave_send.at[to], wave_recv.at[2], me + RING, tip)

        def onward_pair(to):
            return remote(
                states.at[RING - 1], pair_in.at[tip], wave_send.at[to], wave_recv.at[3 + tip], me + RING, to
            )

        def onward_columns(to):
            return remote(columns_out, columns_in.at[tip], wave_send.at[to], wave_recv.at[5 + tip], me + RING, to)

        @pl.when(direct)
        def _():
            remote(few_in, few_in, wave_send.at[0], wave_recv.at[2], me, other).wait_recv()
            state = few_in[...]
            for step in range(RING):
                state = next_state(step, state)

            @pl.when(row < PRODUCT_ROW - 1)
            def _():
                onward_rows(0).start()

            @pl.when(jnp.logical_and(row == PRODUCT_ROW - 1, jnp.logical_not(final_row)))
            def _():
                for to in (tip, other):
                    onward_pair(to).start()

            for step in range(RING):
                send_home(step)

        @pl.when(jnp.logical_not(direct))
        def _():
            def prepare(last):
                leading_maps(last, maps, tips_both, tip, high, low, local)

            def start_state():
                for h in range(2):
                    few_in[:, h * half : (h + 1) * half] = own_of(columns_in[h])
                send_home(0)

            def product_step(last):
                slot = (last - 1) % 2
                parts = split_rows(jnp.concatenate([columns_in[0], columns_in[1]], 1))
                fresh = jnp.dot(parts, high[slot], preferred_element_type=jnp.float32)
                fresh = fresh + jnp.dot(parts, low[slot], preferred_element_type=jnp.float32)
                columns_out[...] = fresh[: 2 * few] + fresh[2 * few :] + local[...]

            @pl.when(jnp.logical_not(final_row))
            def _():
                prepare(RING - 1)

            @pl.when(final_row)
            def _():
                prepare(RING - 2)

            @pl.when(row == PRODUCT_ROW)
            def _():
                for core in range(2):
                    remote(
                        pair_in.at[core], pair_in.at[core], wave_send.at[0], wave_recv.at[3 + core], me, other
                    ).wait_recv()
                for core in range(2):
                    for h in range(2):
                        columns_in[h, core * few : (core + 1) * few, :] = pair_in[core, :, h * half : (h + 1) * half]

            def columns_arrive(core):
                remote(
                    columns_in.at[core], columns_in.at[core], wave_send.at[0], wave_recv.at[5 + core], me, other
                ).wait_recv()

            @pl.when(row > PRODUCT_ROW)
            def _():
                for core in range(2):
                    columns_arrive(core)

            @pl.when(jnp.logical_not(final_row))
            def _():
                product_step(RING - 1)
                for to in (tip, other):
                    onward_columns(to).start()

            @pl.when(final_row)
            def _():
                start_state()
                product_step(RING - 2)
                for to in (tip, other):
                    @pl.when(jnp.logical_or(x != RING - 1, tip != to))
                    def _():
                        to_last(to).start()

                @pl.when(x == RING - 1)
                def _():
                    last_in[x, tip] = columns_out[...]

            @pl.when(jnp.logical_not(final_row))
            def _():
                start_state()

            state = few_in[...]
            for step in range(RING - 2):
                state = next_state(step, state)
                send_home(step + 1)

            @pl.when(jnp.logical_not(final_row))
            def _():
                next_state(RING - 2, state)
                send_home(RING - 1)

        @pl.when(to_the_end)
        def _():
            for chip in range(RING):
                for core in range(2):
                    @pl.when(jnp.logical_or(chip != x, core != tip))
                    def _():
                        block = last_in.at[chip, core]
                        remote(block, block, last_send.at[0], last_recv.at[chip, core], me, other).wait_recv()
            for chip in range(RING):
                for core in range(2):
                    columns = slice(core * half, (core + 1) * half)
                    for group in range(2):
                        start = group * many + chip * few
                        block = last_in[chip, core, group * few : (group + 1) * few, :]
                        full[start : start + few, columns] = block

        @pl.when(jnp.logical_not(to_the_end))
        def _():
            for piece in range(2 * RING):
                @pl.when(piece != mine)
                def _():
                    remote(
                        prior.at[piece], prior.at[piece], home_send.at[0, 0], home_recv.at[piece], me, other
                    ).wait_recv()
            for piece in range(2 * RING):
                full[piece * few : (piece + 1) * few, :] = prior[piece]

        @pl.when(jnp.logical_not(all_helped))
        def _():
            whole.drain()

        for those, first, n, _, chip, in_chain in helping:
            if not in_chain:
                @pl.when(those)
                def _():
                    relay_drain(first, n, chip)

        for (those, _, parts), gather in zip(helped, gathers):
            @pl.when(those)
            def _():
                gather.drain()
                for first, n, chip in parts:
                    for k in range(first, first + n):
                        to_relay(k, chip).wait_send()
                        for step in range(1, RING):
                            relayed_to_sibling(step, k).wait_send()

        for part in range(2):
            own_sibling_map(part).wait_send()
        for number, (step, to) in enumerate(partners):
            tip_copy(step, to, number).wait_send()

        @pl.when(row < PRODUCT_ROW - 1)
        def _():
            onward_rows(0).wait_send()

        @pl.when(jnp.logical_and(row == PRODUCT_ROW - 1, jnp.logical_not(final_row)))
        def _():
            for to in range(2):
                onward_pair(to).wait_send()

        @pl.when(jnp.logical_and(row >= PRODUCT_ROW, jnp.logical_not(final_row)))
        def _():
            for to in range(2):
                onward_columns(to).wait_send()

        for step in range(RING - 1):
            for to in range(2):
                @pl.when(jnp.logical_or(x != step, tip != to))
                def _():
                    home_copy(step, to).wait_send()

        for to in range(2):
            @pl.when(jnp.logical_or(x != RING - 1, tip != to))
            def _():
                @pl.when(final_row)
                def _():
                    to_last(to).wait_send()

                @pl.when(jnp.logical_not(final_row))
                def _():
                    home_copy(RING - 1, to).wait_send()

    own_spikes.wait()
    spikes_out.wait()
    count = full.shape[0]
    parts = split_rows(full[...])
    fresh = jnp.dot(parts, maps[x, tip], preferred_element_type=jnp.float32)
    interface_ref[0] = fresh[:count] + fresh[count:]
    middle = spikes.shape[1]
    product = jnp.dot(parts[:count, :middle], spikes[0], preferred_element_type=jnp.float32)
    product_ref[0] = product + jnp.dot(parts[:count, middle:], spikes[1], preferred_element_type=jnp.float32)


def on_device(band_maps, right_tips, spikes, local_parts):
    rows_total = lax.axis_size("dom") // RING
    _, depth, half = band_maps.shape
    count = right_tips.shape[1]
    many = count // 2
    few = many // RING
    _, spike_rows, spike_columns = spikes.shape
    width = spike_columns // 2
    f32, b16, dma = jnp.float32, jnp.bfloat16, pltpu.SemaphoreType.DMA
    interface, product = pl.pallas_call(
        functools.partial(sweep, rows_total),
        out_shape=(
            jax.ShapeDtypeStruct((1, count, half), f32),
            jax.ShapeDtypeStruct((1, count, width), f32),
        ),
        in_specs=[
            pl.BlockSpec(memory_space=pltpu.HBM),
            pl.BlockSpec(memory_space=pltpu.HBM),
            pl.BlockSpec(memory_space=pltpu.HBM),
        ],
        out_specs=(pl.BlockSpec(memory_space=pltpu.VMEM),) * 2,
        scratch_shapes=[
            pltpu.VMEM((RING, 2, depth, half), b16),
            pltpu.VMEM((count, half), f32),
            pltpu.VMEM((RING, 2 * few, half), f32),
            pltpu.VMEM((RING, 2, 2 * few, half), f32),
            pltpu.VMEM((RING, 2, few, half), f32),
            pltpu.VMEM((2, many, half), f32),
            pltpu.VMEM((few, depth), f32),
            pltpu.VMEM((2, few, depth), f32),
            pltpu.VMEM((2, 2 * few, half), f32),
            pltpu.VMEM((2 * few, half), f32),
            pltpu.VMEM((2 * few, half), f32),
            pltpu.VMEM((2, depth, half), b16),
            pltpu.VMEM((2, depth, half), b16),
            pltpu.VMEM((2, many, half), f32),
            pltpu.VMEM((2, many, half), f32),
            pltpu.VMEM((RING, few, depth), f32),
            pltpu.VMEM((2 * RING, few, depth), f32),
            pltpu.VMEM((2, many, half), f32),
            pltpu.VMEM((count, depth), f32),
            pltpu.VMEM((2, spike_rows, width), b16),
            dma((3,)),
            dma((RING, 2)),
            dma((RING, 2)),
            dma((2, 2)),
            dma((2, 2)),
            pltpu.VMEM((5, depth // 16, half), b16),
            pltpu.SemaphoreType.REGULAR((2,)),
            dma((RING, 5)),
            dma((RING, 5)),
            dma((RING, 5)),
            dma((RING, 5)),
            dma((2, 2)),
            dma((2, 2)),
            dma((2, 2)),
            dma((2, 2)),
            dma((2 * RING - 1,)),
            dma((RING, 2)),
            dma((2,)),
            dma((7,)),
            dma((RING, 2)),
            dma((2 * RING,)),
            dma((2,)),
            dma((2,)),
            pltpu.VMEM((RING, 2, 2 * few, half), f32),
            dma((2,)),
            dma((RING, 2)),
        ],
        compiler_params=pltpu.CompilerParams(
            collective_id=0, has_side_effects=True, vmem_limit_bytes=53 << 20
        ),
    )(band_maps, pltpu.with_memory_space_constraint(right_tips, pltpu.HBM), spikes)
    return right_tips + interface, local_parts - product


def solution(mesh):
    return jax.shard_map(
        on_device,
        mesh=mesh,
        in_specs=(
            P("dom", None, "tip"),
            P("dom", None, "tip"),
            P("dom", "tip", None),
            P("dom", None, "tip"),
        ),
        out_specs=(P("dom", None, "tip"), P("dom", None, "tip")),
        check_vma=False,
    )
```

```python
import functools

import jax
import jax.numpy as jnp
from jax import lax
from jax.experimental import pallas as pl
from jax.experimental.pallas import tpu as pltpu
from jax.sharding import PartitionSpec as P

MESH = pl.DeviceIdType.MESH
RING = 4
CHAIN_ROWS = 2
HELPERS = {
    2: ((14, 3), (1, 2)),
    3: ((15, 4),),
    4: ((13, 4),),
    5: ((12, 3),),
    6: ((10, 2),),
    7: ((11, 2),),
}
PRODUCT_ROW = 4


def split_rows(value):
    high = value.astype(jnp.bfloat16)
    low = value - high.astype(jnp.float32)
    return jnp.concatenate([high.astype(jnp.float32), low], 0).astype(jnp.bfloat16)


def times_map(value, left, right):
    rows = value.shape[0]
    parts = split_rows(value)
    out = [jnp.dot(parts, half, preferred_element_type=jnp.float32) for half in (left, right)]
    return [piece[:rows] + piece[rows:] for piece in out]


def leading_maps(last, maps, tips, tip, high, low, local):
    depth, half = maps.shape[2], maps.shape[3]
    count = local.shape[0]
    local[...] = tips[last, tip]
    block = min(256, half)
    for turn, step in enumerate(range(last - 1, -1, -1)):
        rows = split_rows(jnp.concatenate([tips[step, 0], tips[step, 1]], 1))
        factor = jnp.concatenate([jnp.concatenate([maps[step, 0], maps[step, 1]], 1), rows], 0)
        for start in range(0, half, block):
            columns = slice(start, start + block)
            if turn == 0:
                total = jnp.dot(factor, maps[last, tip, :, columns], preferred_element_type=jnp.float32)
            else:
                total = jnp.dot(factor, high[(turn - 1) % 2, :, columns], preferred_element_type=jnp.float32)
                total += jnp.dot(factor, low[(turn - 1) % 2, :, columns], preferred_element_type=jnp.float32)
            local[:, columns] += total[depth : depth + count] + total[depth + count :]
            total = total[:depth]
            top = total.astype(jnp.bfloat16)
            high[turn % 2, :, columns] = top
            low[turn % 2, :, columns] = (total - top.astype(jnp.float32)).astype(jnp.bfloat16)


def sweep(
    rows_total, maps_hbm, tips_hbm, spikes_hbm, interface_ref, product_ref,
    maps, tips_ref, tips_out, tips_both, tips_few, tips_many, few_in, pair_in, columns_in, columns_out, local,
    high, low, many_in, many_out, states, prior, prior_many, full, spikes,
    local_sem, sib_send, sib_recv, quarter_send, quarter_recv, relay, relay_open, relay_send, relay_recv,
    relay_sib_send, relay_sib_recv,
    link_send, link_recv, fwd_send, opp_recv,
    tip_send, tip_recv, wave_send, wave_recv, home_send, home_recv, side_send, side_recv,
    last_in, last_send, last_recv,
):
    me, tip = lax.axis_index("dom"), lax.axis_index("tip")
    x, row = lax.rem(me, RING), lax.div(me, RING)
    other = 1 - tip
    base = me - x
    depth = maps_hbm.shape[1]
    half = maps_hbm.shape[2]
    cut = depth // 2
    width = spikes_hbm.shape[2] // 2
    chained = row < CHAIN_ROWS
    ringed = row >= CHAIN_ROWS
    def among(rows):
        return functools.reduce(jnp.logical_or, [row == r for r in rows])

    def first_chip(pairs):
        value = pairs[0][1]
        for this, that in pairs[1:]:
            value = jnp.where(row == this, that, value)
        return value * RING

    by_shares, by_part = {}, {}
    for r, helpers in HELPERS.items():
        by_shares.setdefault(tuple(n for _, n in helpers), []).append(r)
        first = 0
        for which, (h, n) in enumerate(helpers):
            by_part.setdefault((first, n, which, h < CHAIN_ROWS), []).append((h, r))
            first += n
    helped = []
    for shares, rows in by_shares.items():
        parts = [
            (sum(shares[:which]), shares[which], first_chip([(r, HELPERS[r][which][0]) for r in rows]))
            for which in range(len(shares))
        ]
        helped.append((among(rows), sum(shares), parts))
    helping = [
        (among([h for h, _ in pairs]), first, n, which, first_chip(pairs), in_chain)
        for (first, n, which, in_chain), pairs in by_part.items()
    ]
    all_helped = among(list(HELPERS))
    all_helping = among([h for helpers in HELPERS.values() for h, _ in helpers])
    unit = maps_hbm.shape[1] // 16
    last_chain = CHAIN_ROWS * RING - 1
    right, left = base + lax.rem(x + 1, RING), base + lax.rem(x + 3, RING)
    opposite = base + lax.rem(x + 2, RING)
    many = full.shape[0] // 2
    few = many // RING

    def remote(src, dst, send, recv, dom, to):
        return pltpu.make_async_remote_copy(
            src_ref=src, dst_ref=dst, send_sem=send, recv_sem=recv, device_id=(dom, to), device_id_type=MESH
        )

    barrier = pltpu.get_barrier_semaphore()

    def greet(dom, to):
        pl.semaphore_signal(barrier, inc=1, device_id=(dom, to), device_id_type=MESH)

    greet(me, other)

    @pl.when(chained)
    def _():
        @pl.when(me > 0)
        def _():
            greet(me - 1, tip)

        @pl.when(me == 1)
        def _():
            greet(0, other)

    @pl.when(ringed)
    def _():
        for step in range(1, RING):
            for to in range(2):
                greet(base + lax.rem(x + step, RING), to)
        before = jnp.where(row == CHAIN_ROWS, last_chain, me - RING)
        greet(before, tip)

        @pl.when(row >= PRODUCT_ROW)
        def _():
            greet(before, other)

        for those, _, parts in helped:
            @pl.when(those)
            def _():
                for _, _, chip in parts:
                    greet(chip + x, tip)

    own_map = pltpu.make_async_copy(maps_hbm.at[0], maps.at[x, tip], local_sem.at[0])
    own_map.start()
    own_columns = pl.ds(pl.multiple_of(tip * width, width), width)
    other_columns = pl.ds(pl.multiple_of(other * width, width), width)
    own_spikes = pltpu.make_async_copy(spikes_hbm.at[0, :, own_columns], spikes.at[tip], local_sem.at[1])
    own_spikes.start()
    own_tips = pltpu.make_async_copy(tips_hbm.at[0], tips_ref, local_sem.at[2])
    own_tips.start()
    asked = jnp.where(all_helping, 1, 0)

    @pl.when(chained)
    def _():
        pl.semaphore_wait(barrier, jnp.where(me == last_chain, 1 + RING, jnp.where(me == 0, 3, 2)) + asked)

    @pl.when(ringed)
    def _():
        after = jnp.where(row == rows_total - 1, 0, jnp.where(row >= PRODUCT_ROW - 1, 2, 1))
        pl.semaphore_wait(barrier, 2 * RING - 1 + after + asked)

    for those, _, _, which, chip, _ in helping:
        @pl.when(those)
        def _():
            pl.semaphore_signal(relay_open.at[which], inc=1, device_id=(chip + x, tip), device_id_type=MESH)

    pieces = [slice(0, cut), slice(cut, depth)]

    def sibling_map_arrives(step, part):
        slot = lax.rem(x + step, RING)
        block = maps.at[slot, other, pieces[part]]
        remote(block, block, sib_send.at[step, part], sib_recv.at[step, part], me, other).wait_recv()

    def own_sibling_map(part):
        src = maps_hbm.at[0, pieces[part]]
        return remote(src, maps.at[x, tip, pieces[part]], sib_send.at[0, part], sib_recv.at[0, part], me, other)

    spikes_out = remote(
        spikes_hbm.at[0, :, other_columns], spikes.at[tip], side_send.at[0], side_recv.at[0], me, other
    )

    def first_rows(to):
        rows = slice(to * many, (to + 1) * many)
        return remote(tips_hbm.at[0, rows, :], many_in.at[tip], wave_send.at[to], wave_recv.at[tip], 1, to)

    def relay_rows(k):
        return slice(depth - (k + 1) * unit, depth - k * unit)

    def to_relay(k, chip):
        src = maps_hbm.at[0, relay_rows(k)]
        return remote(src, relay.at[k], relay_send.at[0, k], relay_recv.at[0, k], chip + x, tip)

    def from_relay(step, k, chip):
        dst = maps.at[x, tip, relay_rows(k)]
        dom = chip + lax.rem(x + step, RING)
        return remote(relay.at[k], dst, relay_send.at[step, k], relay_recv.at[step, k], dom, tip)

    def pass_on(first, n, chip):
        for k in range(first, first + n):
            remote(relay.at[k], relay.at[k], relay_send.at[0, k], relay_recv.at[0, k], me, other).wait_recv()
            for step in range(1, RING):
                from_relay(step, k, chip).start()

    def relay_drain(first, n, chip):
        for k in range(first, first + n):
            for step in range(1, RING):
                from_relay(step, k, chip).wait_send()

    @pl.when(chained)
    def _():
        @pl.when(me == 0)
        def _():
            for to in range(2):
                first_rows(to).start()

        own_tips.wait()
        for part in range(2):
            own_sibling_map(part).start()
        tip_rows = pl.ds(pl.multiple_of(other * many, many), many)
        tips_copy = remote(
            tips_ref.at[tip_rows, :], tips_many.at[tip], tip_send.at[0], tip_recv.at[0, 1], me, other
        )
        tips_copy.start()
        spikes_out.start()
        tips_copy.wait_recv()

        def many_send(h, dom):
            return remote(many_out.at[h], many_in.at[h], wave_send.at[h], wave_recv.at[h], dom, tip)

        own_rows = pl.ds(pl.multiple_of(tip * many, many), many)
        tips_many[tip] = tips_ref[own_rows, :]

        @pl.when(me == 0)
        def _():
            many_in[...] = jnp.zeros_like(many_in)

        for those, first, n, _, chip, in_chain in helping:
            if in_chain:
                @pl.when(those)
                def _():
                    pass_on(first, n, chip)

        total = [None, None]
        for k in range(2):
            @pl.when(me > 0)
            def _():
                remote(many_in.at[k], many_in.at[k], wave_send.at[k], wave_recv.at[k], me, other).wait_recv()

            if k == 0:
                own_map.wait()
            sibling_map_arrives(0, k)
            parts = split_rows(many_in[k])
            for h in range(2):
                term = jnp.dot(parts, maps[x, h, k * half : (k + 1) * half, :], preferred_element_type=jnp.float32)
                total[h] = term if k == 0 else total[h] + term
                if k == 1:
                    fresh = total[h][:many] + total[h][many:] + tips_many[h]
                    many_out[h] = fresh

                    @pl.when(jnp.logical_and(me > 0, me < last_chain))
                    def _():
                        many_send(h, me + 1).start()

        @pl.when(me == last_chain)
        def _():
            for piece in range(RING):
                for h in range(2):
                    states[piece, :, h * half : (h + 1) * half] = many_out[h, piece * few : (piece + 1) * few, :]
            for piece in range(RING):
                remote(
                    states.at[piece], few_in, home_send.at[piece, 0], wave_recv.at[2], last_chain + 1 + piece, tip
                ).start()

        to_sibling = remote(many_in, prior_many, side_send.at[1], side_recv.at[1], me, other)
        to_sibling.start()
        for h in range(2):
            full[own_rows, h * half : (h + 1) * half] = many_in[h]
        to_sibling.wait_recv()
        for h in range(2):
            full[tip_rows, h * half : (h + 1) * half] = prior_many[h]

        for those, first, n, _, chip, in_chain in helping:
            if in_chain:
                @pl.when(those)
                def _():
                    relay_drain(first, n, chip)

        to_sibling.wait_send()
        tips_copy.wait_send()
        for part in range(2):
            own_sibling_map(part).wait_send()

        @pl.when(me == 0)
        def _():
            for to in range(2):
                first_rows(to).wait_send()

        @pl.when(jnp.logical_and(me > 0, me < last_chain))
        def _():
            for h in range(2):
                many_send(h, me + 1).wait_send()

        @pl.when(me == last_chain)
        def _():
            for piece in range(RING):
                remote(
                    states.at[piece], few_in, home_send.at[piece, 0], wave_recv.at[2], last_chain + 1 + piece, tip
                ).wait_send()

    @pl.when(ringed)
    def _():
        class Gather:
            def __init__(self, count):
                self.cut = count // 2

            def rows(self, part, k=None):
                if k is None:
                    return slice(part * self.cut, (part + 1) * self.cut)
                size = self.cut // 2
                return slice(part * self.cut + k * size, part * self.cut + (k + 1) * size)

            def own(self, part, side):
                rows = self.rows(part)
                return remote(
                    maps_hbm.at[0, rows], maps.at[x, tip, rows],
                    link_send.at[side, part], link_recv.at[side, part], right if side == 0 else left, tip,
                )

            def neighbour_arrives(self, part, side):
                block = maps.at[lax.rem(x + (3 if side == 0 else 1), RING), tip, self.rows(part)]
                remote(block, block, link_send.at[side, part], link_recv.at[side, part], right, tip).wait_recv()

            def forward(self, side, k):
                block = maps.at[lax.rem(x + (3 if side == 0 else 1), RING), tip, self.rows(side, k)]
                dom = right if side == 0 else left
                return remote(block, block, fwd_send.at[side, k], opp_recv.at[side, k], dom, tip)

            def opposite_arrives(self, side, k):
                block = maps.at[lax.rem(x + 2, RING), tip, self.rows(side, k)]
                remote(block, block, fwd_send.at[side, k], opp_recv.at[side, k], right, tip).wait_recv()

            def to_sibling(self, step, part):
                block = maps.at[lax.rem(x + step, RING), tip, self.rows(part)]
                return remote(block, block, sib_send.at[step, part], sib_recv.at[step, part], me, other)

            def sibling_arrives(self, step, part):
                block = maps.at[lax.rem(x + step, RING), other, self.rows(part)]
                remote(block, block, sib_send.at[step, part], sib_recv.at[step, part], me, other).wait_recv()

            def quarter_to_sibling(self, side, k):
                block = maps.at[lax.rem(x + 2, RING), tip, self.rows(side, k)]
                return remote(block, block, quarter_send.at[side, k], quarter_recv.at[side, k], me, other)

            def sibling_quarter_arrives(self, side, k):
                block = maps.at[lax.rem(x + 2, RING), other, self.rows(side, k)]
                remote(block, block, quarter_send.at[side, k], quarter_recv.at[side, k], me, other).wait_recv()

            def start(self, which=(0, 1)):
                for turn in which:
                    for part, side in (((0, 0), (1, 1)), ((1, 0), (0, 1)))[turn]:
                        self.own(part, side).start()

            def middle(self):
                for part, side in ((0, 0), (1, 1)):
                    self.neighbour_arrives(part, side)
                    for k in range(2):
                        self.forward(side, k).start()
                    self.to_sibling(3 if side == 0 else 1, part).start()
                for part, side in ((1, 0), (0, 1)):
                    self.neighbour_arrives(part, side)
                    self.to_sibling(3 if side == 0 else 1, part).start()

            def last(self):
                for k in range(2):
                    for side in range(2):
                        self.opposite_arrives(side, k)
                        self.quarter_to_sibling(side, k).start()
                for step in (1, 3):
                    for part in range(2):
                        self.sibling_arrives(step, part)
                for k in range(2):
                    for side in range(2):
                        self.sibling_quarter_arrives(side, k)

            def drain(self):
                for part in range(2):
                    for side in range(2):
                        self.own(part, side).wait_send()
                    for k in range(2):
                        self.forward(part, k).wait_send()
                        self.quarter_to_sibling(part, k).wait_send()
                    for step in (1, 3):
                        self.to_sibling(step, part).wait_send()

        whole = Gather(depth)
        gathers = [Gather(depth - count * unit) for _, count, _ in helped]

        def relayed_to_sibling(step, k):
            block = maps.at[lax.rem(x + RING - step, RING), tip, relay_rows(k)]
            return remote(block, block, relay_sib_send.at[step, k], relay_sib_recv.at[step, k], me, other)

        for (those, _, _), gather in zip(helped, gathers):
            @pl.when(those)
            def _():
                gather.start()

        @pl.when(jnp.logical_not(jnp.logical_or(all_helped, all_helping)))
        def _():
            whole.start()

        for those, _, n, _, _, in_chain in helping:
            if not in_chain and n < 3:
                @pl.when(those)
                def _():
                    whole.start((0,))

        own_tips.wait()
        for piece in range(RING):
            for to in range(2):
                start = to * many + piece * few
                tips_out[piece, to * few : (to + 1) * few, :] = tips_ref[start : start + few, :]

        def tip_copy(step, to, number):
            dst_x = lax.rem(x + step, RING)
            return remote(
                tips_out.at[dst_x], tips_both.at[x, tip],
                tip_send.at[number], tip_recv.at[step, jnp.where(to == tip, 0, 1)], base + dst_x, to,
            )

        partners = [(0, other), (1, tip), (1, other), (2, tip), (2, other), (3, tip), (3, other)]
        for number, (step, to) in enumerate(partners):
            tip_copy(step, to, number).start()
        tips_both[x, tip] = tips_out[x]

        for those, _, parts in helped:
            @pl.when(those)
            def _():
                for which, (first, n, chip) in reversed(list(enumerate(parts))):
                    pl.semaphore_wait(relay_open.at[which], 1)
                    for k in range(first, first + n):
                        to_relay(k, chip).start()

        for those, first, n, _, chip, in_chain in helping:
            if not in_chain:
                @pl.when(those)
                def _():
                    pass_on(first, n, chip)
                    whole.start((1,) if n < 3 else (0, 1))

        for part in range(2):
            own_sibling_map(part).start()
        spikes_out.start()

        @pl.when(jnp.logical_not(all_helped))
        def _():
            whole.middle()
            whole.last()

        for (those, count, _), gather in zip(helped, gathers):
            @pl.when(those)
            def _():
                gather.middle()
                for k in range(count):
                    for step in range(1, RING):
                        block = maps.at[lax.rem(x + RING - step, RING), tip, relay_rows(k)]
                        remote(block, block, relay_send.at[step, k], relay_recv.at[step, k], me, other).wait_recv()
                        relayed_to_sibling(step, k).start()
                gather.last()
                for k in range(count):
                    for step in range(1, RING):
                        block = maps.at[lax.rem(x + RING - step, RING), other, relay_rows(k)]
                        remote(
                            block, block, relay_sib_send.at[step, k], relay_sib_recv.at[step, k], me, other
                        ).wait_recv()

        own_map.wait()
        for part in range(2):
            sibling_map_arrives(0, part)
        for step, to in partners:
            remote(
                tips_both.at[0, 0], tips_both.at[0, 0], tip_send.at[0],
                tip_recv.at[step, jnp.where(to == tip, 0, 1)], me, other,
            ).wait_recv()

        mine = tip * RING + x

        def home_copy(step, to):
            src = few_in if step == 0 else states.at[step - 1]
            return remote(src, prior.at[mine], home_send.at[step, to], home_recv.at[mine], base + step, to)

        def send_home(step):
            for to in (tip, other):
                @pl.when(jnp.logical_or(x != step, tip != to))
                def _():
                    home_copy(step, to).start()

            @pl.when(x == step)
            def _():
                prior[mine] = few_in[...] if step == 0 else states[step - 1]

        def next_state(step, state):
            fresh = times_map(state, maps[step, 0], maps[step, 1])
            for h in range(2):
                states[step, :, h * half : (h + 1) * half] = fresh[h] + tips_few[step, h]
            return states[step]

        def own_of(pair):
            return jnp.where(tip == 0, pair[:few], pair[few:])

        for step in range(RING):
            for h in range(2):
                tips_few[step, h] = own_of(tips_both[step, h])

        final_row = row == rows_total - 1
        to_the_end = jnp.logical_and(final_row, x == RING - 1)

        def to_last(to):
            dom = base + RING - 1
            return remote(columns_out, last_in.at[x, tip], last_send.at[to], last_recv.at[x, tip], dom, to)
        direct = row < PRODUCT_ROW

        def onward_rows(to):
            return remote(states.at[RING - 1], few_in, wave_send.at[to], wave_recv.at[2], me + RING, tip)

        def onward_pair(to):
            return remote(
                states.at[RING - 1], pair_in.at[tip], wave_send.at[to], wave_recv.at[3 + tip], me + RING, to
            )

        def onward_columns(to):
            return remote(columns_out, columns_in.at[tip], wave_send.at[to], wave_recv.at[5 + tip], me + RING, to)

        def drain():
            @pl.when(jnp.logical_not(all_helped))
            def _():
                whole.drain()

            for those, first, n, _, chip, in_chain in helping:
                if not in_chain:
                    @pl.when(those)
                    def _():
                        relay_drain(first, n, chip)

            for (those, _, parts), gather in zip(helped, gathers):
                @pl.when(those)
                def _():
                    gather.drain()
                    for first, n, chip in parts:
                        for k in range(first, first + n):
                            to_relay(k, chip).wait_send()
                            for step in range(1, RING):
                                relayed_to_sibling(step, k).wait_send()

            for part in range(2):
                own_sibling_map(part).wait_send()
            for number, (step, to) in enumerate(partners):
                tip_copy(step, to, number).wait_send()

        @pl.when(direct)
        def _():
            remote(few_in, few_in, wave_send.at[0], wave_recv.at[2], me, other).wait_recv()
            state = few_in[...]
            for step in range(RING):
                state = next_state(step, state)

            @pl.when(row < PRODUCT_ROW - 1)
            def _():
                onward_rows(0).start()

            @pl.when(jnp.logical_and(row == PRODUCT_ROW - 1, jnp.logical_not(final_row)))
            def _():
                for to in (tip, other):
                    onward_pair(to).start()

            for step in range(RING):
                send_home(step)

        @pl.when(jnp.logical_not(direct))
        def _():
            def prepare(last):
                leading_maps(last, maps, tips_both, tip, high, low, local)

            def start_state():
                for h in range(2):
                    few_in[:, h * half : (h + 1) * half] = own_of(columns_in[h])
                send_home(0)

            def product_step(last):
                slot = (last - 1) % 2
                parts = split_rows(jnp.concatenate([columns_in[0], columns_in[1]], 1))
                fresh = jnp.dot(parts, high[slot], preferred_element_type=jnp.float32)
                fresh = fresh + jnp.dot(parts, low[slot], preferred_element_type=jnp.float32)
                columns_out[...] = fresh[: 2 * few] + fresh[2 * few :] + local[...]

            @pl.when(jnp.logical_not(final_row))
            def _():
                prepare(RING - 1)

            @pl.when(final_row)
            def _():
                prepare(RING - 2)

            @pl.when(final_row)
            def _():
                drain()

            @pl.when(row == PRODUCT_ROW)
            def _():
                for core in range(2):
                    remote(
                        pair_in.at[core], pair_in.at[core], wave_send.at[0], wave_recv.at[3 + core], me, other
                    ).wait_recv()
                for core in range(2):
                    for h in range(2):
                        columns_in[h, core * few : (core + 1) * few, :] = pair_in[core, :, h * half : (h + 1) * half]

            def columns_arrive(core):
                remote(
                    columns_in.at[core], columns_in.at[core], wave_send.at[0], wave_recv.at[5 + core], me, other
                ).wait_recv()

            @pl.when(row > PRODUCT_ROW)
            def _():
                for core in range(2):
                    columns_arrive(core)

            @pl.when(jnp.logical_not(final_row))
            def _():
                product_step(RING - 1)
                for to in (tip, other):
                    onward_columns(to).start()

            @pl.when(final_row)
            def _():
                start_state()
                product_step(RING - 2)
                for to in (tip, other):
                    @pl.when(jnp.logical_or(x != RING - 1, tip != to))
                    def _():
                        to_last(to).start()

                @pl.when(x == RING - 1)
                def _():
                    last_in[x, tip] = columns_out[...]

            @pl.when(jnp.logical_not(final_row))
            def _():
                start_state()

            state = few_in[...]
            for step in range(RING - 2):
                state = next_state(step, state)
                send_home(step + 1)

            @pl.when(jnp.logical_not(final_row))
            def _():
                next_state(RING - 2, state)
                send_home(RING - 1)

        @pl.when(to_the_end)
        def _():
            for chip in range(RING):
                for core in range(2):
                    @pl.when(jnp.logical_or(chip != x, core != tip))
                    def _():
                        block = last_in.at[chip, core]
                        remote(block, block, last_send.at[0], last_recv.at[chip, core], me, other).wait_recv()
            for chip in range(RING):
                for core in range(2):
                    columns = slice(core * half, (core + 1) * half)
                    for group in range(2):
                        start = group * many + chip * few
                        block = last_in[chip, core, group * few : (group + 1) * few, :]
                        full[start : start + few, columns] = block

        @pl.when(jnp.logical_not(to_the_end))
        def _():
            for piece in range(2 * RING):
                @pl.when(piece != mine)
                def _():
                    remote(
                        prior.at[piece], prior.at[piece], home_send.at[0, 0], home_recv.at[piece], me, other
                    ).wait_recv()
            for piece in range(2 * RING):
                full[piece * few : (piece + 1) * few, :] = prior[piece]

        @pl.when(jnp.logical_not(final_row))
        def _():
            drain()

        @pl.when(row < PRODUCT_ROW - 1)
        def _():
            onward_rows(0).wait_send()

        @pl.when(jnp.logical_and(row == PRODUCT_ROW - 1, jnp.logical_not(final_row)))
        def _():
            for to in range(2):
                onward_pair(to).wait_send()

        @pl.when(jnp.logical_and(row >= PRODUCT_ROW, jnp.logical_not(final_row)))
        def _():
            for to in range(2):
                onward_columns(to).wait_send()

        for step in range(RING - 1):
            for to in range(2):
                @pl.when(jnp.logical_or(x != step, tip != to))
                def _():
                    home_copy(step, to).wait_send()

        for to in range(2):
            @pl.when(jnp.logical_or(x != RING - 1, tip != to))
            def _():
                @pl.when(final_row)
                def _():
                    to_last(to).wait_send()

                @pl.when(jnp.logical_not(final_row))
                def _():
                    home_copy(RING - 1, to).wait_send()

    own_spikes.wait()
    spikes_out.wait()
    count = full.shape[0]
    parts = split_rows(full[...])
    fresh = jnp.dot(parts, maps[x, tip], preferred_element_type=jnp.float32)
    interface_ref[0] = fresh[:count] + fresh[count:]
    middle = spikes.shape[1]
    product = jnp.dot(parts[:count, :middle], spikes[0], preferred_element_type=jnp.float32)
    product_ref[0] = product + jnp.dot(parts[:count, middle:], spikes[1], preferred_element_type=jnp.float32)


def on_device(band_maps, right_tips, spikes, local_parts):
    rows_total = lax.axis_size("dom") // RING
    _, depth, half = band_maps.shape
    count = right_tips.shape[1]
    many = count // 2
    few = many // RING
    _, spike_rows, spike_columns = spikes.shape
    width = spike_columns // 2
    f32, b16, dma = jnp.float32, jnp.bfloat16, pltpu.SemaphoreType.DMA
    interface, product = pl.pallas_call(
        functools.partial(sweep, rows_total),
        out_shape=(
            jax.ShapeDtypeStruct((1, count, half), f32),
            jax.ShapeDtypeStruct((1, count, width), f32),
        ),
        in_specs=[
            pl.BlockSpec(memory_space=pltpu.HBM),
            pl.BlockSpec(memory_space=pltpu.HBM),
            pl.BlockSpec(memory_space=pltpu.HBM),
        ],
        out_specs=(pl.BlockSpec(memory_space=pltpu.VMEM),) * 2,
        scratch_shapes=[
            pltpu.VMEM((RING, 2, depth, half), b16),
            pltpu.VMEM((count, half), f32),
            pltpu.VMEM((RING, 2 * few, half), f32),
            pltpu.VMEM((RING, 2, 2 * few, half), f32),
            pltpu.VMEM((RING, 2, few, half), f32),
            pltpu.VMEM((2, many, half), f32),
            pltpu.VMEM((few, depth), f32),
            pltpu.VMEM((2, few, depth), f32),
            pltpu.VMEM((2, 2 * few, half), f32),
            pltpu.VMEM((2 * few, half), f32),
            pltpu.VMEM((2 * few, half), f32),
            pltpu.VMEM((2, depth, half), b16),
            pltpu.VMEM((2, depth, half), b16),
            pltpu.VMEM((2, many, half), f32),
            pltpu.VMEM((2, many, half), f32),
            pltpu.VMEM((RING, few, depth), f32),
            pltpu.VMEM((2 * RING, few, depth), f32),
            pltpu.VMEM((2, many, half), f32),
            pltpu.VMEM((count, depth), f32),
            pltpu.VMEM((2, spike_rows, width), b16),
            dma((3,)),
            dma((RING, 2)),
            dma((RING, 2)),
            dma((2, 2)),
            dma((2, 2)),
            pltpu.VMEM((5, depth // 16, half), b16),
            pltpu.SemaphoreType.REGULAR((2,)),
            dma((RING, 5)),
            dma((RING, 5)),
            dma((RING, 5)),
            dma((RING, 5)),
            dma((2, 2)),
            dma((2, 2)),
            dma((2, 2)),
            dma((2, 2)),
            dma((2 * RING - 1,)),
            dma((RING, 2)),
            dma((2,)),
            dma((7,)),
            dma((RING, 2)),
            dma((2 * RING,)),
            dma((2,)),
            dma((2,)),
            pltpu.VMEM((RING, 2, 2 * few, half), f32),
            dma((2,)),
            dma((RING, 2)),
        ],
        compiler_params=pltpu.CompilerParams(
            collective_id=0, has_side_effects=True, vmem_limit_bytes=53 << 20
        ),
    )(band_maps, pltpu.with_memory_space_constraint(right_tips, pltpu.HBM), spikes)
    return right_tips + interface, local_parts - product


def solution(mesh):
    return jax.shard_map(
        on_device,
        mesh=mesh,
        in_specs=(
            P("dom", None, "tip"),
            P("dom", None, "tip"),
            P("dom", "tip", None),
            P("dom", None, "tip"),
        ),
        out_specs=(P("dom", None, "tip"), P("dom", None, "tip")),
        check_vma=False,
    )
```
